256 devices in a mesh: ctx: 32 (over z_hi, y, core), exp: 8 (over x, z_lo).
Axes of the slice: x: 4, y: 4, z: 8 (z_hi: 4, z_lo: 2; z = z_hi * 2 + z_lo), core: 2. Of those that a mesh axis runs over, the one named last changes fastest.
Arguments:
- query: bfloat16 [4096, 8192], P('ctx', 'exp'), may hold values from -200 to 200
- new_kv: bfloat16 [2, 4096, 512], P(None, 'ctx'), may hold values from -6 to 6
- old_kv: bfloat16 [2, 8192, 512], P(None, 'ctx'), may hold values from -4 to 4
- new_pos: int32 [4096], P('ctx'), may hold values from 0 to 4095, as said below
- o_weight: bfloat16 [8192, 4096], P('exp', 'ctx'), may hold values from -1 to 1
- hidden: bfloat16 [4096, 4096], P(('ctx', 'exp')), may hold values from -1.1953125 to 1.1953125
- norm_gain: float32 [4096], replicated, may hold values from 0.5 to 1.5
- expert_ids: int32 [4096, 8], P('ctx'), may hold values from 0 to 63, all different within a row; in each aligned block of 128 rows (0 to 127, 128 to 255, ...) at most 20 rows name the same one
- gate_weights: float32 [4096, 8], P('ctx'), may hold values from 0.1 to 0.6
- w_in: bfloat16 [32, 8, 4096, 768], P('ctx', 'exp'), may hold values from -0.09375 to 0.09375
- w_out: bfloat16 [32, 8, 384, 4096], P('ctx', 'exp'), may hold values from -0.15625 to 0.15625
Outputs:
- mixed: bfloat16 [4096, 4096], P(('ctx', 'exp'))
The draws below stay inside these ranges and needn't reach their ends.
Inputs may be any that keep to these rules, and one draw needn't show every extreme that they name: `new_pos`: row block c of 128 rows holds two runs of 64 consecutive positions, run p and run 2 * 32 - 1 - p, p a drawn permutation of the row blocks. `expert_ids`: in the rows of one index of ctx no expert is chosen more than 20 times.
All inputs are finite; a program needn't handle non-finite values.
Results may differ from the reference program's by a relative error of at most 0.034.
Values may be sent and summed in bfloat16 or wider, within the bound.
A program may use at most 192 MiB of HBM per device.

```python
import math
import jax
import jax.numpy as jnp
import numpy as np
from jax import lax

D = 4096
HQ = 64
KVH = 4
HD = 128
FF = 1536
TOPK = 8
SPLIT = 4
NEW_DEV = 128
FFQ = 384
GROUP = 16
NEW_TOK = 4096
OLD_TOK = 8192
EXP_LOCAL = 8
EXPERTS = 64
CAP = 20
N_CTX = 32
N_EXP = 8


def cache_keys(key):
    return jnp.clip(jax.random.normal(key, (OLD_TOK, KVH * HD), jnp.float32), -4.0, 4.0)


def draw_old_kv(key, part):
    shared = cache_keys(key)
    key = jax.random.fold_in(key, 11)
    values = jnp.clip(jax.random.normal(key, (OLD_TOK, KVH * HD), jnp.float32), -4.0, 4.0)
    return jnp.stack([shared, values], 0).astype(jnp.bfloat16)


def draw_query(key, part):
    key = jax.random.fold_in(key, 13)
    base = jnp.clip(jax.random.normal(key, (NEW_TOK, HQ * HD), jnp.float32), -4.0, 4.0)
    return base.astype(jnp.bfloat16)


def draw_new_pos(key, part):
    key = jax.random.fold_in(key, 7)
    order = jax.random.permutation(key, N_CTX).astype(jnp.int32)
    half = NEW_DEV // 2
    rows = jnp.arange(NEW_TOK, dtype=jnp.int32)
    block = rows // NEW_DEV
    inner = rows % NEW_DEV
    first_run = order[block]
    run = jnp.where(inner < half, first_run, 2 * N_CTX - 1 - first_run)
    return (run * half + inner % half).astype(jnp.int32)


def level_of(own_key, shape, shards, low, high):
    level, own = 1.0, jax.random.fold_in(own_key, 6)
    for axis_at, blocks in shards:
        draws = jnp.exp(jax.random.uniform(jax.random.fold_in(own, axis_at), (blocks,), jnp.float32, low / len(shards), high / len(shards)))
        level = level * jnp.repeat(draws, shape[axis_at] // blocks).reshape([-1 if axis == axis_at else 1 for axis in range(len(shape))])
    return level


def shared_out(key, own, number, rows, count, top, limit, skew):
    order = jax.random.permutation(key, count)
    packed, ordinary = portions_of(count, rows * top, limit, skew, True), portions_of(count, rows * top, limit, skew, False)
    places = jnp.arange(count)

    def named(sizes, rotation):
        used = int((sizes > 0).sum())
        fixed = max(1, used // 4)
        moved = fixed + (places - fixed + rotation * (used - fixed)) % max(1, count - fixed)
        return jnp.zeros((count,), jnp.int32).at[order[jnp.where(places < fixed, places, moved)]].set(jnp.asarray(sizes, jnp.int32))

    sizes = jnp.where(number % 4 == 0, named(packed, number // 4), named(ordinary, number - number // 4 - 1))
    mixed = jax.random.permutation(jax.random.fold_in(own, 3), count)
    donor, sink = mixed[0:count // 2 * 2:2], mixed[1:count // 2 * 2:2]
    margin = jnp.minimum(sizes[donor] - 1, limit - sizes[sink]) // 2
    margin = jnp.where((donor == order[0]) | (sink == order[0]) | (sizes[sink] == 0), 0, jnp.maximum(margin, 0))
    moved = jax.random.randint(jax.random.fold_in(own, 4), (count // 2,), 0, 1 << 20) % (margin + 1)
    sizes = sizes.at[donor].add(-moved).at[sink].add(moved)
    labels = jnp.searchsorted(jnp.cumsum(sizes), jnp.arange(rows * top), side="right").astype(jnp.int32)
    table = labels.reshape(top, rows).T
    table = table[jax.random.permutation(jax.random.fold_in(own, 1), rows)]
    rotation = jax.random.randint(jax.random.fold_in(own, 2), (rows, 1), 0, top)
    return jnp.take_along_axis(table, (jnp.arange(top)[None, :] + rotation) % top, axis=1)


def portions_of(count, total, most, skew, full):
    loads = [(1 << 20) // math.isqrt(rank ** skew) + 1 for rank in range(1, count + 1)]
    largest = most if full else min(most, max(-(-total // count), total * loads[0] // sum(loads)))
    least = 1 if total - largest >= count - 1 else 0
    given, rest = [largest] + [least] * (count - 1), total - largest - least * (count - 1)
    while rest > 0:
        candidates = [i for i in range(1, count) if given[i] < largest] or [i for i in range(1, count) if given[i] < most]
        mass, budget = sum([loads[i] for i in candidates]), rest
        for i in candidates:
            addition = min(most - given[i], max(1, budget * loads[i] // mass), rest)
            given[i] = given[i] + addition
            rest = rest - addition
    return np.array(given)


def scatter_about(rng, shape, deviation, most, shards=(), kind=jnp.bfloat16):
    result = jax.random.normal(rng, shape, jnp.float32) * deviation
    if len(shards) > 0:
        result = level_of(rng, shape, shards, -0.22, 0.18) * result
    return jnp.clip(result, min=-most, max=most).astype(kind)


def setup_inputs(seed: int = 0) -> dict:
    arg_keys = jax.random.split(jax.random.key(seed), 12)
    query = draw_query(jax.random.fold_in(arg_keys[11], 71), 0)
    new_kv = scatter_about(arg_keys[1], (2, NEW_TOK, KVH * HD), 1.0, 6.0, ((1, 32),))
    old_kv = draw_old_kv(jax.random.fold_in(arg_keys[11], 71), 0)
    new_pos = draw_new_pos(jax.random.fold_in(arg_keys[11], 71), 0)
    o_weight = scatter_about(arg_keys[4], (HQ * HD, D), (HD // 4) ** -0.5, 1.0, ((0, 8), (1, 32)))
    hidden = scatter_about(arg_keys[5], (NEW_TOK, D), 0.2, 1.1953125, ((0, 256),))
    norm_gain = jnp.clip(1.0 + 0.1 * jax.random.normal(arg_keys[6], (D,), jnp.float32), 0.5, 1.5)
    expert_ids_keys = jax.random.split(jax.random.fold_in(arg_keys[7], 1), NEW_TOK // NEW_DEV)
    expert_ids_turns = jax.random.permutation(jax.random.fold_in(arg_keys[7], 3), NEW_TOK // NEW_DEV)
    expert_ids = jax.vmap(lambda own, number: shared_out(jax.random.fold_in(arg_keys[7], 2), own, number, NEW_DEV, EXPERTS, TOPK, CAP, 2))(expert_ids_keys, expert_ids_turns).reshape((NEW_TOK, TOPK))
    gate_weights = jnp.clip(0.1 + 0.5 * jax.random.uniform(arg_keys[8], (NEW_TOK, TOPK), jnp.float32) ** level_of(arg_keys[8], (NEW_TOK, TOPK), ((0, 32),), -0.2, 0.2), 0.1, 0.6)
    w_in = scatter_about(arg_keys[9], (N_CTX, N_EXP, D, 2 * FFQ), D ** -0.5, 0.09375, ((0, 32), (1, 8)))
    w_out = scatter_about(arg_keys[10], (N_CTX, N_EXP, FFQ, D), FF ** -0.5, 0.15625, ((0, 32), (1, 8)))
    return dict(query=query, new_kv=new_kv, old_kv=old_kv, new_pos=new_pos, o_weight=o_weight, hidden=hidden, norm_gain=norm_gain, expert_ids=expert_ids, gate_weights=gate_weights, w_in=w_in, w_out=w_out)


def attention(query, new_kv, old_kv, new_pos):
    scale = 1.0 / HD ** 0.5
    heads_q = query.reshape(NEW_TOK, HQ, HD)
    old_keys = old_kv[0].reshape(OLD_TOK, KVH, HD)
    old_vals = old_kv[1].reshape(OLD_TOK, KVH, HD)
    new_keys = new_kv[0].reshape(NEW_TOK, KVH, HD)
    new_vals = new_kv[1].reshape(NEW_TOK, KVH, HD)
    allowed = jnp.concatenate([jnp.ones((NEW_TOK, OLD_TOK), bool), new_pos[None, :] <= new_pos[:, None]], 1)

    def one_head(head):
        kv_head = head // GROUP
        q_rows = lax.dynamic_index_in_dim(heads_q, head, 1, keepdims=False)
        keys = jnp.concatenate([lax.dynamic_index_in_dim(old_keys, kv_head, 1, keepdims=False), lax.dynamic_index_in_dim(new_keys, kv_head, 1, keepdims=False)], 0)
        vals = jnp.concatenate([lax.dynamic_index_in_dim(old_vals, kv_head, 1, keepdims=False), lax.dynamic_index_in_dim(new_vals, kv_head, 1, keepdims=False)], 0)
        scores = jnp.dot(q_rows, keys.T, preferred_element_type=jnp.float32) * scale
        scores = jnp.where(allowed, scores, -1e+30)
        top = lax.optimization_barrier(jnp.max(scores, 1, keepdims=True))
        weights = jnp.where(allowed, jnp.exp(scores - top), 0.0)
        total = lax.optimization_barrier(jnp.sum(weights, 1, keepdims=True))
        probs = weights.astype(jnp.bfloat16)
        return (jnp.dot(probs, vals, preferred_element_type=jnp.float32) / total).astype(jnp.bfloat16)
    per_head = lax.map(one_head, jnp.arange(HQ, dtype=jnp.int32))
    return jnp.transpose(per_head, (1, 0, 2)).reshape(NEW_TOK, HQ * HD)

def reference(query, new_kv, old_kv, new_pos, o_weight, hidden, norm_gain, expert_ids, gate_weights, w_in, w_out):
    attended = attention(query, new_kv, old_kv, new_pos)
    residual = hidden.astype(jnp.float32) + jnp.dot(attended, o_weight, preferred_element_type=jnp.float32)
    normed = (residual * lax.rsqrt(lax.optimization_barrier(jnp.mean(residual * residual, 1, keepdims=True)) + 1e-06) * norm_gain).astype(jnp.bfloat16)
    slots = N_CTX * CAP

    def one_expert(total_out, expert):
        group = expert // EXP_LOCAL
        local = expert % EXP_LOCAL
        member = expert_ids == expert
        picked = jnp.any(member, 1)
        weight_tok = lax.optimization_barrier(jnp.sum(jnp.where(member, gate_weights, 0.0), 1))
        index = jnp.nonzero(picked, size=slots, fill_value=0)[0].astype(jnp.int32)
        valid = jnp.arange(slots, dtype=jnp.int32) < jnp.sum(picked.astype(jnp.int32))
        rows = normed[index]
        summed = jnp.zeros((slots, D), jnp.float32)
        for quarter in range(SPLIT):
            w_both = w_in[local * SPLIT + quarter, group]
            both = jnp.dot(rows, w_both, preferred_element_type=jnp.float32)
            act = (jax.nn.silu(both[:, :FFQ]) * both[:, FFQ:]).astype(jnp.bfloat16)
            part = jnp.dot(act, w_out[local * SPLIT + quarter, group], preferred_element_type=jnp.float32).astype(jnp.bfloat16)
            summed = summed + lax.optimization_barrier(part).astype(jnp.float32)
        factor = jnp.where(valid, weight_tok[index], 0.0)
        return (total_out.at[index].add(summed * factor[:, None]), None)
    moe_out, unused = lax.scan(one_expert, jnp.zeros((NEW_TOK, D), jnp.float32), jnp.arange(EXPERTS, dtype=jnp.int32))
    return (residual + moe_out).astype(jnp.bfloat16)
```

```python
import functools

import jax
import jax.numpy as jnp
from jax import lax
from jax.experimental import pallas as pl
from jax.experimental.pallas import tpu as pltpu
from jax.sharding import PartitionSpec as P

HD = 128
TOPK = 8
SPLIT = 4
FFQ = 384
GROUP = 16
CAP = 20
MESH = pl.DeviceIdType.MESH
ARRIVE = (1, 2, 6, 3, 7, 4, 5)


def rms_normed(residual, norm_gain):
    return (
        residual * lax.rsqrt(jnp.mean(residual * residual, 1, keepdims=True) + 1e-06) * norm_gain
    ).astype(jnp.bfloat16)


def place():
    ctx = lax.axis_index("ctx")
    return ctx // 8, (ctx // 2) % 4, ctx % 2, lax.axis_index("exp")


def ctx_of(hi, y, core):
    return lax.rem(hi, 4) * 8 + y * 2 + core


def remote(src, dst, send, recv, device):
    return pltpu.make_async_remote_copy(
        src_ref=src, dst_ref=dst, send_sem=send, recv_sem=recv, device_id=device, device_id_type=MESH
    )


def moe_kernel(
    normed,
    residual_own,
    pick,
    pick_rest,
    mix_hi,
    mix_lo,
    w_in,
    w_out,
    out_ref,
    sent,
    got,
    both,
    rest_in,
    act,
    rest_out,
    part,
    from_core,
    to_pair,
    from_pair,
    to_home,
    home,
    mixed,
    from_exp,
    d_send,
    d_recv,
    f_send,
    f_recv,
    c_send,
    c_recv,
    rc_send,
    rc_recv,
    rf_send,
    rf_recv,
    rd_send,
    rd_recv,
    x_send,
    x_recv,
):
    hi, y, core, e = place()
    width = sent.shape[-1]
    sibling = (ctx_of(hi, y, 1 - core), e)
    pair = (ctx_of(hi, y + 1 - 2 * lax.rem(y, 2), core), e)

    def there(i):
        return (ctx_of(hi + i // 2, y if i % 2 == 0 else 3 - y, core), e)

    def back(i):
        return (ctx_of(hi + 4 - i // 2, y if i % 2 == 0 else 3 - y, core), e)

    def other(d):
        return lax.rem(e + d, 8)

    barrier = pltpu.get_barrier_semaphore()
    for i in range(1, 8):
        pl.semaphore_signal(barrier, inc=1, device_id=there(i), device_id_type=MESH)
    pl.semaphore_signal(barrier, inc=1, device_id=sibling, device_id_type=MESH)
    pl.semaphore_signal(barrier, inc=1, device_id=pair, device_id_type=MESH)
    for d in range(1, 8):
        pl.semaphore_signal(
            barrier, inc=1, device_id=(lax.axis_index("ctx"), other(d)), device_id_type=MESH
        )

    for m in range(4):
        rows = jnp.dot(
            pick[...], normed[:, m * width : (m + 1) * width], preferred_element_type=jnp.float32
        )
        sent[:, m] = rows.astype(jnp.bfloat16).reshape(8, 16, width)
    rest = jnp.zeros((128, width), jnp.float32)
    for m in range(4):
        rest += jnp.dot(
            pick_rest[:, m * 128 : (m + 1) * 128],
            normed[:, m * width : (m + 1) * width],
            preferred_element_type=jnp.float32,
        )
    sent[:, 4] = rest.astype(jnp.bfloat16).reshape(8, 16, width)
    got[0] = sent[0]

    pl.semaphore_wait(barrier, 16)

    d_copy = [
        None if i == 0 else remote(sent.at[i], got.at[i], d_send.at[i], d_recv.at[i], there(i))
        for i in range(8)
    ]
    for i in (4, 5, 2, 6, 3, 7, 1):
        d_copy[i].start()
    f_copy = [
        remote(got.at[i], got.at[16 + i], f_send.at[i], f_recv.at[i], pair) for i in range(8)
    ]
    c_copy = [
        remote(got.at[i], got.at[8 + i], c_send.at[i], c_recv.at[i], sibling) for i in range(8)
    ] + [
        remote(got.at[16 + i], got.at[24 + i], c_send.at[8 + i], c_recv.at[8 + i], sibling)
        for i in range(8)
    ]
    order = (0,) + ARRIVE
    for n in range(8):
        i = order[n]
        if i > 0:
            d_copy[i].wait_recv()
        f_copy[i].start()
        c_copy[i].start()
        if n >= 2:
            f_copy[order[n - 2]].wait_recv()
            c_copy[8 + order[n - 2]].start()

    def regroup(m, rows, columns):
        row = lax.broadcasted_iota(jnp.int32, (rows, columns), 0)
        column = lax.broadcasted_iota(jnp.int32, (rows, columns), 1)
        small, large = (row, column) if rows < columns else (column, row)
        return (large == (small // 4) * 16 + m * 4 + small % 4).astype(jnp.bfloat16)

    def experts(base):
        rest_rows = got[base : base + 16, 4].reshape(256, width)
        for m in range(4):
            rest_in[:, m * width : (m + 1) * width] = jnp.dot(
                regroup(m, 64, 256), rest_rows, preferred_element_type=jnp.float32
            ).astype(jnp.bfloat16)

        @pl.loop(0, 3)
        def _(n):
            columns = pl.ds(pl.multiple_of(n * 256, 256), 256)
            total = jnp.zeros((320, 256), jnp.float32)
            for m in range(4):
                rows = jnp.concatenate(
                    [
                        got[base : base + 16, m].reshape(256, width),
                        rest_in[:, m * width : (m + 1) * width],
                    ],
                    0,
                )
                total += jnp.dot(
                    rows,
                    w_in[m * width : (m + 1) * width, columns],
                    preferred_element_type=jnp.float32,
                )
            both[:, columns] = total

        gate = both[:, :FFQ]
        act[...] = (gate / (1.0 + jnp.exp(-gate)) * both[:, FFQ:]).astype(jnp.bfloat16)
        steps = width // 256

        @pl.loop(0, 4 * steps)
        def _(n):
            columns = pl.ds(pl.multiple_of(n * 256, 256), 256)
            inner = pl.ds(pl.multiple_of((n % steps) * 256, 256), 256)
            result = jnp.dot(
                act[...], w_out[:, columns], preferred_element_type=jnp.float32
            ).astype(jnp.bfloat16)
            part[base : base + 16, n // steps, :, inner] = result[:256].reshape(16, 16, 256)
            rest_out[:, columns] = result[256:]

        rest_part = jnp.zeros((256, width), jnp.float32)
        for m in range(4):
            rest_part += jnp.dot(
                regroup(m, 256, 64),
                rest_out[:, m * width : (m + 1) * width],
                preferred_element_type=jnp.float32,
            )
        part[base : base + 16, 4] = rest_part.astype(jnp.bfloat16).reshape(16, 16, width)

    for i in order:
        c_copy[i].wait_recv()
    experts(0)
    rc_copy = [
        remote(part.at[8 + i], from_core.at[i], rc_send.at[i], rc_recv.at[i], sibling)
        for i in range(8)
    ] + [
        remote(part.at[24 + i], from_core.at[8 + i], rc_send.at[8 + i], rc_recv.at[8 + i], sibling)
        for i in range(8)
    ]
    for i in order:
        rc_copy[i].start()
    for n in (6, 7):
        f_copy[order[n]].wait_recv()
        c_copy[8 + order[n]].start()
    for i in order:
        c_copy[8 + i].wait_recv()
    experts(16)
    for i in order:
        rc_copy[8 + i].start()

    rf_copy = [
        remote(to_pair.at[i], from_pair.at[i], rf_send.at[i], rf_recv.at[i], pair)
        for i in range(8)
    ]
    rd_copy = [
        None if i == 0 else remote(to_home.at[i], home.at[i], rd_send.at[i], rd_recv.at[i], back(i))
        for i in range(8)
    ]
    final = (4, 5, 2, 6, 3, 7, 1, 0)
    for i in final:
        rc_copy[8 + i].wait_recv()
        to_pair[i] = (
            part[16 + i].astype(jnp.float32) + from_core[8 + i].astype(jnp.float32)
        ).astype(jnp.bfloat16)
        rf_copy[i].start()
    for i in final:
        rc_copy[i].wait_recv()
        rf_copy[i].wait_recv()
        total = (
            part[i].astype(jnp.float32)
            + from_core[i].astype(jnp.float32)
            + from_pair[i].astype(jnp.float32)
        ).astype(jnp.bfloat16)
        if i == 0:
            home[0] = total
        else:
            to_home[i] = total
            rd_copy[i].start()
    for i in ARRIVE:
        rd_copy[i].wait_recv()

    for m in range(4):
        rows = jnp.concatenate(
            [home[:, m].reshape(128, width), home[:, 4].reshape(128, width)], 0
        )
        mixed[:, m * width : (m + 1) * width] = (
            jnp.dot(mix_hi[m], rows, preferred_element_type=jnp.float32)
            + jnp.dot(mix_lo[m], rows, preferred_element_type=jnp.float32)
        ).astype(jnp.bfloat16)

    x_copy = [None]
    for d in range(1, 8):
        own = pl.ds(pl.multiple_of(other(d) * 16, 16), 16)
        x_copy.append(
            remote(
                mixed.at[own],
                from_exp.at[d],
                x_send.at[d],
                x_recv.at[d],
                (lax.axis_index("ctx"), other(d)),
            )
        )
        x_copy[d].start()
    total = (
        residual_own[...] + mixed[pl.ds(pl.multiple_of(e * 16, 16), 16), :].astype(jnp.float32)
    )
    for d in range(1, 8):
        x_copy[d].wait_recv()
        total += from_exp[d].astype(jnp.float32)
    out_ref[...] = total.astype(jnp.bfloat16)

    for i in range(8):
        if i > 0:
            d_copy[i].wait_send()
            rd_copy[i].wait_send()
            x_copy[i].wait_send()
        f_copy[i].wait_send()
        rf_copy[i].wait_send()
    for i in range(16):
        c_copy[i].wait_send()
        rc_copy[i].wait_send()


def moe(normed, residual_own, pick, pick_rest, mix_hi, mix_lo, w_in, w_out):
    model = normed.shape[1]
    width = model // 4
    block = (5, 16, width)
    half = jnp.bfloat16
    vmem = pl.BlockSpec(memory_space=pltpu.VMEM)
    dma = pltpu.SemaphoreType.DMA
    return pl.pallas_call(
        moe_kernel,
        out_shape=jax.ShapeDtypeStruct(residual_own.shape, half),
        in_specs=[vmem] * 8,
        out_specs=vmem,
        scratch_shapes=[
            pltpu.VMEM((8,) + block, half),
            pltpu.VMEM((32,) + block, half),
            pltpu.VMEM((320, 2 * FFQ), jnp.float32),
            pltpu.VMEM((64, model), half),
            pltpu.VMEM((320, FFQ), half),
            pltpu.VMEM((64, model), half),
            pltpu.VMEM((32,) + block, half),
            pltpu.VMEM((16,) + block, half),
            pltpu.VMEM((8,) + block, half),
            pltpu.VMEM((8,) + block, half),
            pltpu.VMEM((8,) + block, half),
            pltpu.VMEM((8,) + block, half),
            pltpu.VMEM((128, model), half),
            pltpu.VMEM((8, 16, model), half),
            dma((8,)),
            dma((8,)),
            dma((8,)),
            dma((8,)),
            dma((16,)),
            dma((16,)),
            dma((16,)),
            dma((16,)),
            dma((8,)),
            dma((8,)),
            dma((8,)),
            dma((8,)),
            dma((8,)),
            dma((8,)),
        ],
        compiler_params=pltpu.CompilerParams(
            collective_id=1, has_side_effects=True, vmem_limit_bytes=56 * 2**20
        ),
        name="moe",
    )(normed, residual_own, pick, pick_rest, mix_hi, mix_lo, w_in, w_out)


def tables(expert_ids, gate_weights):
    hi, y, core, e = place()
    i = jnp.arange(8, dtype=jnp.int32)
    local = ((hi + i // 2) % 4) * 2 + ((y // 2) + i) % 2
    expert = e * 8 + local
    ids = expert_ids.T
    hits = ids[None, :, :] == expert[:, None, None]
    member = jnp.any(hits, 1)
    gate = jnp.sum(jnp.where(hits, gate_weights.T[None], 0.0), 1)
    before = jnp.arange(128)[:, None] < jnp.arange(128)[None, :]
    rank = jnp.dot(
        member.astype(jnp.bfloat16), before.astype(jnp.bfloat16), preferred_element_type=jnp.float32
    ).astype(jnp.int32)
    slot = jnp.where(member, rank, -1)
    r = jnp.arange(16, dtype=jnp.int32)
    pick = slot[:, None, :] == r[None, :, None]
    m = jnp.arange(4, dtype=jnp.int32)
    rest = (slot[:, None, None, :] == 16 + (r % 4)[None, :, None, None]) & (
        (r // 4)[None, :, None, None] == m[None, None, :, None]
    )
    mix = jnp.where(pick, gate[:, None, :], 0.0).reshape(128, 128).T
    mix_rest = jnp.where(rest, gate[:, None, None, :], 0.0).reshape(128, 4, 128).transpose(1, 2, 0)
    mix = jnp.concatenate([jnp.broadcast_to(mix[None], (4, 128, 128)), mix_rest], 2)
    mix_hi = mix.astype(jnp.bfloat16)
    mix_lo = (mix - mix_hi.astype(jnp.float32)).astype(jnp.bfloat16)
    return (
        pick.reshape(128, 128).astype(jnp.bfloat16),
        rest.reshape(128, 512).astype(jnp.bfloat16),
        mix_hi,
        mix_lo,
    )


def per_device(
    query,
    new_kv,
    old_kv,
    new_pos,
    o_weight,
    hidden,
    norm_gain,
    expert_ids,
    gate_weights,
    w_in,
    w_out,
):
    exp_index = lax.axis_index("exp")
    n_exp = lax.axis_size("exp")
    rows = query.shape[0]
    heads_here = query.shape[1] // HD
    kv_here = max(1, heads_here // GROUP)
    per_kv = heads_here // kv_here
    kv_first = exp_index * heads_here // GROUP
    new_sel = lax.dynamic_slice_in_dim(new_kv, kv_first * HD, kv_here * HD, 2)
    old_sel = lax.dynamic_slice_in_dim(old_kv, kv_first * HD, kv_here * HD, 2)
    queries = query.reshape(rows, kv_here, per_kv, HD)
    scale = 1.0 / HD**0.5
    pos_row = new_pos.reshape(1, rows)
    old_piece = lax.all_gather(old_sel, "ctx", axis=1, tiled=True)
    new_piece = lax.all_gather(new_sel, "ctx", axis=1, tiled=True)
    pos_piece = lax.all_gather(pos_row, "ctx", axis=1, tiled=True)
    keys = jnp.concatenate([old_piece[0], new_piece[0]], 0).reshape(-1, kv_here, HD)
    values = jnp.concatenate([old_piece[1], new_piece[1]], 0).reshape(-1, kv_here, HD)
    allowed = jnp.concatenate(
        [jnp.ones((rows, old_piece.shape[1]), bool), pos_piece[0][None, :] <= new_pos[:, None]], 1
    )
    mask_full = allowed[:, None, None, :]
    scores = jnp.einsum("qkgd,nkd->qkgn", queries, keys, preferred_element_type=jnp.float32) * scale
    scores = jnp.where(mask_full, scores, -1e30)
    top_new = jnp.max(scores, -1)
    weights = jnp.where(mask_full, jnp.exp(scores - top_new[..., None]), 0.0)
    total_new = jnp.sum(weights, -1)
    acc_new = jnp.einsum(
        "qkgn,nkd->qkgd", weights.astype(jnp.bfloat16), values, preferred_element_type=jnp.float32
    )
    attended = (acc_new / total_new[..., None]).reshape(rows, heads_here * HD).astype(jnp.bfloat16)
    projected = jnp.dot(
        attended,
        lax.all_gather(o_weight, "ctx", axis=1, tiled=True),
        preferred_element_type=jnp.float32,
    )
    own_rows = rows // n_exp
    own_part = lax.dynamic_slice_in_dim(
        projected, exp_index * own_rows, own_rows, 0
    ) + hidden.astype(jnp.float32)
    term = lax.dynamic_update_slice_in_dim(projected, own_part, exp_index * own_rows, 0)
    residual_all = lax.psum(term.astype(jnp.bfloat16), "exp").astype(jnp.float32)
    normed_all = rms_normed(residual_all, norm_gain)
    residual_own = lax.dynamic_slice_in_dim(residual_all, exp_index * own_rows, own_rows, 0)
    return moe(
        normed_all, residual_own, *tables(expert_ids, gate_weights), w_in[0, 0], w_out[0, 0]
    )


def solution(mesh):
    return jax.shard_map(
        per_device,
        mesh=mesh,
        in_specs=(
            P("ctx", "exp"),
            P(None, "ctx", None),
            P(None, "ctx", None),
            P("ctx"),
            P("exp", "ctx"),
            P(("ctx", "exp"), None),
            P(),
            P("ctx", None),
            P("ctx", None),
            P("ctx", "exp", None, None),
            P("ctx", "exp", None, None),
        ),
        out_specs=P(("ctx", "exp"), None),
        check_vma=False,
    )
```

```python
import jax
import jax.numpy as jnp
from jax import lax
from jax.experimental import pallas as pl
from jax.experimental.pallas import tpu as pltpu
from jax.sharding import PartitionSpec as P

HD = 128
FFQ = 384
MESH = pl.DeviceIdType.MESH
ARRIVE = (1, 2, 6, 3, 7, 4, 5)


def place():
    ctx = lax.axis_index("ctx")
    return ctx // 8, (ctx // 2) % 4, ctx % 2, lax.axis_index("exp")


def ctx_of(hi, y, core):
    return lax.rem(hi, 4) * 8 + y * 2 + core


def remote(src, dst, send, recv, device):
    return pltpu.make_async_remote_copy(
        src_ref=src, dst_ref=dst, send_sem=send, recv_sem=recv, device_id=device, device_id_type=MESH
    )


def attention_kernel(
    query,
    new_kv,
    old_kv,
    new_pos,
    o_weight,
    hidden,
    norm_gain,
    normed_ref,
    residual_ref,
    kv,
    weight,
    queries,
    bias,
    top,
    acc,
    attended,
    projected,
    from_exp,
    own_normed,
    normed,
    kz_send,
    kz_recv,
    ky_send,
    ky_recv,
    kc_send,
    kc_recv,
    wz_send,
    wz_recv,
    wy_send,
    wy_recv,
    wc_send,
    wc_recv,
    x_send,
    x_recv,
    n_send,
    n_recv,
):
    hi, y, core, e = place()
    ctx = lax.axis_index("ctx")
    model = hidden.shape[1]
    sibling = (ctx_of(hi, y, 1 - core), e)
    up = (ctx_of(hi, lax.rem(y + 1, 4), core), e)
    down = (ctx_of(hi, lax.rem(y + 3, 4), core), e)

    def along(d):
        return (ctx_of(hi + d, y, core), e)

    def other(d):
        return lax.rem(e + d, 8)

    barrier = pltpu.get_barrier_semaphore()
    for device in (along(1), along(2), along(3), up, down, sibling):
        pl.semaphore_signal(barrier, inc=1, device_id=device, device_id_type=MESH)
    for d in range(1, 8):
        pl.semaphore_signal(barrier, inc=1, device_id=(ctx, other(d)), device_id_type=MESH)

    lanes = pl.ds(pl.multiple_of((e // 2) * HD, HD), HD)
    kv[0, 0:256] = old_kv[0, :, lanes]
    kv[0, 256:384] = new_kv[0, :, lanes]
    for b in range(3):
        values = new_kv[1, :, lanes] if b == 2 else old_kv[1, b * 128 : (b + 1) * 128, lanes]
        kv[0, 384 + b * 128 : 512 + b * 128] = values.astype(jnp.float32).T.astype(jnp.bfloat16)
    own_pos = new_pos[...]
    row = lax.broadcasted_iota(jnp.int32, (16, 128), 0)
    kv[0, 768:784] = (
        jnp.where(row == 0, own_pos >> 6, jnp.where(row == 1, own_pos & 63, 0))
        .astype(jnp.float32)
        .astype(jnp.bfloat16)
    )
    weight[0] = o_weight[...]

    pl.semaphore_wait(barrier, 13)

    def gather(blocks, z_send, z_recv, y_send, y_recv, c_send, c_recv):
        z_copy = [None] + [
            remote(blocks.at[0], blocks.at[d], z_send.at[d], z_recv.at[d], along(d))
            for d in range(1, 4)
        ]
        y_copy = {}
        for d in range(4):
            for dy, device in ((1, up), (3, down)):
                y_copy[dy, d] = remote(
                    blocks.at[d],
                    blocks.at[dy * 4 + d],
                    y_send.at[dy * 4 + d],
                    y_recv.at[dy * 4 + d],
                    device,
                )
            source = 4 + d if d % 2 == 0 else 12 + d
            y_copy[2, d] = remote(
                blocks.at[source],
                blocks.at[8 + d],
                y_send.at[8 + d],
                y_recv.at[8 + d],
                up if d % 2 == 0 else down,
            )
        c_copy = [
            remote(blocks.at[s], blocks.at[16 + s], c_send.at[s], c_recv.at[s], sibling)
            for s in range(16)
        ]
        return z_copy, y_copy, c_copy

    kz, ky, kc = gather(kv, kz_send, kz_recv, ky_send, ky_recv, kc_send, kc_recv)
    wz, wy, wc = gather(weight, wz_send, wz_recv, wy_send, wy_recv, wc_send, wc_recv)

    def begin_y(y_copy, c_copy, d):
        y_copy[1, d].start()
        y_copy[3, d].start()
        c_copy[d].start()

    def pass_on(y_copy, c_copy, d):
        y_copy[1, d].wait_recv()
        if d % 2 == 0:
            y_copy[2, d].start()
        c_copy[4 + d].start()
        y_copy[3, d].wait_recv()
        if d % 2 == 1:
            y_copy[2, d].start()
        c_copy[12 + d].start()

    def last(y_copy, c_copy, d):
        y_copy[2, d].wait_recv()
        c_copy[8 + d].start()

    near = (0, 1, 3, 2)
    for d in (1, 3, 2):
        kz[d].start()
    begin_y(ky, kc, 0)

    for h in range(8):
        part = query[:, h * HD : (h + 1) * HD].astype(jnp.float32).T.astype(jnp.bfloat16)
        queries[h // 2, :, (h % 2) * 128 : (h % 2 + 1) * 128] = part
    top[...] = jnp.full_like(top, -1e30)
    acc[...] = jnp.zeros_like(acc)
    factor = 1.4426950408889634 / HD**0.5

    def attend(group):
        base = group * 4
        for b in range(4):
            digits = kv[base + b, 768:784].astype(jnp.float32)
            place_of = digits[0:1] * 64.0 + digits[1:2]
            column = jnp.broadcast_to(place_of, (128, 128)).T
            seen = column <= own_pos.astype(jnp.float32)
            bias[b] = jnp.where(seen, 0.0, -1e30)

        @pl.loop(0, 4)
        def _(t):
            part = queries[t]
            pieces = []
            for b in range(4):
                scores = jnp.dot(kv[base + b, 0:384], part, preferred_element_type=jnp.float32)
                wide = jnp.concatenate([bias[b], bias[b]], 1)
                pieces += [scores[:256], scores[256:] + wide]
            old_top = top[t, 0:1]
            new_top = old_top
            for piece in pieces:
                new_top = jnp.maximum(new_top, jnp.max(piece, 0, keepdims=True))
            probs = jnp.concatenate(
                [jnp.exp2((piece - new_top) * factor).astype(jnp.bfloat16) for piece in pieces], 0
            )
            values = jnp.concatenate(
                [
                    kv[base + b, 384 + 128 * i : 512 + 128 * i]
                    for b in range(4)
                    for i in range(3)
                ],
                1,
            )
            ones = jnp.ones((16, values.shape[1]), jnp.bfloat16)
            added = jnp.dot(
                jnp.concatenate([values, ones], 0), probs, preferred_element_type=jnp.float32
            )
            acc[t] = acc[t] * jnp.exp2((old_top - new_top) * factor) + added
            top[t] = jnp.broadcast_to(new_top, (8, 256))

    for d in (1, 3, 2):
        kz[d].wait_recv()
        begin_y(ky, kc, d)
    for d in (1, 3, 2):
        wz[d].start()
    attend(0)
    for d in near:
        pass_on(ky, kc, d)
    begin_y(wy, wc, 0)
    for d in near:
        kc[d].wait_recv()
    attend(4)
    for d in (1, 3, 2):
        wz[d].wait_recv()
        begin_y(wy, wc, d)
    attend(1)
    for d in near:
        last(ky, kc, d)
    attend(3)
    for d in near:
        pass_on(wy, wc, d)
    attend(2)
    for d in near:
        kc[4 + d].wait_recv()
    attend(5)
    for d in near:
        kc[12 + d].wait_recv()
    attend(7)
    for d in near:
        last(wy, wc, d)
    for d in near:
        kc[8 + d].wait_recv()
    attend(6)

    for h in range(8):
        part = slice((h % 2) * 128, (h % 2 + 1) * 128)
        scaled = acc[h // 2, 0:128, part] / acc[h // 2, 128:129, part]
        attended[:, h * HD : (h + 1) * HD] = scaled.T.astype(jnp.bfloat16)
    for s in range(16):
        wc[s].wait_recv()

    def column_of(slot):
        k, dy, dh = slot // 16, (slot // 4) % 4, slot % 4
        owner = ctx_of(hi + 4 - dh, lax.rem(y + 4 - dy, 4), lax.rem(core + k, 2))
        return pl.ds(pl.multiple_of(owner * 128, 128), 128)

    @pl.loop(0, 16)
    def _(n):
        both = jnp.concatenate([weight[2 * n], weight[2 * n + 1]], 1)
        result = jnp.dot(attended[...], both, preferred_element_type=jnp.float32)
        result = result.astype(jnp.bfloat16)
        projected[:, column_of(2 * n)] = result[:, :128]
        projected[:, column_of(2 * n + 1)] = result[:, 128:]

    def rows_of(index):
        return pl.ds(pl.multiple_of(index * 16, 16), 16)

    x_copy = [None] + [
        remote(
            projected.at[rows_of(other(d))],
            from_exp.at[d],
            x_send.at[d],
            x_recv.at[d],
            (ctx, other(d)),
        )
        for d in range(1, 8)
    ]
    for d in range(1, 8):
        x_copy[d].start()
    residual = hidden[...].astype(jnp.float32) + projected[rows_of(e), :].astype(jnp.float32)
    for d in range(1, 8):
        x_copy[d].wait_recv()
        residual += from_exp[d].astype(jnp.float32)
    residual_ref[...] = residual
    mean = jnp.sum(residual * residual, 1, keepdims=True) * (1.0 / model)
    own = (residual * lax.rsqrt(mean + 1e-06) * norm_gain[...]).astype(jnp.bfloat16)
    own_normed[...] = own
    n_copy = [None] + [
        remote(own_normed, normed.at[rows_of(e)], n_send.at[d], n_recv.at[d], (ctx, other(d)))
        for d in range(1, 8)
    ]
    for d in range(1, 8):
        n_copy[d].start()
    normed[rows_of(e), :] = own
    for d in range(1, 8):
        n_copy[d].wait_recv()
    normed_ref[...] = normed[...]

    for d in range(1, 4):
        kz[d].wait_send()
        wz[d].wait_send()
    for d in range(4):
        for dy in range(1, 4):
            ky[dy, d].wait_send()
            wy[dy, d].wait_send()
    for s in range(16):
        kc[s].wait_send()
        wc[s].wait_send()
    for d in range(1, 8):
        x_copy[d].wait_send()
        n_copy[d].wait_send()


def attention(query, new_kv, old_kv, new_pos, o_weight, hidden, norm_gain):
    rows = query.shape[0]
    model = hidden.shape[1]
    half = jnp.bfloat16
    vmem = pl.BlockSpec(memory_space=pltpu.VMEM)
    dma = pltpu.SemaphoreType.DMA
    return pl.pallas_call(
        attention_kernel,
        out_shape=(
            jax.ShapeDtypeStruct((rows, model), half),
            jax.ShapeDtypeStruct(hidden.shape, jnp.float32),
        ),
        in_specs=[vmem] * 7,
        out_specs=(vmem, vmem),
        scratch_shapes=[
            pltpu.VMEM((32, 784, HD), half),
            pltpu.VMEM((32,) + o_weight.shape, half),
            pltpu.VMEM((4, HD, 256), half),
            pltpu.VMEM((4, 128, 128), jnp.float32),
            pltpu.VMEM((4, 8, 256), jnp.float32),
            pltpu.VMEM((4, 144, 256), jnp.float32),
            pltpu.VMEM(query.shape, half),
            pltpu.VMEM((rows, model), half),
            pltpu.VMEM((8, 16, model), half),
            pltpu.VMEM((16, model), half),
            pltpu.VMEM((rows, model), half),
            dma((4,)),
            dma((4,)),
            dma((16,)),
            dma((16,)),
            dma((16,)),
            dma((16,)),
            dma((4,)),
            dma((4,)),
            dma((16,)),
            dma((16,)),
            dma((16,)),
            dma((16,)),
            dma((8,)),
            dma((8,)),
            dma((8,)),
            dma((8,)),
        ],
        compiler_params=pltpu.CompilerParams(
            collective_id=2, has_side_effects=True, vmem_limit_bytes=56 * 2**20
        ),
        name="attention",
    )(query, new_kv, old_kv, new_pos.reshape(1, rows), o_weight, hidden, norm_gain.reshape(1, model))


def moe_kernel(
    normed,
    residual_own,
    pick,
    pick_rest,
    mix_hi,
    mix_lo,
    w_in,
    w_out,
    out_ref,
    sent,
    got,
    both,
    rest_in,
    act,
    rest_out,
    part,
    from_core,
    to_pair,
    from_pair,
    to_home,
    home,
    mixed,
    from_exp,
    d_send,
    d_recv,
    f_send,
    f_recv,
    c_send,
    c_recv,
    rc_send,
    rc_recv,
    rf_send,
    rf_recv,
    rd_send,
    rd_recv,
    x_send,
    x_recv,
):
    hi, y, core, e = place()
    width = sent.shape[-1]
    sibling = (ctx_of(hi, y, 1 - core), e)
    pair = (ctx_of(hi, y + 1 - 2 * lax.rem(y, 2), core), e)

    def there(i):
        return (ctx_of(hi + i // 2, y if i % 2 == 0 else 3 - y, core), e)

    def back(i):
        return (ctx_of(hi + 4 - i // 2, y if i % 2 == 0 else 3 - y, core), e)

    def other(d):
        return lax.rem(e + d, 8)

    barrier = pltpu.get_barrier_semaphore()
    for i in range(1, 8):
        pl.semaphore_signal(barrier, inc=1, device_id=there(i), device_id_type=MESH)
    pl.semaphore_signal(barrier, inc=1, device_id=sibling, device_id_type=MESH)
    pl.semaphore_signal(barrier, inc=1, device_id=pair, device_id_type=MESH)
    for d in range(1, 8):
        pl.semaphore_signal(
            barrier, inc=1, device_id=(lax.axis_index("ctx"), other(d)), device_id_type=MESH
        )

    for m in range(4):
        rows = jnp.dot(
            pick[...], normed[:, m * width : (m + 1) * width], preferred_element_type=jnp.float32
        )
        sent[:, m] = rows.astype(jnp.bfloat16).reshape(8, 16, width)
    rest = jnp.zeros((128, width), jnp.float32)
    for m in range(4):
        rest += jnp.dot(
            pick_rest[:, m * 128 : (m + 1) * 128],
            normed[:, m * width : (m + 1) * width],
            preferred_element_type=jnp.float32,
        )
    sent[:, 4] = rest.astype(jnp.bfloat16).reshape(8, 16, width)
    got[0] = sent[0]

    pl.semaphore_wait(barrier, 16)

    d_copy = [
        None if i == 0 else remote(sent.at[i], got.at[i], d_send.at[i], d_recv.at[i], there(i))
        for i in range(8)
    ]
    for i in (4, 5, 2, 6, 3, 7, 1):
        d_copy[i].start()
    f_copy = [
        remote(got.at[i], got.at[16 + i], f_send.at[i], f_recv.at[i], pair) for i in range(8)
    ]
    c_copy = [
        remote(got.at[i], got.at[8 + i], c_send.at[i], c_recv.at[i], sibling) for i in range(8)
    ] + [
        remote(got.at[16 + i], got.at[24 + i], c_send.at[8 + i], c_recv.at[8 + i], sibling)
        for i in range(8)
    ]
    order = (0,) + ARRIVE
    for n in range(8):
        i = order[n]
        if i > 0:
            d_copy[i].wait_recv()
        f_copy[i].start()
        c_copy[i].start()
        if n >= 2:
            f_copy[order[n - 2]].wait_recv()
            c_copy[8 + order[n - 2]].start()

    def regroup(m, rows, columns):
        row = lax.broadcasted_iota(jnp.int32, (rows, columns), 0)
        column = lax.broadcasted_iota(jnp.int32, (rows, columns), 1)
        small, large = (row, column) if rows < columns else (column, row)
        return (large == (small // 4) * 16 + m * 4 + small % 4).astype(jnp.bfloat16)

    def experts(base):
        rest_rows = got[base : base + 16, 4].reshape(256, width)
        for m in range(4):
            rest_in[:, m * width : (m + 1) * width] = jnp.dot(
                regroup(m, 64, 256), rest_rows, preferred_element_type=jnp.float32
            ).astype(jnp.bfloat16)

        @pl.loop(0, 3)
        def _(n):
            columns = pl.ds(pl.multiple_of(n * 256, 256), 256)
            total = jnp.zeros((320, 256), jnp.float32)
            for m in range(4):
                rows = jnp.concatenate(
                    [
                        got[base : base + 16, m].reshape(256, width),
                        rest_in[:, m * width : (m + 1) * width],
                    ],
                    0,
                )
                total += jnp.dot(
                    rows,
                    w_in[m * width : (m + 1) * width, columns],
                    preferred_element_type=jnp.float32,
                )
            both[:, columns] = total

        gate = both[:, :FFQ]
        act[...] = (gate / (1.0 + jnp.exp(-gate)) * both[:, FFQ:]).astype(jnp.bfloat16)
        steps = width // 256

        @pl.loop(0, 4 * steps)
        def _(n):
            columns = pl.ds(pl.multiple_of(n * 256, 256), 256)
            inner = pl.ds(pl.multiple_of((n % steps) * 256, 256), 256)
            result = jnp.dot(
                act[...], w_out[:, columns], preferred_element_type=jnp.float32
            ).astype(jnp.bfloat16)
            part[base : base + 16, n // steps, :, inner] = result[:256].reshape(16, 16, 256)
            rest_out[:, columns] = result[256:]

        rest_part = jnp.zeros((256, width), jnp.float32)
        for m in range(4):
            rest_part += jnp.dot(
                regroup(m, 256, 64),
                rest_out[:, m * width : (m + 1) * width],
                preferred_element_type=jnp.float32,
            )
        part[base : base + 16, 4] = rest_part.astype(jnp.bfloat16).reshape(16, 16, width)

    for i in order:
        c_copy[i].wait_recv()
    experts(0)
    rc_copy = [
        remote(part.at[8 + i], from_core.at[i], rc_send.at[i], rc_recv.at[i], sibling)
        for i in range(8)
    ] + [
        remote(part.at[24 + i], from_core.at[8 + i], rc_send.at[8 + i], rc_recv.at[8 + i], sibling)
        for i in range(8)
    ]
    for i in order:
        rc_copy[i].start()
    for n in (6, 7):
        f_copy[order[n]].wait_recv()
        c_copy[8 + order[n]].start()
    for i in order:
        c_copy[8 + i].wait_recv()
    experts(16)
    for i in order:
        rc_copy[8 + i].start()

    rf_copy = [
        remote(to_pair.at[i], from_pair.at[i], rf_send.at[i], rf_recv.at[i], pair)
        for i in range(8)
    ]
    rd_copy = [
        None if i == 0 else remote(to_home.at[i], home.at[i], rd_send.at[i], rd_recv.at[i], back(i))
        for i in range(8)
    ]
    final = (4, 5, 2, 6, 3, 7, 1, 0)
    for i in final:
        rc_copy[8 + i].wait_recv()
        to_pair[i] = (
            part[16 + i].astype(jnp.float32) + from_core[8 + i].astype(jnp.float32)
        ).astype(jnp.bfloat16)
        rf_copy[i].start()
    for i in final:
        rc_copy[i].wait_recv()
        rf_copy[i].wait_recv()
        total = (
            part[i].astype(jnp.float32)
            + from_core[i].astype(jnp.float32)
            + from_pair[i].astype(jnp.float32)
        ).astype(jnp.bfloat16)
        if i == 0:
            home[0] = total
        else:
            to_home[i] = total
            rd_copy[i].start()
    for i in ARRIVE:
        rd_copy[i].wait_recv()

    for m in range(4):
        rows = jnp.concatenate(
            [home[:, m].reshape(128, width), home[:, 4].reshape(128, width)], 0
        )
        mixed[:, m * width : (m + 1) * width] = (
            jnp.dot(mix_hi[m], rows, preferred_element_type=jnp.float32)
            + jnp.dot(mix_lo[m], rows, preferred_element_type=jnp.float32)
        ).astype(jnp.bfloat16)

    x_copy = [None]
    for d in range(1, 8):
        own = pl.ds(pl.multiple_of(other(d) * 16, 16), 16)
        x_copy.append(
            remote(
                mixed.at[own],
                from_exp.at[d],
                x_send.at[d],
                x_recv.at[d],
                (lax.axis_index("ctx"), other(d)),
            )
        )
        x_copy[d].start()
    total = (
        residual_own[...] + mixed[pl.ds(pl.multiple_of(e * 16, 16), 16), :].astype(jnp.float32)
    )
    for d in range(1, 8):
        x_copy[d].wait_recv()
        total += from_exp[d].astype(jnp.float32)
    out_ref[...] = total.astype(jnp.bfloat16)

    for i in range(8):
        if i > 0:
            d_copy[i].wait_send()
            rd_copy[i].wait_send()
            x_copy[i].wait_send()
        f_copy[i].wait_send()
        rf_copy[i].wait_send()
    for i in range(16):
        c_copy[i].wait_send()
        rc_copy[i].wait_send()


def moe(normed, residual_own, pick, pick_rest, mix_hi, mix_lo, w_in, w_out):
    model = normed.shape[1]
    width = model // 4
    block = (5, 16, width)
    half = jnp.bfloat16
    vmem = pl.BlockSpec(memory_space=pltpu.VMEM)
    dma = pltpu.SemaphoreType.DMA
    return pl.pallas_call(
        moe_kernel,
        out_shape=jax.ShapeDtypeStruct(residual_own.shape, half),
        in_specs=[vmem] * 8,
        out_specs=vmem,
        scratch_shapes=[
            pltpu.VMEM((8,) + block, half),
            pltpu.VMEM((32,) + block, half),
            pltpu.VMEM((320, 2 * FFQ), jnp.float32),
            pltpu.VMEM((64, model), half),
            pltpu.VMEM((320, FFQ), half),
            pltpu.VMEM((64, model), half),
            pltpu.VMEM((32,) + block, half),
            pltpu.VMEM((16,) + block, half),
            pltpu.VMEM((8,) + block, half),
            pltpu.VMEM((8,) + block, half),
            pltpu.VMEM((8,) + block, half),
            pltpu.VMEM((8,) + block, half),
            pltpu.VMEM((128, model), half),
            pltpu.VMEM((8, 16, model), half),
            dma((8,)),
            dma((8,)),
            dma((8,)),
            dma((8,)),
            dma((16,)),
            dma((16,)),
            dma((16,)),
            dma((16,)),
            dma((8,)),
            dma((8,)),
            dma((8,)),
            dma((8,)),
            dma((8,)),
            dma((8,)),
        ],
        compiler_params=pltpu.CompilerParams(
            collective_id=1, has_side_effects=True, vmem_limit_bytes=56 * 2**20
        ),
        name="moe",
    )(normed, residual_own, pick, pick_rest, mix_hi, mix_lo, w_in, w_out)


def tables(expert_ids, gate_weights):
    hi, y, core, e = place()
    i = jnp.arange(8, dtype=jnp.int32)
    local = ((hi + i // 2) % 4) * 2 + ((y // 2) + i) % 2
    expert = e * 8 + local
    ids = expert_ids.T
    hits = ids[None, :, :] == expert[:, None, None]
    member = jnp.any(hits, 1)
    gate = jnp.sum(jnp.where(hits, gate_weights.T[None], 0.0), 1)
    before = jnp.arange(128)[:, None] < jnp.arange(128)[None, :]
    rank = jnp.dot(
        member.astype(jnp.bfloat16), before.astype(jnp.bfloat16), preferred_element_type=jnp.float32
    ).astype(jnp.int32)
    slot = jnp.where(member, rank, -1)
    r = jnp.arange(16, dtype=jnp.int32)
    pick = slot[:, None, :] == r[None, :, None]
    m = jnp.arange(4, dtype=jnp.int32)
    rest = (slot[:, None, None, :] == 16 + (r % 4)[None, :, None, None]) & (
        (r // 4)[None, :, None, None] == m[None, None, :, None]
    )
    mix = jnp.where(pick, gate[:, None, :], 0.0).reshape(128, 128).T
    mix_rest = jnp.where(rest, gate[:, None, None, :], 0.0).reshape(128, 4, 128).transpose(1, 2, 0)
    mix = jnp.concatenate([jnp.broadcast_to(mix[None], (4, 128, 128)), mix_rest], 2)
    mix_hi = mix.astype(jnp.bfloat16)
    mix_lo = (mix - mix_hi.astype(jnp.float32)).astype(jnp.bfloat16)
    return (
        pick.reshape(128, 128).astype(jnp.bfloat16),
        rest.reshape(128, 512).astype(jnp.bfloat16),
        mix_hi,
        mix_lo,
    )


def per_device(
    query,
    new_kv,
    old_kv,
    new_pos,
    o_weight,
    hidden,
    norm_gain,
    expert_ids,
    gate_weights,
    w_in,
    w_out,
):
    normed, residual_own = attention(
        query, new_kv, old_kv, new_pos, o_weight, hidden, norm_gain
    )
    return moe(
        normed, residual_own, *tables(expert_ids, gate_weights), w_in[0, 0], w_out[0, 0]
    )


def solution(mesh):
    return jax.shard_map(
        per_device,
        mesh=mesh,
        in_specs=(
            P("ctx", "exp"),
            P(None, "ctx", None),
            P(None, "ctx", None),
            P("ctx"),
            P("exp", "ctx"),
            P(("ctx", "exp"), None),
            P(),
            P("ctx", None),
            P("ctx", None),
            P("ctx", "exp", None, None),
            P("ctx", "exp", None, None),
        ),
        out_specs=P(("ctx", "exp"), None),
        check_vma=False,
    )
```

```python
import jax
import jax.numpy as jnp
from jax import lax
from jax.experimental import pallas as pl
from jax.experimental.pallas import tpu as pltpu
from jax.sharding import PartitionSpec as P

HD = 128
FFQ = 384
MESH = pl.DeviceIdType.MESH
ARRIVE = (1, 2, 6, 3, 7, 4, 5)


def place():
    ctx = lax.axis_index("ctx")
    return ctx // 8, (ctx // 2) % 4, ctx % 2, lax.axis_index("exp")


def ctx_of(hi, y, core):
    return lax.rem(hi, 4) * 8 + y * 2 + core


def remote(src, dst, send, recv, device):
    return pltpu.make_async_remote_copy(
        src_ref=src, dst_ref=dst, send_sem=send, recv_sem=recv, device_id=device, device_id_type=MESH
    )


def attention_kernel(
    query,
    new_kv,
    old_kv,
    new_pos,
    o_weight,
    hidden,
    norm_gain,
    normed_ref,
    residual_ref,
    kv,
    weight,
    queries,
    bias,
    top,
    acc,
    attended,
    projected,
    from_exp,
    own_normed,
    normed,
    kz_send,
    kz_recv,
    ky_send,
    ky_recv,
    kc_send,
    kc_recv,
    wz_send,
    wz_recv,
    wy_send,
    wy_recv,
    wc_send,
    wc_recv,
    x_send,
    x_recv,
    n_send,
    n_recv,
):
    hi, y, core, e = place()
    ctx = lax.axis_index("ctx")
    model = hidden.shape[1]
    sibling = (ctx_of(hi, y, 1 - core), e)
    up = (ctx_of(hi, lax.rem(y + 1, 4), core), e)
    down = (ctx_of(hi, lax.rem(y + 3, 4), core), e)

    def along(d):
        return (ctx_of(hi + d, y, core), e)

    def other(d):
        return lax.rem(e + d, 8)

    barrier = pltpu.get_barrier_semaphore()
    for device in (along(1), along(2), along(3), up, down, sibling):
        pl.semaphore_signal(barrier, inc=1, device_id=device, device_id_type=MESH)
    for d in range(1, 8):
        pl.semaphore_signal(barrier, inc=1, device_id=(ctx, other(d)), device_id_type=MESH)

    lanes = pl.ds(pl.multiple_of((e // 2) * HD, HD), HD)
    kv[0, 0:256] = old_kv[0, :, lanes]
    kv[0, 256:384] = new_kv[0, :, lanes]
    for b in range(3):
        values = new_kv[1, :, lanes] if b == 2 else old_kv[1, b * 128 : (b + 1) * 128, lanes]
        kv[0, 384 + b * 128 : 512 + b * 128] = values.astype(jnp.float32).T.astype(jnp.bfloat16)
    own_pos = new_pos[...]
    row = lax.broadcasted_iota(jnp.int32, (16, 128), 0)
    kv[0, 768:784] = (
        jnp.where(row == 0, own_pos >> 6, jnp.where(row == 1, own_pos & 63, 0))
        .astype(jnp.float32)
        .astype(jnp.bfloat16)
    )
    weight[0] = o_weight[...]

    pl.semaphore_wait(barrier, 13)

    def gather(blocks, z_send, z_recv, y_send, y_recv, c_send, c_recv):
        z_copy = [None] + [
            remote(blocks.at[0], blocks.at[d], z_send.at[d], z_recv.at[d], along(d))
            for d in range(1, 4)
        ]
        y_copy = {}
        for d in range(4):
            for dy, device in ((1, up), (3, down)):
                y_copy[dy, d] = remote(
                    blocks.at[d],
                    blocks.at[dy * 4 + d],
                    y_send.at[dy * 4 + d],
                    y_recv.at[dy * 4 + d],
                    device,
                )
            source = 4 + d if d % 2 == 0 else 12 + d
            y_copy[2, d] = remote(
                blocks.at[source],
                blocks.at[8 + d],
                y_send.at[8 + d],
                y_recv.at[8 + d],
                up if d % 2 == 0 else down,
            )
        c_copy = [
            remote(blocks.at[s], blocks.at[16 + s], c_send.at[s], c_recv.at[s], sibling)
            for s in range(16)
        ]
        return z_copy, y_copy, c_copy

    kz, ky, kc = gather(kv, kz_send, kz_recv, ky_send, ky_recv, kc_send, kc_recv)
    wz, wy, wc = gather(weight, wz_send, wz_recv, wy_send, wy_recv, wc_send, wc_recv)

    def begin_y(y_copy, c_copy, d):
        y_copy[1, d].start()
        y_copy[3, d].start()
        c_copy[d].start()

    def pass_on(y_copy, c_copy, d):
        y_copy[1, d].wait_recv()
        if d % 2 == 0:
            y_copy[2, d].start()
        c_copy[4 + d].start()
        y_copy[3, d].wait_recv()
        if d % 2 == 1:
            y_copy[2, d].start()
        c_copy[12 + d].start()

    def last(y_copy, c_copy, d):
        y_copy[2, d].wait_recv()
        c_copy[8 + d].start()

    near = (0, 1, 3, 2)
    for d in (1, 3, 2):
        kz[d].start()
    begin_y(ky, kc, 0)

    for h in range(8):
        part = query[:, h * HD : (h + 1) * HD].astype(jnp.float32).T.astype(jnp.bfloat16)
        queries[h // 2, :, (h % 2) * 128 : (h % 2 + 1) * 128] = part
    top[...] = jnp.full_like(top, -1e30)
    acc[...] = jnp.zeros_like(acc)
    factor = 1.4426950408889634 / HD**0.5

    def attend(group):
        base = group * 4
        for b in range(4):
            digits = kv[base + b, 768:784].astype(jnp.float32)
            place_of = digits[0:1] * 64.0 + digits[1:2]
            column = jnp.broadcast_to(place_of, (128, 128)).T
            seen = column <= own_pos.astype(jnp.float32)
            bias[b] = jnp.where(seen, 0.0, -1e30)

        @pl.loop(0, 4)
        def _(t):
            part = queries[t]
            pieces = []
            for b in range(4):
                scores = jnp.dot(kv[base + b, 0:384], part, preferred_element_type=jnp.float32)
                wide = jnp.concatenate([bias[b], bias[b]], 1)
                pieces += [scores[:256], scores[256:] + wide]
            old_top = top[t, 0:1]
            new_top = old_top
            for piece in pieces:
                new_top = jnp.maximum(new_top, jnp.max(piece, 0, keepdims=True))
            probs = jnp.concatenate(
                [jnp.exp2((piece - new_top) * factor).astype(jnp.bfloat16) for piece in pieces], 0
            )
            values = jnp.concatenate(
                [
                    kv[base + b, 384 + 128 * i : 512 + 128 * i]
                    for b in range(4)
                    for i in range(3)
                ],
                1,
            )
            ones = jnp.ones((16, values.shape[1]), jnp.bfloat16)
            added = jnp.dot(
                jnp.concatenate([values, ones], 0), probs, preferred_element_type=jnp.float32
            )
            acc[t] = acc[t] * jnp.exp2((old_top - new_top) * factor) + added
            top[t] = jnp.broadcast_to(new_top, (8, 256))

    for d in (1, 3, 2):
        kz[d].wait_recv()
        begin_y(ky, kc, d)
    for d in (1, 3, 2):
        wz[d].start()
    attend(0)
    for d in near:
        pass_on(ky, kc, d)
    begin_y(wy, wc, 0)
    for d in near:
        kc[d].wait_recv()
    attend(4)
    for d in (1, 3, 2):
        wz[d].wait_recv()
        begin_y(wy, wc, d)
    attend(1)
    for d in near:
        last(ky, kc, d)
    attend(3)
    for d in near:
        pass_on(wy, wc, d)
    attend(2)
    for d in near:
        kc[4 + d].wait_recv()
    attend(5)
    for d in near:
        kc[12 + d].wait_recv()
    attend(7)
    for d in near:
        last(wy, wc, d)
    for d in near:
        kc[8 + d].wait_recv()
    attend(6)

    for h in range(8):
        part = slice((h % 2) * 128, (h % 2 + 1) * 128)
        scaled = acc[h // 2, 0:128, part] / acc[h // 2, 128:129, part]
        attended[:, h * HD : (h + 1) * HD] = scaled.T.astype(jnp.bfloat16)
    for s in range(16):
        wc[s].wait_recv()

    def column_of(slot):
        k, dy, dh = slot // 16, (slot // 4) % 4, slot % 4
        owner = ctx_of(hi + 4 - dh, lax.rem(y + 4 - dy, 4), lax.rem(core + k, 2))
        return pl.ds(pl.multiple_of(owner * 128, 128), 128)

    @pl.loop(0, 16)
    def _(n):
        both = jnp.concatenate([weight[2 * n], weight[2 * n + 1]], 1)
        result = jnp.dot(attended[...], both, preferred_element_type=jnp.float32)
        result = result.astype(jnp.bfloat16)
        projected[:, column_of(2 * n)] = result[:, :128]
        projected[:, column_of(2 * n + 1)] = result[:, 128:]

    def rows_of(index):
        return pl.ds(pl.multiple_of(index * 16, 16), 16)

    x_copy = [None] + [
        remote(
            projected.at[rows_of(other(d))],
            from_exp.at[d],
            x_send.at[d],
            x_recv.at[d],
            (ctx, other(d)),
        )
        for d in range(1, 8)
    ]
    for d in range(1, 8):
        x_copy[d].start()
    residual = hidden[...].astype(jnp.float32) + projected[rows_of(e), :].astype(jnp.float32)
    for d in range(1, 8):
        x_copy[d].wait_recv()
        residual += from_exp[d].astype(jnp.float32)
    residual_ref[...] = residual
    mean = jnp.sum(residual * residual, 1, keepdims=True) * (1.0 / model)
    own = (residual * lax.rsqrt(mean + 1e-06) * norm_gain[...]).astype(jnp.bfloat16)
    own_normed[...] = own
    n_copy = [None] + [
        remote(own_normed, normed.at[rows_of(e)], n_send.at[d], n_recv.at[d], (ctx, other(d)))
        for d in range(1, 8)
    ]
    for d in range(1, 8):
        n_copy[d].start()
    normed[rows_of(e), :] = own
    for d in range(1, 8):
        n_copy[d].wait_recv()
    normed_ref[...] = normed[...]

    for d in range(1, 4):
        kz[d].wait_send()
        wz[d].wait_send()
    for d in range(4):
        for dy in range(1, 4):
            ky[dy, d].wait_send()
            wy[dy, d].wait_send()
    for s in range(16):
        kc[s].wait_send()
        wc[s].wait_send()
    for d in range(1, 8):
        x_copy[d].wait_send()
        n_copy[d].wait_send()


def attention(query, new_kv, old_kv, new_pos, o_weight, hidden, norm_gain):
    rows = query.shape[0]
    model = hidden.shape[1]
    half = jnp.bfloat16
    vmem = pl.BlockSpec(memory_space=pltpu.VMEM)
    dma = pltpu.SemaphoreType.DMA
    return pl.pallas_call(
        attention_kernel,
        out_shape=(
            jax.ShapeDtypeStruct((rows, model), half),
            jax.ShapeDtypeStruct(hidden.shape, jnp.float32),
        ),
        in_specs=[vmem] * 7,
        out_specs=(vmem, vmem),
        scratch_shapes=[
            pltpu.VMEM((32, 784, HD), half),
            pltpu.VMEM((32,) + o_weight.shape, half),
            pltpu.VMEM((4, HD, 256), half),
            pltpu.VMEM((4, 128, 128), jnp.float32),
            pltpu.VMEM((4, 8, 256), jnp.float32),
            pltpu.VMEM((4, 144, 256), jnp.float32),
            pltpu.VMEM(query.shape, half),
            pltpu.VMEM((rows, model), half),
            pltpu.VMEM((8, 16, model), half),
            pltpu.VMEM((16, model), half),
            pltpu.VMEM((rows, model), half),
            dma((4,)),
            dma((4,)),
            dma((16,)),
            dma((16,)),
            dma((16,)),
            dma((16,)),
            dma((4,)),
            dma((4,)),
            dma((16,)),
            dma((16,)),
            dma((16,)),
            dma((16,)),
            dma((8,)),
            dma((8,)),
            dma((8,)),
            dma((8,)),
        ],
        compiler_params=pltpu.CompilerParams(
            collective_id=2, has_side_effects=True, vmem_limit_bytes=56 * 2**20
        ),
        name="attention",
    )(query, new_kv, old_kv, new_pos.reshape(1, rows), o_weight, hidden, norm_gain.reshape(1, model))


def tables(ids, gates, pick, pick_rest, mix_hi, mix_lo):
    hi, y, core, e = place()
    chosen = ids[...]
    weights = gates[...]
    members, factors = [], []
    for i in range(8):
        expert = e * 8 + lax.rem(hi + i // 2, 4) * 2 + lax.rem(y // 2 + i, 2)
        hit = chosen == expert
        members.append(jnp.max(jnp.where(hit, 1.0, 0.0), 0, keepdims=True))
        factors.append(jnp.sum(jnp.where(hit, weights, 0.0), 0, keepdims=True))
    member = jnp.concatenate(members, 0)
    row = lax.broadcasted_iota(jnp.int32, (128, 128), 0)
    column = lax.broadcasted_iota(jnp.int32, (128, 128), 1)
    before = jnp.where(row < column, 1.0, 0.0).astype(jnp.bfloat16)
    rank = jnp.dot(member.astype(jnp.bfloat16), before, preferred_element_type=jnp.float32)
    slot = jnp.where(member > 0.5, rank, -1.0)
    slots = jnp.concatenate([jnp.broadcast_to(slot[i : i + 1], (16, 128)) for i in range(8)], 0)
    factor = jnp.concatenate([jnp.broadcast_to(f, (16, 128)) for f in factors], 0)
    r = row & 15
    for m in range(5):
        if m < 4:
            wanted = jnp.where(r >> 2 == m, 16 + (r & 3), -2)
        else:
            wanted = r
        found = slots == wanted.astype(jnp.float32)
        ones = jnp.where(found, 1.0, 0.0).astype(jnp.bfloat16)
        mix = jnp.where(found, factor, 0.0).T
        high = mix.astype(jnp.bfloat16)
        low = (mix - high.astype(jnp.float32)).astype(jnp.bfloat16)
        if m < 4:
            pick_rest[:, m * 128 : (m + 1) * 128] = ones
            mix_hi[m, :, 128:256] = high
            mix_lo[m, :, 128:256] = low
        else:
            pick[...] = ones
            for q in range(4):
                mix_hi[q, :, 0:128] = high
                mix_lo[q, :, 0:128] = low


def moe_kernel(
    normed,
    residual_own,
    ids,
    gates,
    w_in_hbm,
    w_out_hbm,
    out_ref,
    w_in,
    w_out,
    w_sem,
    pick,
    pick_rest,
    mix_hi,
    mix_lo,
    sent,
    got,
    both,
    rest_in,
    act,
    rest_out,
    part,
    from_core,
    to_pair,
    from_pair,
    to_home,
    home,
    mixed,
    from_exp,
    d_send,
    d_recv,
    f_send,
    f_recv,
    c_send,
    c_recv,
    rc_send,
    rc_recv,
    rf_send,
    rf_recv,
    rd_send,
    rd_recv,
    x_send,
    x_recv,
):
    hi, y, core, e = place()
    width = sent.shape[-1]
    sibling = (ctx_of(hi, y, 1 - core), e)
    pair = (ctx_of(hi, y + 1 - 2 * lax.rem(y, 2), core), e)

    def there(i):
        return (ctx_of(hi + i // 2, y if i % 2 == 0 else 3 - y, core), e)

    def back(i):
        return (ctx_of(hi + 4 - i // 2, y if i % 2 == 0 else 3 - y, core), e)

    def other(d):
        return lax.rem(e + d, 8)

    barrier = pltpu.get_barrier_semaphore()
    for i in range(1, 8):
        pl.semaphore_signal(barrier, inc=1, device_id=there(i), device_id_type=MESH)
    pl.semaphore_signal(barrier, inc=1, device_id=sibling, device_id_type=MESH)
    pl.semaphore_signal(barrier, inc=1, device_id=pair, device_id_type=MESH)
    for d in range(1, 8):
        pl.semaphore_signal(
            barrier, inc=1, device_id=(lax.axis_index("ctx"), other(d)), device_id_type=MESH
        )

    loads = [
        pltpu.make_async_copy(w_in_hbm, w_in, w_sem.at[0]),
        pltpu.make_async_copy(w_out_hbm, w_out, w_sem.at[1]),
    ]
    for load in loads:
        load.start()
    tables(ids, gates, pick, pick_rest, mix_hi, mix_lo)

    for m in range(4):
        rows = jnp.dot(
            pick[...], normed[:, m * width : (m + 1) * width], preferred_element_type=jnp.float32
        )
        sent[:, m] = rows.astype(jnp.bfloat16).reshape(8, 16, width)
    rest = jnp.zeros((128, width), jnp.float32)
    for m in range(4):
        rest += jnp.dot(
            pick_rest[:, m * 128 : (m + 1) * 128],
            normed[:, m * width : (m + 1) * width],
            preferred_element_type=jnp.float32,
        )
    sent[:, 4] = rest.astype(jnp.bfloat16).reshape(8, 16, width)
    got[0] = sent[0]

    pl.semaphore_wait(barrier, 16)

    d_copy = [
        None if i == 0 else remote(sent.at[i], got.at[i], d_send.at[i], d_recv.at[i], there(i))
        for i in range(8)
    ]
    for i in (2, 6, 1):
        d_copy[i].start()
    f_copy = [
        remote(got.at[i], got.at[16 + i], f_send.at[i], f_recv.at[i], pair) for i in range(8)
    ]
    c_copy = [
        remote(got.at[i], got.at[8 + i], c_send.at[i], c_recv.at[i], sibling) for i in range(8)
    ] + [
        remote(got.at[16 + i], got.at[24 + i], c_send.at[8 + i], c_recv.at[8 + i], sibling)
        for i in range(8)
    ]
    order = (0,) + ARRIVE
    for n in range(8):
        i = order[n]
        if i == 2:
            for sent_now, begun in ((2, 3), (6, 7)):
                d_copy[sent_now].wait_send()
                d_copy[begun].start()
        if i == 3:
            for sent_now, begun in ((3, 4), (7, 5)):
                d_copy[sent_now].wait_send()
                d_copy[begun].start()
        if i > 0:
            d_copy[i].wait_recv()
        f_copy[i].start()
        c_copy[i].start()
        if n >= 2:
            f_copy[order[n - 2]].wait_recv()
            c_copy[8 + order[n - 2]].start()

    def regroup(m, rows, columns):
        row = lax.broadcasted_iota(jnp.int32, (rows, columns), 0)
        column = lax.broadcasted_iota(jnp.int32, (rows, columns), 1)
        small, large = (row, column) if rows < columns else (column, row)
        return (large == (small // 4) * 16 + m * 4 + small % 4).astype(jnp.bfloat16)

    def experts(base):
        rest_rows = got[base : base + 16, 4].reshape(256, width)
        for m in range(4):
            rest_in[:, m * width : (m + 1) * width] = jnp.dot(
                regroup(m, 64, 256), rest_rows, preferred_element_type=jnp.float32
            ).astype(jnp.bfloat16)

        @pl.loop(0, 3)
        def _(n):
            columns = pl.ds(pl.multiple_of(n * 256, 256), 256)
            total = jnp.zeros((320, 256), jnp.float32)
            for m in range(4):
                rows = jnp.concatenate(
                    [
                        got[base : base + 16, m].reshape(256, width),
                        rest_in[:, m * width : (m + 1) * width],
                    ],
                    0,
                )
                total += jnp.dot(
                    rows,
                    w_in[m * width : (m + 1) * width, columns],
                    preferred_element_type=jnp.float32,
                )
            both[:, columns] = total

        gate = both[:, :FFQ]
        act[...] = (gate / (1.0 + jnp.exp(-gate)) * both[:, FFQ:]).astype(jnp.bfloat16)
        steps = width // 256

        @pl.loop(0, 4 * steps)
        def _(n):
            columns = pl.ds(pl.multiple_of(n * 256, 256), 256)
            inner = pl.ds(pl.multiple_of((n % steps) * 256, 256), 256)
            result = jnp.dot(
                act[...], w_out[:, columns], preferred_element_type=jnp.float32
            ).astype(jnp.bfloat16)
            part[base : base + 16, n // steps, :, inner] = result[:256].reshape(16, 16, 256)
            rest_out[:, columns] = result[256:]

        rest_part = jnp.zeros((256, width), jnp.float32)
        for m in range(4):
            rest_part += jnp.dot(
                regroup(m, 256, 64),
                rest_out[:, m * width : (m + 1) * width],
                preferred_element_type=jnp.float32,
            )
        part[base : base + 16, 4] = rest_part.astype(jnp.bfloat16).reshape(16, 16, width)

    for i in order:
        c_copy[i].wait_recv()
    for load in loads:
        load.wait()
    experts(0)
    rc_copy = [
        remote(part.at[8 + i], from_core.at[i], rc_send.at[i], rc_recv.at[i], sibling)
        for i in range(8)
    ] + [
        remote(part.at[24 + i], from_core.at[8 + i], rc_send.at[8 + i], rc_recv.at[8 + i], sibling)
        for i in range(8)
    ]
    for i in order:
        rc_copy[i].start()
    for n in (6, 7):
        f_copy[order[n]].wait_recv()
        c_copy[8 + order[n]].start()
    for i in order:
        c_copy[8 + i].wait_recv()
    experts(16)
    for i in order:
        rc_copy[8 + i].start()

    rf_copy = [
        remote(to_pair.at[i], from_pair.at[i], rf_send.at[i], rf_recv.at[i], pair)
        for i in range(8)
    ]
    rd_copy = [
        None if i == 0 else remote(to_home.at[i], home.at[i], rd_send.at[i], rd_recv.at[i], back(i))
        for i in range(8)
    ]
    final = (4, 5, 2, 6, 3, 7, 1, 0)
    for n in range(10):
        if n < 8:
            i = final[n]
            rc_copy[8 + i].wait_recv()
            to_pair[i] = (
                part[16 + i].astype(jnp.float32) + from_core[8 + i].astype(jnp.float32)
            ).astype(jnp.bfloat16)
            if n >= 2:
                rf_copy[final[n - 2]].wait_send()
            rf_copy[i].start()
        if n >= 2:
            i = final[n - 2]
            rc_copy[i].wait_recv()
            rf_copy[i].wait_recv()
            total = (
                part[i].astype(jnp.float32)
                + from_core[i].astype(jnp.float32)
                + from_pair[i].astype(jnp.float32)
            ).astype(jnp.bfloat16)
            if i == 0:
                home[0] = total
            else:
                to_home[i] = total
                rd_copy[i].start()
    for i in ARRIVE:
        rd_copy[i].wait_recv()

    for m in range(4):
        rows = jnp.concatenate(
            [home[:, m].reshape(128, width), home[:, 4].reshape(128, width)], 0
        )
        mixed[:, m * width : (m + 1) * width] = (
            jnp.dot(mix_hi[m], rows, preferred_element_type=jnp.float32)
            + jnp.dot(mix_lo[m], rows, preferred_element_type=jnp.float32)
        ).astype(jnp.bfloat16)

    x_copy = [None]
    for d in range(1, 8):
        own = pl.ds(pl.multiple_of(other(d) * 16, 16), 16)
        x_copy.append(
            remote(
                mixed.at[own],
                from_exp.at[d],
                x_send.at[d],
                x_recv.at[d],
                (lax.axis_index("ctx"), other(d)),
            )
        )
        x_copy[d].start()
    total = (
        residual_own[...] + mixed[pl.ds(pl.multiple_of(e * 16, 16), 16), :].astype(jnp.float32)
    )
    for d in range(1, 8):
        x_copy[d].wait_recv()
        total += from_exp[d].astype(jnp.float32)
    out_ref[...] = total.astype(jnp.bfloat16)

    for i in (1, 4, 5):
        d_copy[i].wait_send()
    for i in (1, 0):
        rf_copy[i].wait_send()
    for i in range(8):
        if i > 0:
            rd_copy[i].wait_send()
            x_copy[i].wait_send()
        f_copy[i].wait_send()
    for i in range(16):
        c_copy[i].wait_send()
        rc_copy[i].wait_send()


def moe(normed, residual_own, expert_ids, gate_weights, w_in, w_out):
    model = normed.shape[1]
    width = model // 4
    block = (5, 16, width)
    half = jnp.bfloat16
    vmem = pl.BlockSpec(memory_space=pltpu.VMEM)
    dma = pltpu.SemaphoreType.DMA
    return pl.pallas_call(
        moe_kernel,
        out_shape=jax.ShapeDtypeStruct(residual_own.shape, half),
        in_specs=[vmem] * 4 + [pl.BlockSpec(memory_space=pl.ANY)] * 2,
        out_specs=vmem,
        scratch_shapes=[
            pltpu.VMEM(w_in.shape, half),
            pltpu.VMEM(w_out.shape, half),
            dma((2,)),
            pltpu.VMEM((128, 128), half),
            pltpu.VMEM((128, 512), half),
            pltpu.VMEM((4, 128, 256), half),
            pltpu.VMEM((4, 128, 256), half),
            pltpu.VMEM((8,) + block, half),
            pltpu.VMEM((32,) + block, half),
            pltpu.VMEM((320, 2 * FFQ), jnp.float32),
            pltpu.VMEM((64, model), half),
            pltpu.VMEM((320, FFQ), half),
            pltpu.VMEM((64, model), half),
            pltpu.VMEM((32,) + block, half),
            pltpu.VMEM((16,) + block, half),
            pltpu.VMEM((8,) + block, half),
            pltpu.VMEM((8,) + block, half),
            pltpu.VMEM((8,) + block, half),
            pltpu.VMEM((8,) + block, half),
            pltpu.VMEM((128, model), half),
            pltpu.VMEM((8, 16, model), half),
            dma((8,)),
            dma((8,)),
            dma((8,)),
            dma((8,)),
            dma((16,)),
            dma((16,)),
            dma((16,)),
            dma((16,)),
            dma((8,)),
            dma((8,)),
            dma((8,)),
            dma((8,)),
            dma((8,)),
            dma((8,)),
        ],
        compiler_params=pltpu.CompilerParams(
            collective_id=1, has_side_effects=True, vmem_limit_bytes=56 * 2**20
        ),
        name="moe",
    )(normed, residual_own, expert_ids.T, gate_weights.T, w_in, w_out)


def per_device(
    query,
    new_kv,
    old_kv,
    new_pos,
    o_weight,
    hidden,
    norm_gain,
    expert_ids,
    gate_weights,
    w_in,
    w_out,
):
    normed, residual_own = attention(
        query, new_kv, old_kv, new_pos, o_weight, hidden, norm_gain
    )
    return moe(
        normed, residual_own, expert_ids, gate_weights, w_in[0, 0], w_out[0, 0]
    )


def solution(mesh):
    return jax.shard_map(
        per_device,
        mesh=mesh,
        in_specs=(
            P("ctx", "exp"),
            P(None, "ctx", None),
            P(None, "ctx", None),
            P("ctx"),
            P("exp", "ctx"),
            P(("ctx", "exp"), None),
            P(),
            P("ctx", None),
            P("ctx", None),
            P("ctx", "exp", None, None),
            P("ctx", "exp", None, None),
        ),
        out_specs=P(("ctx", "exp"), None),
        check_vma=False,
    )
```

```python
import jax
import jax.numpy as jnp
from jax import lax
from jax.experimental import pallas as pl
from jax.experimental.pallas import tpu as pltpu
from jax.sharding import PartitionSpec as P

HD = 128
FFQ = 384
MESH = pl.DeviceIdType.MESH
ARRIVE = (1, 2, 6, 3, 7, 4, 5)
ORDER = (0, 4, 1, 3, 5, 7, 2, 6)


CHUNKS = ((2, 6, 3, 7), (0, 1, 4, 5))
SCHEDULE = (
    ("send", 2, 6, 1),
    ("pass", 0, 1),
    ("sent", 2),
    ("send", 3),
    ("sent", 6),
    ("send", 7),
    ("pass", 2, 6),
    ("core", 0, 1),
    ("sent", 3),
    ("send", 4),
    ("sent", 7),
    ("send", 5),
    ("pass", 3, 7),
    ("core", 2, 6, 3, 7),
    ("work", 0),
    ("pass", 4, 5),
    ("back", 2, 6),
    ("core", 4, 5),
    ("home", 2),
    ("back", 3, 7),
    ("home", 6),
    ("work", 1),
    ("home", 3, 7),
    ("back", 4, 5, 1, 0),
    ("home", 4, 5, 1, 0),
)


def place():
    ctx = lax.axis_index("ctx")
    return ctx // 8, (ctx // 2) % 4, ctx % 2, lax.axis_index("exp")


def ctx_of(hi, y, core):
    return lax.rem(hi, 4) * 8 + y * 2 + core


def remote(src, dst, send, recv, device):
    return pltpu.make_async_remote_copy(
        src_ref=src, dst_ref=dst, send_sem=send, recv_sem=recv, device_id=device, device_id_type=MESH
    )


def attention_kernel(
    query,
    new_kv,
    old_kv,
    new_pos,
    o_weight,
    hidden,
    norm_gain,
    normed_ref,
    residual_ref,
    kv,
    weight,
    queries,
    bias,
    top,
    acc,
    attended,
    projected,
    from_exp,
    summed,
    pieces,
    gathered,
    own_normed,
    normed,
    kz_send,
    kz_recv,
    ky_send,
    ky_recv,
    kc_send,
    kc_recv,
    wz_send,
    wz_recv,
    ay_send,
    ay_recv,
    ac_send,
    ac_recv,
    x_send,
    x_recv,
    p_send,
    p_recv,
    n_send,
    n_recv,
):
    hi, y, core, e = place()
    ctx = lax.axis_index("ctx")
    model = hidden.shape[1]
    sibling = (ctx_of(hi, y, 1 - core), e)
    up = (ctx_of(hi, lax.rem(y + 1, 4), core), e)
    down = (ctx_of(hi, lax.rem(y + 3, 4), core), e)

    def along(d):
        return (ctx_of(hi + d, y, core), e)

    low = lax.rem(e, 2)
    outer = (ctx_of(hi + 3 + 2 * low, y, core), e + 1 - 2 * low)
    inner = (ctx, e + 1 - 2 * low)

    def behind(s):
        return (ctx_of(hi, lax.rem(y + 4 - s % 4, 4), core if s < 4 else 1 - core), e)

    def other(d):
        return lax.rem(e + d, 8)

    barrier = pltpu.get_barrier_semaphore()
    for d in range(1, 4):
        pl.semaphore_signal(barrier, inc=1, device_id=along(d), device_id_type=MESH)
    pl.semaphore_signal(barrier, inc=1, device_id=outer, device_id_type=MESH)
    for s in range(1, 8):
        pl.semaphore_signal(barrier, inc=1, device_id=behind(s), device_id_type=MESH)
    for d in range(1, 8):
        pl.semaphore_signal(barrier, inc=1, device_id=(ctx, other(d)), device_id_type=MESH)

    lanes = pl.ds(pl.multiple_of((e // 2) * HD, HD), HD)
    kv[0, 0:256] = old_kv[0, :, lanes]
    kv[0, 256:384] = new_kv[0, :, lanes]
    for b in range(3):
        values = new_kv[1, :, lanes] if b == 2 else old_kv[1, b * 128 : (b + 1) * 128, lanes]
        kv[0, 384 + b * 128 : 512 + b * 128] = values.astype(jnp.float32).T.astype(jnp.bfloat16)
    own_pos = new_pos[...]
    row = lax.broadcasted_iota(jnp.int32, (16, 128), 0)
    kv[0, 768:784] = (
        jnp.where(row == 0, own_pos >> 6, jnp.where(row == 1, own_pos & 63, 0))
        .astype(jnp.float32)
        .astype(jnp.bfloat16)
    )
    weight[0] = o_weight[...]

    pl.semaphore_wait(barrier, 18)

    kz = [None] + [
        remote(kv.at[d * 8 - 8], kv.at[d * 8], kz_send.at[d], kz_recv.at[d], device)
        for d, device in ((1, outer), (2, inner), (3, outer))
    ]
    wz = [None] + [
        remote(weight.at[0], weight.at[d], wz_send.at[d], wz_recv.at[d], along(d))
        for d in range(1, 4)
    ]
    ky = {}
    for d in range(4):
        for dy, device in ((1, up), (3, down)):
            ky[dy, d] = remote(
                kv.at[d * 8],
                kv.at[d * 8 + dy],
                ky_send.at[d * 4 + dy],
                ky_recv.at[d * 4 + dy],
                device,
            )
        ky[2, d] = remote(
            kv.at[d * 8 + (1 if d % 2 == 0 else 3)],
            kv.at[d * 8 + 2],
            ky_send.at[d * 4 + 2],
            ky_recv.at[d * 4 + 2],
            up if d % 2 == 0 else down,
        )
    kc = {
        (dy, d): remote(
            kv.at[d * 8 + dy],
            kv.at[d * 8 + 4 + dy],
            kc_send.at[d * 4 + dy],
            kc_recv.at[d * 4 + dy],
            sibling,
        )
        for d in range(4)
        for dy in range(4)
    }

    def begin_y(d):
        ky[1, d].start()
        ky[3, d].start()
        kc[0, d].start()

    def pass_on(d):
        ky[1, d].wait_recv()
        if d % 2 == 0:
            ky[2, d].start()
        kc[1, d].start()
        ky[3, d].wait_recv()
        if d % 2 == 1:
            ky[2, d].start()
        kc[3, d].start()

    def last(d):
        ky[2, d].wait_recv()
        kc[2, d].start()

    kz[1].start()
    begin_y(0)

    for h in range(8):
        part = query[:, h * HD : (h + 1) * HD].astype(jnp.float32).T.astype(jnp.bfloat16)
        queries[h // 2, :, (h % 2) * 128 : (h % 2 + 1) * 128] = part
    top[...] = jnp.full_like(top, -1e30)
    acc[...] = jnp.zeros_like(acc)
    factor = 1.4426950408889634 / HD**0.5

    def attend(blocks):
        for b in range(4):
            digits = kv[blocks[b], 768:784].astype(jnp.float32)
            place_of = digits[0:1] * 64.0 + digits[1:2]
            column = jnp.broadcast_to(place_of, (128, 128)).T
            seen = column <= own_pos.astype(jnp.float32)
            bias[b] = jnp.where(seen, 0.0, -1e30)

        @pl.loop(0, 4, unroll=4)
        def _(t):
            part = queries[t]
            pieces = []
            for b in range(4):
                scores = jnp.dot(kv[blocks[b], 0:384], part, preferred_element_type=jnp.float32)
                wide = jnp.concatenate([bias[b], bias[b]], 1)
                pieces += [scores[:256], scores[256:] + wide]
            old_top = top[t, 0:1]
            new_top = old_top
            for piece in pieces:
                new_top = jnp.maximum(new_top, jnp.max(piece, 0, keepdims=True))
            probs = jnp.concatenate(
                [jnp.exp2((piece - new_top) * factor).astype(jnp.bfloat16) for piece in pieces], 0
            )
            values = jnp.concatenate(
                [
                    kv[blocks[b], 384 + 128 * i : 512 + 128 * i]
                    for b in range(4)
                    for i in range(3)
                ],
                1,
            )
            ones = jnp.ones((16, values.shape[1]), jnp.bfloat16)
            added = jnp.dot(
                jnp.concatenate([values, ones], 0), probs, preferred_element_type=jnp.float32
            )
            acc[t] = acc[t] * jnp.exp2((old_top - new_top) * factor) + added
            top[t] = jnp.broadcast_to(new_top, (8, 256))

    def attend_near(d):
        kc[0, d].wait_recv()
        attend([d * 8 + b for b in (0, 4, 1, 3)])

    def attend_far(d):
        for dy in (1, 3, 2):
            kc[dy, d].wait_recv()
        attend([d * 8 + b for b in (5, 7, 2, 6)])

    kz[1].wait_recv()
    kz[2].start()
    begin_y(1)
    pass_on(0)
    attend_near(0)
    kz[2].wait_recv()
    kz[3].start()
    begin_y(2)
    for d in (1, 3):
        wz[d].start()
    last(0)
    pass_on(1)
    attend_far(0)
    attend_near(1)
    kz[3].wait_recv()
    begin_y(3)
    wz[2].start()
    last(1)
    pass_on(2)
    attend_far(1)
    attend_near(2)
    last(2)
    pass_on(3)
    attend_far(2)
    attend_near(3)
    last(3)
    attend_far(3)

    for h in range(8):
        part = slice((h % 2) * 128, (h % 2 + 1) * 128)
        scaled = acc[h // 2, 0:128, part] / acc[h // 2, 128:129, part]
        attended[0, :, h * HD : (h + 1) * HD] = scaled.T.astype(jnp.bfloat16)

    def half_of(slot, k):
        return attended.at[slot, pl.ds(k * 64, 64)]

    ay = {
        1: remote(attended.at[0], attended.at[1], ay_send.at[0], ay_recv.at[0], up),
        3: remote(attended.at[0], attended.at[3], ay_send.at[1], ay_recv.at[1], down),
        "up": remote(half_of(1, 0), half_of(2, 0), ay_send.at[2], ay_recv.at[2], up),
        "down": remote(half_of(3, 1), half_of(2, 1), ay_send.at[3], ay_recv.at[3], down),
    }
    ac = [
        remote(attended.at[s], attended.at[4 + s], ac_send.at[s], ac_recv.at[s], sibling)
        for s in range(4)
    ]
    ay[1].start()
    ay[3].start()
    ac[0].start()
    for d in range(1, 4):
        wz[d].wait_recv()

    def project(s):
        for pair in range(2):
            both = jnp.concatenate([weight[2 * pair], weight[2 * pair + 1]], 1)
            result = jnp.dot(attended[s], both, preferred_element_type=jnp.float32)
            projected[:, ORDER.index(s), :, pair * 256 : (pair + 1) * 256] = result.astype(
                jnp.bfloat16
            ).reshape(8, 16, 256)

    x_copy = [
        None
        if d == 0
        else remote(
            projected.at[other(d), pl.ds(half * 4, 4)],
            from_exp.at[d, pl.ds(half * 4, 4)],
            x_send.at[half * 8 + d],
            x_recv.at[half * 8 + d],
            (ctx, other(d)),
        )
        for half in range(2)
        for d in range(8)
    ]
    p_copy = [None] + [
        remote(summed.at[s], pieces.at[s], p_send.at[s], p_recv.at[s], behind(s))
        for s in range(1, 8)
    ]

    project(0)
    ac[0].wait_recv()
    project(4)
    ay[1].wait_recv()
    ay["up"].start()
    ac[1].start()
    ay[3].wait_recv()
    ay["down"].start()
    ac[3].start()
    project(1)
    project(3)
    for d in range(1, 8):
        x_copy[d].start()
    ac[1].wait_recv()
    project(5)
    ac[3].wait_recv()
    project(7)
    ay["up"].wait_recv()
    ay["down"].wait_recv()
    ac[2].start()
    project(2)
    ac[2].wait_recv()
    project(6)
    for d in range(1, 8):
        x_copy[8 + d].start()

    for half in range(2):
        for d in range(1, 8):
            x_copy[half * 8 + d].wait_recv()
        for k in range(half * 4, half * 4 + 4):
            s = ORDER[k]
            total = projected[e, k].astype(jnp.float32)
            for d in range(1, 8):
                total += from_exp[d, k].astype(jnp.float32)
            if s == 0:
                pieces[0] = total
            else:
                summed[s] = total
                p_copy[s].start()
    for s in ORDER:
        if s > 0:
            p_copy[s].wait_recv()
        sender = lax.rem(y + s % 4, 4) * 2 + (core if s < 4 else 1 - core)
        for d in range(4):
            owner = lax.rem(hi + 4 - d, 4) * 8 + sender
            gathered[:, pl.ds(pl.multiple_of(owner * 128, 128), 128)] = pieces[
                s, :, d * 128 : (d + 1) * 128
            ]

    def rows_of(index):
        return pl.ds(pl.multiple_of(index * 16, 16), 16)

    residual = hidden[...].astype(jnp.float32) + gathered[...]
    residual_ref[...] = residual
    mean = jnp.sum(residual * residual, 1, keepdims=True) * (1.0 / model)
    own = (residual * lax.rsqrt(mean + 1e-06) * norm_gain[...]).astype(jnp.bfloat16)
    own_normed[...] = own
    n_copy = [None] + [
        remote(own_normed, normed.at[rows_of(e)], n_send.at[d], n_recv.at[d], (ctx, other(d)))
        for d in range(1, 8)
    ]
    for d in range(1, 8):
        n_copy[d].start()
    normed[rows_of(e), :] = own
    for d in range(1, 8):
        n_copy[d].wait_recv()
    normed_ref[...] = normed[...]

    for d in range(1, 4):
        kz[d].wait_send()
        wz[d].wait_send()
    for d in range(4):
        for dy in range(4):
            if dy > 0:
                ky[dy, d].wait_send()
            kc[dy, d].wait_send()
        ac[d].wait_send()
    for copy in ay.values():
        copy.wait_send()
    for d in range(1, 8):
        x_copy[d].wait_send()
        x_copy[8 + d].wait_send()
        p_copy[d].wait_send()
        n_copy[d].wait_send()


def attention(query, new_kv, old_kv, new_pos, o_weight, hidden, norm_gain):
    rows = query.shape[0]
    model = hidden.shape[1]
    half = jnp.bfloat16
    vmem = pl.BlockSpec(memory_space=pltpu.VMEM)
    dma = pltpu.SemaphoreType.DMA
    return pl.pallas_call(
        attention_kernel,
        out_shape=(
            jax.ShapeDtypeStruct((rows, model), half),
            jax.ShapeDtypeStruct(hidden.shape, jnp.float32),
        ),
        in_specs=[vmem] * 7,
        out_specs=(vmem, vmem),
        scratch_shapes=[
            pltpu.VMEM((32, 784, HD), half),
            pltpu.VMEM((4,) + o_weight.shape, half),
            pltpu.VMEM((4, HD, 256), half),
            pltpu.VMEM((4, 128, 128), jnp.float32),
            pltpu.VMEM((4, 8, 256), jnp.float32),
            pltpu.VMEM((4, 144, 256), jnp.float32),
            pltpu.VMEM((8,) + query.shape, half),
            pltpu.VMEM((8, 8, 16, 512), half),
            pltpu.VMEM((8, 8, 16, 512), half),
            pltpu.VMEM((8, 16, 512), jnp.float32),
            pltpu.VMEM((8, 16, 512), jnp.float32),
            pltpu.VMEM(hidden.shape, jnp.float32),
            pltpu.VMEM(hidden.shape, half),
            pltpu.VMEM((rows, model), half),
            dma((4,)),
            dma((4,)),
            dma((16,)),
            dma((16,)),
            dma((16,)),
            dma((16,)),
            dma((4,)),
            dma((4,)),
            dma((4,)),
            dma((4,)),
            dma((4,)),
            dma((4,)),
            dma((16,)),
            dma((16,)),
            dma((8,)),
            dma((8,)),
            dma((8,)),
            dma((8,)),
        ],
        compiler_params=pltpu.CompilerParams(
            collective_id=2, has_side_effects=True, vmem_limit_bytes=56 * 2**20
        ),
        name="attention",
    )(query, new_kv, old_kv, new_pos.reshape(1, rows), o_weight, hidden, norm_gain.reshape(1, model))


def tables(ids, gates, pick, pick_rest, mix_hi, mix_lo):
    hi, y, core, e = place()
    chosen = ids[...]
    weights = gates[...]
    members, factors = [], []
    for i in range(8):
        expert = e * 8 + lax.rem(hi + i // 2, 4) * 2 + lax.rem(y // 2 + i, 2)
        hit = chosen == expert
        members.append(jnp.max(jnp.where(hit, 1.0, 0.0), 0, keepdims=True))
        factors.append(jnp.sum(jnp.where(hit, weights, 0.0), 0, keepdims=True))
    member = jnp.concatenate(members, 0)
    row = lax.broadcasted_iota(jnp.int32, (128, 128), 0)
    column = lax.broadcasted_iota(jnp.int32, (128, 128), 1)
    before = jnp.where(row < column, 1.0, 0.0).astype(jnp.bfloat16)
    rank = jnp.dot(member.astype(jnp.bfloat16), before, preferred_element_type=jnp.float32)
    slot = jnp.where(member > 0.5, rank, -1.0)
    slots = jnp.concatenate([jnp.broadcast_to(slot[i : i + 1], (16, 128)) for i in range(8)], 0)
    factor = jnp.concatenate([jnp.broadcast_to(f, (16, 128)) for f in factors], 0)
    r = row & 15
    for m in range(5):
        if m < 4:
            wanted = jnp.where(r >> 2 == m, 16 + (r & 3), -2)
        else:
            wanted = r
        found = slots == wanted.astype(jnp.float32)
        ones = jnp.where(found, 1.0, 0.0).astype(jnp.bfloat16)
        mix = jnp.where(found, factor, 0.0).T
        high = mix.astype(jnp.bfloat16)
        low = (mix - high.astype(jnp.float32)).astype(jnp.bfloat16)
        if m < 4:
            pick_rest[:, m * 128 : (m + 1) * 128] = ones
            mix_hi[m, :, 128:256] = high
            mix_lo[m, :, 128:256] = low
        else:
            pick[...] = ones
            for q in range(4):
                mix_hi[q, :, 0:128] = high
                mix_lo[q, :, 0:128] = low


def moe_kernel(
    normed,
    residual_own,
    ids,
    gates,
    w_in_hbm,
    w_out_hbm,
    out_ref,
    w_in,
    w_out,
    w_sem,
    pick,
    pick_rest,
    mix_hi,
    mix_lo,
    sent,
    got,
    both,
    rest_in,
    act,
    rest_out,
    part,
    from_core,
    to_pair,
    from_pair,
    to_home,
    home,
    mixed,
    from_exp,
    d_send,
    d_recv,
    f_send,
    f_recv,
    c_send,
    c_recv,
    rc_send,
    rc_recv,
    rf_send,
    rf_recv,
    rd_send,
    rd_recv,
    x_send,
    x_recv,
):
    hi, y, core, e = place()
    width = sent.shape[-1]
    sibling = (ctx_of(hi, y, 1 - core), e)
    pair = (ctx_of(hi, y + 1 - 2 * lax.rem(y, 2), core), e)

    def slot(i, group):
        chunk = int(i in CHUNKS[1])
        return chunk * 16 + group * 4 + CHUNKS[chunk].index(i)

    def there(i):
        return (ctx_of(hi + i // 2, y if i % 2 == 0 else 3 - y, core), e)

    def back(i):
        return (ctx_of(hi + 4 - i // 2, y if i % 2 == 0 else 3 - y, core), e)

    def other(d):
        return lax.rem(e + d, 8)

    barrier = pltpu.get_barrier_semaphore()
    for i in range(1, 8):
        pl.semaphore_signal(barrier, inc=1, device_id=there(i), device_id_type=MESH)
    pl.semaphore_signal(barrier, inc=1, device_id=sibling, device_id_type=MESH)
    pl.semaphore_signal(barrier, inc=1, device_id=pair, device_id_type=MESH)
    for d in range(1, 8):
        pl.semaphore_signal(
            barrier, inc=1, device_id=(lax.axis_index("ctx"), other(d)), device_id_type=MESH
        )

    loads = [
        pltpu.make_async_copy(w_in_hbm, w_in, w_sem.at[0]),
        pltpu.make_async_copy(w_out_hbm, w_out, w_sem.at[1]),
    ]
    for load in loads:
        load.start()
    tables(ids, gates, pick, pick_rest, mix_hi, mix_lo)

    for m in range(4):
        rows = jnp.dot(
            pick[...], normed[:, m * width : (m + 1) * width], preferred_element_type=jnp.float32
        )
        sent[:, m] = rows.astype(jnp.bfloat16).reshape(8, 16, width)
    rest = jnp.zeros((128, width), jnp.float32)
    for m in range(4):
        rest += jnp.dot(
            pick_rest[:, m * 128 : (m + 1) * 128],
            normed[:, m * width : (m + 1) * width],
            preferred_element_type=jnp.float32,
        )
    sent[:, 4] = rest.astype(jnp.bfloat16).reshape(8, 16, width)
    got[slot(0, 0)] = sent[0]

    pl.semaphore_wait(barrier, 16)

    d_copy = [
        None if i == 0 else remote(
            sent.at[i], got.at[slot(i, 0)], d_send.at[i], d_recv.at[i], there(i)
        )
        for i in range(8)
    ]
    f_copy = [
        remote(got.at[slot(i, 0)], got.at[slot(i, 2)], f_send.at[i], f_recv.at[i], pair)
        for i in range(8)
    ]
    c_copy = [
        remote(got.at[slot(i, g)], got.at[slot(i, g + 1)], c_send.at[k], c_recv.at[k], sibling)
        for k, (g, i) in enumerate((g, i) for g in (0, 2) for i in range(8))
    ]
    rc_copy = [
        remote(part.at[slot(i, g)], from_core.at[k], rc_send.at[k], rc_recv.at[k], sibling)
        for k, (g, i) in enumerate((g, i) for g in (1, 3) for i in range(8))
    ]
    rf_copy = [
        remote(to_pair.at[i], from_pair.at[i], rf_send.at[i], rf_recv.at[i], pair)
        for i in range(8)
    ]
    rd_copy = [
        None if i == 0 else remote(to_home.at[i], home.at[i], rd_send.at[i], rd_recv.at[i], back(i))
        for i in range(8)
    ]
    def regroup(m, rows, columns):
        row = lax.broadcasted_iota(jnp.int32, (rows, columns), 0)
        column = lax.broadcasted_iota(jnp.int32, (rows, columns), 1)
        small, large = (row, column) if rows < columns else (column, row)
        return (large == (small // 4) * 16 + m * 4 + small % 4).astype(jnp.bfloat16)

    def experts(base):
        rest_rows = got[base : base + 16, 4].reshape(256, width)
        for m in range(4):
            rest_in[:, m * width : (m + 1) * width] = jnp.dot(
                regroup(m, 64, 256), rest_rows, preferred_element_type=jnp.float32
            ).astype(jnp.bfloat16)

        @pl.loop(0, 3)
        def _(n):
            columns = pl.ds(pl.multiple_of(n * 256, 256), 256)
            total = jnp.zeros((320, 256), jnp.float32)
            for m in range(4):
                rows = jnp.concatenate(
                    [
                        got[base : base + 16, m].reshape(256, width),
                        rest_in[:, m * width : (m + 1) * width],
                    ],
                    0,
                )
                total += jnp.dot(
                    rows,
                    w_in[m * width : (m + 1) * width, columns],
                    preferred_element_type=jnp.float32,
                )
            both[:, columns] = total

        gate = both[:, :FFQ]
        act[...] = (gate / (1.0 + jnp.exp(-gate)) * both[:, FFQ:]).astype(jnp.bfloat16)
        steps = width // 256

        @pl.loop(0, 4 * steps)
        def _(n):
            columns = pl.ds(pl.multiple_of(n * 256, 256), 256)
            inner = pl.ds(pl.multiple_of((n % steps) * 256, 256), 256)
            result = jnp.dot(
                act[...], w_out[:, columns], preferred_element_type=jnp.float32
            ).astype(jnp.bfloat16)
            part[base : base + 16, n // steps, :, inner] = result[:256].reshape(16, 16, 256)
            rest_out[:, columns] = result[256:]

        rest_part = jnp.zeros((256, width), jnp.float32)
        for m in range(4):
            rest_part += jnp.dot(
                regroup(m, 256, 64),
                rest_out[:, m * width : (m + 1) * width],
                preferred_element_type=jnp.float32,
            )
        part[base : base + 16, 4] = rest_part.astype(jnp.bfloat16).reshape(16, 16, width)

    for step, i in ((step, i) for step, *blocks in SCHEDULE for i in blocks):
        if step == "send":
            d_copy[i].start()
        elif step == "sent":
            d_copy[i].wait_send()
        elif step == "pass":
            if i > 0:
                d_copy[i].wait_recv()
            f_copy[i].start()
            c_copy[i].start()
        elif step == "core":
            f_copy[i].wait_recv()
            c_copy[8 + i].start()
        elif step == "work":
            if i == 0:
                for load in loads:
                    load.wait()
            for block in CHUNKS[i]:
                c_copy[block].wait_recv()
                c_copy[8 + block].wait_recv()
            experts(i * 16)
            for block in CHUNKS[i]:
                rc_copy[8 + block].start()
            for block in CHUNKS[i]:
                rc_copy[block].start()
        elif step == "back":
            rc_copy[8 + i].wait_recv()
            to_pair[i] = (
                part[slot(i, 2)].astype(jnp.float32) + from_core[8 + i].astype(jnp.float32)
            ).astype(jnp.bfloat16)
            rf_copy[i].start()
        elif step == "home":
            rc_copy[i].wait_recv()
            rf_copy[i].wait_recv()
            total = (
                part[slot(i, 0)].astype(jnp.float32)
                + from_core[i].astype(jnp.float32)
                + from_pair[i].astype(jnp.float32)
            ).astype(jnp.bfloat16)
            if i == 0:
                home[0] = total
            else:
                to_home[i] = total
                rd_copy[i].start()
    for i in ARRIVE:
        rd_copy[i].wait_recv()

    for m in range(4):
        rows = jnp.concatenate(
            [home[:, m].reshape(128, width), home[:, 4].reshape(128, width)], 0
        )
        mixed[:, m * width : (m + 1) * width] = (
            jnp.dot(mix_hi[m], rows, preferred_element_type=jnp.float32)
            + jnp.dot(mix_lo[m], rows, preferred_element_type=jnp.float32)
        ).astype(jnp.bfloat16)

    x_copy = [None]
    for d in range(1, 8):
        own = pl.ds(pl.multiple_of(other(d) * 16, 16), 16)
        x_copy.append(
            remote(
                mixed.at[own],
                from_exp.at[d],
                x_send.at[d],
                x_recv.at[d],
                (lax.axis_index("ctx"), other(d)),
            )
        )
        x_copy[d].start()
    total = (
        residual_own[...] + mixed[pl.ds(pl.multiple_of(e * 16, 16), 16), :].astype(jnp.float32)
    )
    for d in range(1, 8):
        x_copy[d].wait_recv()
        total += from_exp[d].astype(jnp.float32)
    out_ref[...] = total.astype(jnp.bfloat16)

    for i in range(8):
        if i > 0:
            rd_copy[i].wait_send()
            x_copy[i].wait_send()
            if not any(step == "sent" and i in blocks for step, *blocks in SCHEDULE):
                d_copy[i].wait_send()
        rf_copy[i].wait_send()
        f_copy[i].wait_send()
    for i in range(16):
        c_copy[i].wait_send()
        rc_copy[i].wait_send()


def moe(normed, residual_own, expert_ids, gate_weights, w_in, w_out):
    model = normed.shape[1]
    width = model // 4
    block = (5, 16, width)
    half = jnp.bfloat16
    vmem = pl.BlockSpec(memory_space=pltpu.VMEM)
    dma = pltpu.SemaphoreType.DMA
    return pl.pallas_call(
        moe_kernel,
        out_shape=jax.ShapeDtypeStruct(residual_own.shape, half),
        in_specs=[vmem] * 4 + [pl.BlockSpec(memory_space=pl.ANY)] * 2,
        out_specs=vmem,
        scratch_shapes=[
            pltpu.VMEM(w_in.shape, half),
            pltpu.VMEM(w_out.shape, half),
            dma((2,)),
            pltpu.VMEM((128, 128), half),
            pltpu.VMEM((128, 512), half),
            pltpu.VMEM((4, 128, 256), half),
            pltpu.VMEM((4, 128, 256), half),
            pltpu.VMEM((8,) + block, half),
            pltpu.VMEM((32,) + block, half),
            pltpu.VMEM((320, 2 * FFQ), jnp.float32),
            pltpu.VMEM((64, model), half),
            pltpu.VMEM((320, FFQ), half),
            pltpu.VMEM((64, model), half),
            pltpu.VMEM((32,) + block, half),
            pltpu.VMEM((16,) + block, half),
            pltpu.VMEM((8,) + block, half),
            pltpu.VMEM((8,) + block, half),
            pltpu.VMEM((8,) + block, half),
            pltpu.VMEM((8,) + block, half),
            pltpu.VMEM((128, model), half),
            pltpu.VMEM((8, 16, model), half),
            dma((8,)),
            dma((8,)),
            dma((8,)),
            dma((8,)),
            dma((16,)),
            dma((16,)),
            dma((16,)),
            dma((16,)),
            dma((8,)),
            dma((8,)),
            dma((8,)),
            dma((8,)),
            dma((8,)),
            dma((8,)),
        ],
        compiler_params=pltpu.CompilerParams(
            collective_id=1, has_side_effects=True, vmem_limit_bytes=56 * 2**20
        ),
        name="moe",
    )(normed, residual_own, expert_ids.T, gate_weights.T, w_in, w_out)


def per_device(
    query,
    new_kv,
    old_kv,
    new_pos,
    o_weight,
    hidden,
    norm_gain,
    expert_ids,
    gate_weights,
    w_in,
    w_out,
):
    normed, residual_own = attention(
        query, new_kv, old_kv, new_pos, o_weight, hidden, norm_gain
    )
    return moe(
        normed, residual_own, expert_ids, gate_weights, w_in[0, 0], w_out[0, 0]
    )


def solution(mesh):
    return jax.shard_map(
        per_device,
        mesh=mesh,
        in_specs=(
            P("ctx", "exp"),
            P(None, "ctx", None),
            P(None, "ctx", None),
            P("ctx"),
            P("exp", "ctx"),
            P(("ctx", "exp"), None),
            P(),
            P("ctx", None),
            P("ctx", None),
            P("ctx", "exp", None, None),
            P("ctx", "exp", None, None),
        ),
        out_specs=P(("ctx", "exp"), None),
        check_vma=False,
    )
```

```python
import jax
import jax.numpy as jnp
from jax import lax
from jax.experimental import pallas as pl
from jax.experimental.pallas import tpu as pltpu
from jax.sharding import PartitionSpec as P

HD = 128
FFQ = 384
MESH = pl.DeviceIdType.MESH
ARRIVE = (1, 2, 6, 3, 7, 4, 5)
ATTENTION = 33
NORMED = 13
ORDER = (0, 4, 1, 3, 5, 7, 2, 6)


CHUNKS = ((0, 1), (2, 6), (3, 7), (4,), (5,))
SCHEDULE = (
    ("send", 2, 6, 1),
    ("pass", 0, 1),
    ("sent", 2),
    ("send", 3),
    ("sent", 6),
    ("send", 7),
    ("pass", 2, 6),
    ("core", 0, 1),
    ("work", 0),
    ("sent", 3, 7),
    ("send", 4),
    ("pass", 3, 7),
    ("core", 2, 6),
    ("work", 1),
    ("sent", 4),
    ("send", 5),
    ("pass", 4),
    ("back", 2, 6),
    ("core", 3, 7),
    ("work", 2),
    ("core", 4),
    ("back", 3, 7),
    ("work", 3),
    ("pass", 5),
    ("home", 2, 6),
    ("back", 4),
    ("core", 5),
    ("home", 3, 7),
    ("work", 4),
    ("home", 4),
    ("back", 5, 1, 0),
    ("home", 5, 1, 0),
)


def place():
    ctx = lax.axis_index("ctx")
    return ctx // 8, (ctx // 2) % 4, ctx % 2, lax.axis_index("exp")


def ctx_of(hi, y, core):
    return lax.rem(hi, 4) * 8 + y * 2 + core


def across(i):
    hi, y, core, e = place()
    return (ctx_of(hi + i // 2, y if i % 2 == 0 else 3 - y, core), e)


def remote(src, dst, send, recv, device):
    return pltpu.make_async_remote_copy(
        src_ref=src, dst_ref=dst, send_sem=send, recv_sem=recv, device_id=device, device_id_type=MESH
    )


def attention(
    query,
    new_kv,
    old_kv,
    new_pos,
    o_weight,
    hidden,
    norm_gain,
    meanwhile,
    kv,
    weight,
    queries,
    bias,
    top,
    acc,
    attended,
    projected,
    from_exp,
    summed,
    pieces,
    gathered,
    own_normed,
    normed,
    residual_own,
    kz_send,
    kz_recv,
    ky_send,
    ky_recv,
    kc_send,
    kc_recv,
    wz_send,
    wz_recv,
    ay_send,
    ay_recv,
    ac_send,
    ac_recv,
    x_send,
    x_recv,
    p_send,
    p_recv,
    n_send,
    n_recv,
):
    hi, y, core, e = place()
    ctx = lax.axis_index("ctx")
    model = hidden.shape[1]
    sibling = (ctx_of(hi, y, 1 - core), e)
    up = (ctx_of(hi, lax.rem(y + 1, 4), core), e)
    down = (ctx_of(hi, lax.rem(y + 3, 4), core), e)

    def along(d):
        return (ctx_of(hi + d, y, core), e)

    parity = lax.rem(e, 2)
    outer = (ctx_of(hi + 3 + 2 * parity, y, core), e + 1 - 2 * parity)
    inner = (ctx, e + 1 - 2 * parity)

    def behind(s):
        return (ctx_of(hi, lax.rem(y + 4 - s % 4, 4), core if s < 4 else 1 - core), e)

    def other(d):
        return lax.rem(e + d, 8)

    barrier = pltpu.get_barrier_semaphore()
    for d in range(1, 4):
        pl.semaphore_signal(barrier, inc=1, device_id=along(d), device_id_type=MESH)
        pl.semaphore_signal(
            barrier, inc=1, device_id=across(2 * d + 1), device_id_type=MESH
        )
    pl.semaphore_signal(barrier, inc=1, device_id=outer, device_id_type=MESH)
    for s in range(1, 8):
        pl.semaphore_signal(barrier, inc=1, device_id=behind(s), device_id_type=MESH)
    for d in range(1, 8):
        pl.semaphore_signal(barrier, inc=1, device_id=(ctx, other(d)), device_id_type=MESH)

    lanes = pl.ds(pl.multiple_of((e // 2) * HD, HD), HD)
    kv[0, 0:256] = old_kv[0, :, lanes]
    kv[0, 256:384] = new_kv[0, :, lanes]
    for b in range(3):
        values = new_kv[1, :, lanes] if b == 2 else old_kv[1, b * 128 : (b + 1) * 128, lanes]
        kv[0, 384 + b * 128 : 512 + b * 128] = values.astype(jnp.float32).T.astype(jnp.bfloat16)
    own_pos = new_pos[...]
    row = lax.broadcasted_iota(jnp.int32, (16, 128), 0)
    kv[0, 768:784] = (
        jnp.where(row == 0, own_pos >> 6, jnp.where(row == 1, own_pos & 63, 0))
        .astype(jnp.float32)
        .astype(jnp.bfloat16)
    )
    weight[0] = o_weight[...]

    pl.semaphore_wait(barrier, 21)

    kz = [None] + [
        remote(kv.at[d * 8 - 8], kv.at[d * 8], kz_send.at[d], kz_recv.at[d], device)
        for d, device in ((1, outer), (2, inner), (3, outer))
    ]
    wz = [None] + [
        remote(weight.at[0], weight.at[d], wz_send.at[d], wz_recv.at[d], along(d))
        for d in range(1, 4)
    ]
    ky = {}
    for d in range(4):
        for dy, device in ((1, up), (3, down)):
            ky[dy, d] = remote(
                kv.at[d * 8],
                kv.at[d * 8 + dy],
                ky_send.at[d * 4 + dy],
                ky_recv.at[d * 4 + dy],
                device,
            )
        ky[2, d] = remote(
            kv.at[d * 8 + (1 if d % 2 == 0 else 3)],
            kv.at[d * 8 + 2],
            ky_send.at[d * 4 + 2],
            ky_recv.at[d * 4 + 2],
            up if d % 2 == 0 else down,
        )
    kc = {
        (dy, d): remote(
            kv.at[d * 8 + dy],
            kv.at[d * 8 + 4 + dy],
            kc_send.at[d * 4 + dy],
            kc_recv.at[d * 4 + dy],
            sibling,
        )
        for d in range(4)
        for dy in range(4)
    }

    def begin_y(d):
        ky[1, d].start()
        ky[3, d].start()
        kc[0, d].start()

    def pass_on(d):
        ky[1, d].wait_recv()
        if d % 2 == 0:
            ky[2, d].start()
        kc[1, d].start()
        ky[3, d].wait_recv()
        if d % 2 == 1:
            ky[2, d].start()
        kc[3, d].start()

    def last(d):
        ky[2, d].wait_recv()
        kc[2, d].start()

    kz[1].start()
    begin_y(0)
    meanwhile()

    for h in range(8):
        part = query[:, h * HD : (h + 1) * HD].astype(jnp.float32).T.astype(jnp.bfloat16)
        queries[h // 2, :, (h % 2) * 128 : (h % 2 + 1) * 128] = part
    top[...] = jnp.full_like(top, -1e30)
    acc[...] = jnp.zeros_like(acc)
    factor = 1.4426950408889634 / HD**0.5

    def attend(blocks):
        for b in range(4):
            digits = kv[blocks[b], 768:784].astype(jnp.float32)
            place_of = digits[0:1] * 64.0 + digits[1:2]
            column = jnp.broadcast_to(place_of, (128, 128)).T
            seen = column <= own_pos.astype(jnp.float32)
            bias[b] = jnp.where(seen, 0.0, -1e30)

        @pl.loop(0, 4, unroll=4)
        def _(t):
            part = queries[t]
            pieces = []
            for b in range(4):
                scores = jnp.dot(kv[blocks[b], 0:384], part, preferred_element_type=jnp.float32)
                wide = jnp.concatenate([bias[b], bias[b]], 1)
                pieces += [scores[:256], scores[256:] + wide]
            old_top = top[t, 0:1]
            new_top = old_top
            for piece in pieces:
                new_top = jnp.maximum(new_top, jnp.max(piece, 0, keepdims=True))
            probs = jnp.concatenate(
                [jnp.exp2((piece - new_top) * factor).astype(jnp.bfloat16) for piece in pieces], 0
            )
            values = jnp.concatenate(
                [
                    kv[blocks[b], 384 + 128 * i : 512 + 128 * i]
                    for b in range(4)
                    for i in range(3)
                ],
                1,
            )
            ones = jnp.ones((16, values.shape[1]), jnp.bfloat16)
            added = jnp.dot(
                jnp.concatenate([values, ones], 0), probs, preferred_element_type=jnp.float32
            )
            acc[t] = acc[t] * jnp.exp2((old_top - new_top) * factor) + added
            top[t] = jnp.broadcast_to(new_top, (8, 256))

    def attend_near(d):
        kc[0, d].wait_recv()
        attend([d * 8 + b for b in (0, 4, 1, 3)])

    def attend_far(d):
        for dy in (1, 3, 2):
            kc[dy, d].wait_recv()
        attend([d * 8 + b for b in (5, 7, 2, 6)])

    kz[1].wait_recv()
    kz[2].start()
    begin_y(1)
    pass_on(0)
    attend_near(0)
    kz[2].wait_recv()
    kz[3].start()
    begin_y(2)
    for d in (1, 3):
        wz[d].start()
    last(0)
    pass_on(1)
    attend_far(0)
    attend_near(1)
    kz[3].wait_recv()
    begin_y(3)
    wz[2].start()
    last(1)
    pass_on(2)
    attend_far(1)
    attend_near(2)
    last(2)
    pass_on(3)
    attend_far(2)
    attend_near(3)
    last(3)
    attend_far(3)

    for h in range(8):
        part = slice((h % 2) * 128, (h % 2 + 1) * 128)
        scaled = acc[h // 2, 0:128, part] / acc[h // 2, 128:129, part]
        attended[0, :, h * HD : (h + 1) * HD] = scaled.T.astype(jnp.bfloat16)

    def half_of(slot, k):
        return attended.at[slot, pl.ds(k * 64, 64)]

    ay = {
        1: remote(attended.at[0], attended.at[1], ay_send.at[0], ay_recv.at[0], up),
        3: remote(attended.at[0], attended.at[3], ay_send.at[1], ay_recv.at[1], down),
        "up": remote(half_of(1, 0), half_of(2, 0), ay_send.at[2], ay_recv.at[2], up),
        "down": remote(half_of(3, 1), half_of(2, 1), ay_send.at[3], ay_recv.at[3], down),
    }
    ac = [
        remote(attended.at[s], attended.at[4 + s], ac_send.at[s], ac_recv.at[s], sibling)
        for s in range(4)
    ]
    ay[1].start()
    ay[3].start()
    ac[0].start()
    for d in range(1, 4):
        wz[d].wait_recv()

    def project(s):
        for pair in range(2):
            both = jnp.concatenate([weight[2 * pair], weight[2 * pair + 1]], 1)
            result = jnp.dot(attended[s], both, preferred_element_type=jnp.float32)
            projected[:, ORDER.index(s), :, pair * 256 : (pair + 1) * 256] = result.astype(
                jnp.bfloat16
            ).reshape(8, 16, 256)

    x_copy = [
        None
        if d == 0
        else remote(
            projected.at[other(d), pl.ds(half * 4, 4)],
            from_exp.at[d, pl.ds(half * 4, 4)],
            x_send.at[half * 8 + d],
            x_recv.at[half * 8 + d],
            (ctx, other(d)),
        )
        for half in range(2)
        for d in range(8)
    ]
    p_copy = [None] + [
        remote(summed.at[s], pieces.at[s], p_send.at[s], p_recv.at[s], behind(s))
        for s in range(1, 8)
    ]

    project(0)
    ac[0].wait_recv()
    project(4)
    ay[1].wait_recv()
    ay["up"].start()
    ac[1].start()
    ay[3].wait_recv()
    ay["down"].start()
    ac[3].start()
    project(1)
    project(3)
    for d in range(1, 8):
        x_copy[d].start()
    ac[1].wait_recv()
    project(5)
    ac[3].wait_recv()
    project(7)
    ay["up"].wait_recv()
    ay["down"].wait_recv()
    ac[2].start()
    project(2)
    ac[2].wait_recv()
    project(6)
    for d in range(1, 8):
        x_copy[8 + d].start()

    for half in range(2):
        for d in range(1, 8):
            x_copy[half * 8 + d].wait_recv()
        for k in range(half * 4, half * 4 + 4):
            s = ORDER[k]
            total = projected[e, k].astype(jnp.float32)
            for d in range(1, 8):
                total += from_exp[d, k].astype(jnp.float32)
            if s == 0:
                pieces[0] = total
            else:
                summed[s] = total
                p_copy[s].start()
    for s in ORDER:
        if s > 0:
            p_copy[s].wait_recv()
        sender = lax.rem(y + s % 4, 4) * 2 + (core if s < 4 else 1 - core)
        for d in range(4):
            owner = lax.rem(hi + 4 - d, 4) * 8 + sender
            gathered[:, pl.ds(pl.multiple_of(owner * 128, 128), 128)] = pieces[
                s, :, d * 128 : (d + 1) * 128
            ]

    def rows_of(index):
        return pl.ds(pl.multiple_of(index * 16, 16), 16)

    residual = hidden[...].astype(jnp.float32) + gathered[...]
    residual_own[...] = residual
    mean = jnp.sum(residual * residual, 1, keepdims=True) * (1.0 / model)
    own = (residual * lax.rsqrt(mean + 1e-06) * norm_gain[...]).astype(jnp.bfloat16)
    own_normed[...] = own
    n_copy = [None] + [
        remote(own_normed, normed.at[rows_of(e)], n_send.at[d], n_recv.at[d], (ctx, other(d)))
        for d in range(1, 8)
    ]
    for d in range(1, 8):
        n_copy[d].start()
    normed[rows_of(e), :] = own
    for d in range(1, 8):
        n_copy[d].wait_recv()

    for d in range(1, 4):
        kz[d].wait_send()
        wz[d].wait_send()
    for d in range(4):
        for dy in range(4):
            if dy > 0:
                ky[dy, d].wait_send()
            kc[dy, d].wait_send()
        ac[d].wait_send()
    for copy in ay.values():
        copy.wait_send()
    for d in range(1, 8):
        x_copy[d].wait_send()
        x_copy[8 + d].wait_send()
        p_copy[d].wait_send()
        n_copy[d].wait_send()


def tables(ids, gates, pick, pick_rest, mix_hi, mix_lo):
    hi, y, core, e = place()
    chosen = ids[...]
    weights = gates[...]
    members, factors = [], []
    for i in range(8):
        expert = e * 8 + lax.rem(hi + i // 2, 4) * 2 + lax.rem(y // 2 + i, 2)
        hit = chosen == expert
        members.append(jnp.max(jnp.where(hit, 1.0, 0.0), 0, keepdims=True))
        factors.append(jnp.sum(jnp.where(hit, weights, 0.0), 0, keepdims=True))
    member = jnp.concatenate(members, 0)
    row = lax.broadcasted_iota(jnp.int32, (128, 128), 0)
    column = lax.broadcasted_iota(jnp.int32, (128, 128), 1)
    before = jnp.where(row < column, 1.0, 0.0).astype(jnp.bfloat16)
    rank = jnp.dot(member.astype(jnp.bfloat16), before, preferred_element_type=jnp.float32)
    slot = jnp.where(member > 0.5, rank, -1.0)
    slots = jnp.concatenate([jnp.broadcast_to(slot[i : i + 1], (16, 128)) for i in range(8)], 0)
    factor = jnp.concatenate([jnp.broadcast_to(f, (16, 128)) for f in factors], 0)
    r = row & 15
    for m in range(5):
        if m < 4:
            wanted = jnp.where(r >> 2 == m, 16 + (r & 3), -2)
        else:
            wanted = r
        found = slots == wanted.astype(jnp.float32)
        ones = jnp.where(found, 1.0, 0.0).astype(jnp.bfloat16)
        mix = jnp.where(found, factor, 0.0).T
        high = mix.astype(jnp.bfloat16)
        low = (mix - high.astype(jnp.float32)).astype(jnp.bfloat16)
        if m < 4:
            pick_rest[:, m * 128 : (m + 1) * 128] = ones
            mix_hi[m, :, 128:256] = high
            mix_lo[m, :, 128:256] = low
        else:
            pick[...] = ones
            for q in range(4):
                mix_hi[q, :, 0:128] = high
                mix_lo[q, :, 0:128] = low


def moe(
    normed,
    residual_own,
    out_ref,
    loads,
    w_in,
    w_out,
    pick,
    pick_rest,
    mix_hi,
    mix_lo,
    sent,
    got,
    both,
    rest_in,
    act,
    rest_out,
    part,
    from_core,
    to_pair,
    from_pair,
    to_home,
    home,
    mixed,
    from_exp,
    d_send,
    d_recv,
    f_send,
    f_recv,
    c_send,
    c_recv,
    rc_send,
    rc_recv,
    rf_send,
    rf_recv,
    rd_send,
    rd_recv,
    x_send,
    x_recv,
):
    hi, y, core, e = place()
    width = sent.shape[-1]
    sibling = (ctx_of(hi, y, 1 - core), e)
    pair = (ctx_of(hi, y + 1 - 2 * lax.rem(y, 2), core), e)

    def slot(i, group):
        chunk = [i in blocks for blocks in CHUNKS].index(True)
        blocks = CHUNKS[chunk]
        return 4 * sum(map(len, CHUNKS[:chunk])) + group * len(blocks) + blocks.index(i)

    def back(i):
        return (ctx_of(hi + 4 - i // 2, y if i % 2 == 0 else 3 - y, core), e)

    def other(d):
        return lax.rem(e + d, 8)

    for m in range(4):
        rows = jnp.dot(
            pick[...], normed[:, m * width : (m + 1) * width], preferred_element_type=jnp.float32
        )
        sent[:, m] = rows.astype(jnp.bfloat16).reshape(8, 16, width)
    rest = jnp.zeros((128, width), jnp.float32)
    for m in range(4):
        rest += jnp.dot(
            pick_rest[:, m * 128 : (m + 1) * 128],
            normed[:, m * width : (m + 1) * width],
            preferred_element_type=jnp.float32,
        )
    sent[:, 4] = rest.astype(jnp.bfloat16).reshape(8, 16, width)
    got[slot(0, 0)] = sent[0]

    d_copy = [
        None if i == 0 else remote(
            sent.at[i], got.at[slot(i, 0)], d_send.at[i], d_recv.at[i], across(i)
        )
        for i in range(8)
    ]
    f_copy = [
        remote(got.at[slot(i, 0)], got.at[slot(i, 2)], f_send.at[i], f_recv.at[i], pair)
        for i in range(8)
    ]
    c_copy = [
        remote(got.at[slot(i, g)], got.at[slot(i, g + 1)], c_send.at[k], c_recv.at[k], sibling)
        for k, (g, i) in enumerate((g, i) for g in (0, 2) for i in range(8))
    ]
    rc_copy = [
        remote(part.at[slot(i, g)], from_core.at[k], rc_send.at[k], rc_recv.at[k], sibling)
        for k, (g, i) in enumerate((g, i) for g in (1, 3) for i in range(8))
    ]
    rf_copy = [
        remote(to_pair.at[i], from_pair.at[i], rf_send.at[i], rf_recv.at[i], pair)
        for i in range(8)
    ]
    rd_copy = [
        None if i == 0 else remote(to_home.at[i], home.at[i], rd_send.at[i], rd_recv.at[i], back(i))
        for i in range(8)
    ]
    def regroup(m, rows, columns):
        row = lax.broadcasted_iota(jnp.int32, (rows, columns), 0)
        column = lax.broadcasted_iota(jnp.int32, (rows, columns), 1)
        small, large = (row, column) if rows < columns else (column, row)
        return (large == (small // 4) * 16 + m * 4 + small % 4).astype(jnp.bfloat16)

    def experts(base, count):
        tall, low = count * 16, count * 4
        rest_rows = got[base : base + count, 4].reshape(tall, width)
        for m in range(4):
            rest_in[:low, m * width : (m + 1) * width] = jnp.dot(
                regroup(m, low, tall), rest_rows, preferred_element_type=jnp.float32
            ).astype(jnp.bfloat16)

        @pl.loop(0, 3)
        def _(n):
            columns = pl.ds(pl.multiple_of(n * 256, 256), 256)
            total = jnp.zeros((tall + low, 256), jnp.float32)
            for m in range(4):
                rows = jnp.concatenate(
                    [
                        got[base : base + count, m].reshape(tall, width),
                        rest_in[:low, m * width : (m + 1) * width],
                    ],
                    0,
                )
                total += jnp.dot(
                    rows,
                    w_in[m * width : (m + 1) * width, columns],
                    preferred_element_type=jnp.float32,
                )
            both[: tall + low, columns] = total

        gate = both[: tall + low, :FFQ]
        act[: tall + low] = (gate / (1.0 + jnp.exp(-gate)) * both[: tall + low, FFQ:]).astype(
            jnp.bfloat16
        )
        steps = width // 256

        @pl.loop(0, 4 * steps)
        def _(n):
            columns = pl.ds(pl.multiple_of(n * 256, 256), 256)
            inner = pl.ds(pl.multiple_of((n % steps) * 256, 256), 256)
            result = jnp.dot(
                act[: tall + low], w_out[:, columns], preferred_element_type=jnp.float32
            ).astype(jnp.bfloat16)
            part[base : base + count, n // steps, :, inner] = result[:tall].reshape(count, 16, 256)
            rest_out[:low, columns] = result[tall:]

        rest_part = jnp.zeros((tall, width), jnp.float32)
        for m in range(4):
            rest_part += jnp.dot(
                regroup(m, tall, low),
                rest_out[:low, m * width : (m + 1) * width],
                preferred_element_type=jnp.float32,
            )
        part[base : base + count, 4] = rest_part.astype(jnp.bfloat16).reshape(count, 16, width)

    loaded = False
    for step, i in ((step, i) for step, *blocks in SCHEDULE for i in blocks):
        if step == "send":
            d_copy[i].start()
        elif step == "sent":
            d_copy[i].wait_send()
        elif step == "pass":
            if i > 0:
                d_copy[i].wait_recv()
            f_copy[i].start()
            c_copy[i].start()
        elif step == "core":
            f_copy[i].wait_recv()
            c_copy[8 + i].start()
        elif step == "work":
            if not loaded:
                for load in loads:
                    load.wait()
                loaded = True
            for block in CHUNKS[i]:
                c_copy[block].wait_recv()
                c_copy[8 + block].wait_recv()
            experts(slot(CHUNKS[i][0], 0), 4 * len(CHUNKS[i]))
            for block in CHUNKS[i]:
                rc_copy[8 + block].start()
            for block in CHUNKS[i]:
                rc_copy[block].start()
        elif step == "back":
            rc_copy[8 + i].wait_recv()
            to_pair[i] = (
                part[slot(i, 2)].astype(jnp.float32) + from_core[8 + i].astype(jnp.float32)
            ).astype(jnp.bfloat16)
            rf_copy[i].start()
        elif step == "home":
            rc_copy[i].wait_recv()
            rf_copy[i].wait_recv()
            total = (
                part[slot(i, 0)].astype(jnp.float32)
                + from_core[i].astype(jnp.float32)
                + from_pair[i].astype(jnp.float32)
            ).astype(jnp.bfloat16)
            if i == 0:
                home[0] = total
            else:
                to_home[i] = total
                rd_copy[i].start()
    for i in ARRIVE:
        rd_copy[i].wait_recv()

    for m in range(4):
        rows = jnp.concatenate(
            [home[:, m].reshape(128, width), home[:, 4].reshape(128, width)], 0
        )
        mixed[:, m * width : (m + 1) * width] = (
            jnp.dot(mix_hi[m], rows, preferred_element_type=jnp.float32)
            + jnp.dot(mix_lo[m], rows, preferred_element_type=jnp.float32)
        ).astype(jnp.bfloat16)

    x_copy = [None]
    for d in range(1, 8):
        own = pl.ds(pl.multiple_of(other(d) * 16, 16), 16)
        x_copy.append(
            remote(
                mixed.at[own],
                from_exp.at[d],
                x_send.at[d],
                x_recv.at[d],
                (lax.axis_index("ctx"), other(d)),
            )
        )
        x_copy[d].start()
    total = (
        residual_own[...] + mixed[pl.ds(pl.multiple_of(e * 16, 16), 16), :].astype(jnp.float32)
    )
    for d in range(1, 8):
        x_copy[d].wait_recv()
        total += from_exp[d].astype(jnp.float32)
    out_ref[...] = total.astype(jnp.bfloat16)

    for i in range(8):
        if i > 0:
            rd_copy[i].wait_send()
            x_copy[i].wait_send()
            if not any(step == "sent" and i in blocks for step, *blocks in SCHEDULE):
                d_copy[i].wait_send()
        rf_copy[i].wait_send()
        f_copy[i].wait_send()
    for i in range(16):
        c_copy[i].wait_send()
        rc_copy[i].wait_send()


def kernel(*refs):
    inputs, (ids, gates, w_in_hbm, w_out_hbm, out_ref), rest = refs[:7], refs[7:12], refs[12:]
    first, (w_in, w_out, w_sem), second = rest[:ATTENTION], rest[ATTENTION:][:3], rest[ATTENTION:][3:]
    loads = [
        pltpu.make_async_copy(w_in_hbm, w_in, w_sem.at[0]),
        pltpu.make_async_copy(w_out_hbm, w_out, w_sem.at[1]),
    ]

    def meanwhile():
        for load in loads:
            load.start()
        tables(ids, gates, *second[:4])

    attention(*inputs, meanwhile, *first)
    moe(first[NORMED], first[NORMED + 1], out_ref, loads, w_in, w_out, *second)


def layer(
    query,
    new_kv,
    old_kv,
    new_pos,
    o_weight,
    hidden,
    norm_gain,
    expert_ids,
    gate_weights,
    w_in,
    w_out,
):
    rows = query.shape[0]
    model = hidden.shape[1]
    width = model // 4
    block = (5, 16, width)
    half = jnp.bfloat16
    vmem = pl.BlockSpec(memory_space=pltpu.VMEM)

    def dma(*counts):
        return [pltpu.SemaphoreType.DMA((count,)) for count in counts for _ in range(2)]

    first = [
        pltpu.VMEM((32, 784, HD), half),
        pltpu.VMEM((4,) + o_weight.shape, half),
        pltpu.VMEM((4, HD, 256), half),
        pltpu.VMEM((4, 128, 128), jnp.float32),
        pltpu.VMEM((4, 8, 256), jnp.float32),
        pltpu.VMEM((4, 144, 256), jnp.float32),
        pltpu.VMEM((8,) + query.shape, half),
        pltpu.VMEM((8, 8, 16, 512), half),
        pltpu.VMEM((8, 8, 16, 512), half),
        pltpu.VMEM((8, 16, 512), jnp.float32),
        pltpu.VMEM((8, 16, 512), jnp.float32),
        pltpu.VMEM(hidden.shape, jnp.float32),
        pltpu.VMEM(hidden.shape, half),
        pltpu.VMEM((rows, model), half),
        pltpu.VMEM(hidden.shape, jnp.float32),
    ] + dma(4, 16, 16, 4, 4, 4, 16, 8, 8)
    assert len(first) == ATTENTION
    loaded = [
        pltpu.VMEM(w_in.shape, half),
        pltpu.VMEM(w_out.shape, half),
        pltpu.SemaphoreType.DMA((2,)),
    ]
    second = [
        pltpu.VMEM((128, 128), half),
        pltpu.VMEM((128, 512), half),
        pltpu.VMEM((4, 128, 256), half),
        pltpu.VMEM((4, 128, 256), half),
        pltpu.VMEM((8,) + block, half),
        pltpu.VMEM((32,) + block, half),
        pltpu.VMEM((160, 2 * FFQ), jnp.float32),
        pltpu.VMEM((32, model), half),
        pltpu.VMEM((160, FFQ), half),
        pltpu.VMEM((32, model), half),
        pltpu.VMEM((32,) + block, half),
        pltpu.VMEM((16,) + block, half),
        pltpu.VMEM((8,) + block, half),
        pltpu.VMEM((8,) + block, half),
        pltpu.VMEM((8,) + block, half),
        pltpu.VMEM((8,) + block, half),
        pltpu.VMEM((128, model), half),
        pltpu.VMEM((8, 16, model), half),
    ] + dma(8, 8, 16, 16, 8, 8, 8)
    return pl.pallas_call(
        kernel,
        out_shape=jax.ShapeDtypeStruct(hidden.shape, half),
        in_specs=[vmem] * 9 + [pl.BlockSpec(memory_space=pl.ANY)] * 2,
        out_specs=vmem,
        scratch_shapes=first + loaded + second,
        compiler_params=pltpu.CompilerParams(
            collective_id=1, has_side_effects=True, vmem_limit_bytes=58 * 2**20
        ),
        name="layer",
    )(
        query,
        new_kv,
        old_kv,
        new_pos.reshape(1, rows),
        o_weight,
        hidden,
        norm_gain.reshape(1, model),
        expert_ids.T,
        gate_weights.T,
        w_in,
        w_out,
    )


def per_device(
    query,
    new_kv,
    old_kv,
    new_pos,
    o_weight,
    hidden,
    norm_gain,
    expert_ids,
    gate_weights,
    w_in,
    w_out,
):
    return layer(
        query,
        new_kv,
        old_kv,
        new_pos,
        o_weight,
        hidden,
        norm_gain,
        expert_ids,
        gate_weights,
        w_in[0, 0],
        w_out[0, 0],
    )


def solution(mesh):
    return jax.shard_map(
        per_device,
        mesh=mesh,
        in_specs=(
            P("ctx", "exp"),
            P(None, "ctx", None),
            P(None, "ctx", None),
            P("ctx"),
            P("exp", "ctx"),
            P(("ctx", "exp"), None),
            P(),
            P("ctx", None),
            P("ctx", None),
            P("ctx", "exp", None, None),
            P("ctx", "exp", None, None),
        ),
        out_specs=P(("ctx", "exp"), None),
        check_vma=False,
    )
```

```python
import jax
import jax.numpy as jnp
from jax import lax
from jax.experimental import pallas as pl
from jax.experimental.pallas import tpu as pltpu
from jax.sharding import PartitionSpec as P

HD = 128
FFQ = 384
MESH = pl.DeviceIdType.MESH
ARRIVE = (1, 2, 6, 3, 7, 4, 5)
ATTENTION = 33
NORMED = 13
ORDER = (0, 4, 1, 3, 5, 7, 2, 6)


CHUNKS = ((0, 1), (2, 6), (3, 7), (4,), (5,))
SCHEDULE = (
    ("send", 2, 6, 1),
    ("pass", 0, 1),
    ("sent", 2),
    ("send", 3),
    ("sent", 6),
    ("send", 7),
    ("pass", 2, 6),
    ("core", 0, 1),
    ("work", 0),
    ("sent", 3, 7),
    ("send", 4),
    ("pass", 3, 7),
    ("core", 2, 6),
    ("work", 1),
    ("sent", 4),
    ("send", 5),
    ("pass", 4),
    ("back", 2, 6),
    ("core", 3, 7),
    ("work", 2),
    ("core", 4),
    ("back", 3, 7),
    ("work", 3),
    ("pass", 5),
    ("home", 2, 6),
    ("back", 4),
    ("core", 5),
    ("home", 3, 7),
    ("work", 4),
    ("home", 4),
    ("back", 5, 1, 0),
    ("home", 5, 1, 0),
)


def place():
    ctx = lax.axis_index("ctx")
    return ctx // 8, (ctx // 2) % 4, ctx % 2, lax.axis_index("exp")


def ctx_of(hi, y, core):
    return lax.rem(hi, 4) * 8 + y * 2 + core


def across(i):
    hi, y, core, e = place()
    return (ctx_of(hi + i // 2, y if i % 2 == 0 else 3 - y, core), e)


def remote(src, dst, send, recv, device):
    return pltpu.make_async_remote_copy(
        src_ref=src, dst_ref=dst, send_sem=send, recv_sem=recv, device_id=device, device_id_type=MESH
    )


def attention(
    query,
    new_kv,
    old_kv,
    new_pos,
    o_weight,
    hidden,
    norm_gain,
    meanwhile,
    kv,
    weight,
    queries,
    bias,
    top,
    acc,
    attended,
    projected,
    from_exp,
    summed,
    pieces,
    gathered,
    own_normed,
    normed,
    residual_own,
    kz_send,
    kz_recv,
    ky_send,
    ky_recv,
    kc_send,
    kc_recv,
    wz_send,
    wz_recv,
    ay_send,
    ay_recv,
    ac_send,
    ac_recv,
    x_send,
    x_recv,
    p_send,
    p_recv,
    n_send,
    n_recv,
):
    hi, y, core, e = place()
    ctx = lax.axis_index("ctx")
    model = hidden.shape[1]
    sibling = (ctx_of(hi, y, 1 - core), e)
    up = (ctx_of(hi, lax.rem(y + 1, 4), core), e)
    down = (ctx_of(hi, lax.rem(y + 3, 4), core), e)

    def along(d):
        return (ctx_of(hi + d, y, core), e)

    parity = lax.rem(e, 2)
    outer = (ctx_of(hi + 3 + 2 * parity, y, core), e + 1 - 2 * parity)
    inner = (ctx, e + 1 - 2 * parity)

    def behind(s):
        return (ctx_of(hi, lax.rem(y + 4 - s % 4, 4), core if s < 4 else 1 - core), e)

    def other(d):
        return lax.rem(e + d, 8)

    barrier = pltpu.get_barrier_semaphore()
    for d in range(1, 4):
        pl.semaphore_signal(barrier, inc=1, device_id=along(d), device_id_type=MESH)
        pl.semaphore_signal(
            barrier, inc=1, device_id=across(2 * d + 1), device_id_type=MESH
        )
    pl.semaphore_signal(barrier, inc=1, device_id=outer, device_id_type=MESH)
    for s in range(1, 8):
        pl.semaphore_signal(barrier, inc=1, device_id=behind(s), device_id_type=MESH)
    for d in range(1, 8):
        pl.semaphore_signal(barrier, inc=1, device_id=(ctx, other(d)), device_id_type=MESH)

    lanes = pl.ds(pl.multiple_of((e // 2) * HD, HD), HD)
    kv[0, 0:256] = old_kv[0, :, lanes]
    kv[0, 256:384] = new_kv[0, :, lanes]
    for b in range(3):
        values = new_kv[1, :, lanes] if b == 2 else old_kv[1, b * 128 : (b + 1) * 128, lanes]
        kv[0, 384 + b * 128 : 512 + b * 128] = values.astype(jnp.float32).T.astype(jnp.bfloat16)
    own_pos = new_pos[...]
    row = lax.broadcasted_iota(jnp.int32, (16, 128), 0)
    kv[0, 768:784] = (
        jnp.where(row == 0, own_pos >> 6, jnp.where(row == 1, own_pos & 63, 0))
        .astype(jnp.float32)
        .astype(jnp.bfloat16)
    )
    weight[0] = o_weight[...]

    pl.semaphore_wait(barrier, 21)

    kz = [None] + [
        remote(kv.at[d * 8 - 8], kv.at[d * 8], kz_send.at[d], kz_recv.at[d], device)
        for d, device in ((1, outer), (2, inner), (3, outer))
    ]
    wz = [None] + [
        remote(weight.at[0], weight.at[d], wz_send.at[d], wz_recv.at[d], along(d))
        for d in range(1, 4)
    ]
    ky = {}
    for d in range(4):
        for dy, device in ((1, up), (3, down)):
            ky[dy, d] = remote(
                kv.at[d * 8],
                kv.at[d * 8 + dy],
                ky_send.at[d * 4 + dy],
                ky_recv.at[d * 4 + dy],
                device,
            )
        for part, dy, device in ((0, 1, up), (1, 3, down)):
            some = pl.ds(400 * part, 400 - 16 * part)
            ky["up" if part == 0 else "down", d] = remote(
                kv.at[d * 8 + dy, some],
                kv.at[d * 8 + 2, some],
                ky_send.at[d * 4 + 2 * part],
                ky_recv.at[d * 4 + 2 * part],
                device,
            )
    kc = {
        (dy, d): remote(
            kv.at[d * 8 + dy],
            kv.at[d * 8 + 4 + dy],
            kc_send.at[d * 4 + dy],
            kc_recv.at[d * 4 + dy],
            sibling,
        )
        for d in range(4)
        for dy in range(4)
    }

    def begin_y(d):
        ky[1, d].start()
        ky[3, d].start()
        kc[0, d].start()

    def pass_on(d):
        ky[1, d].wait_recv()
        ky["up", d].start()
        kc[1, d].start()
        ky[3, d].wait_recv()
        ky["down", d].start()
        kc[3, d].start()

    def last(d):
        ky["up", d].wait_recv()
        ky["down", d].wait_recv()
        kc[2, d].start()

    kz[1].start()
    begin_y(0)
    meanwhile()

    for h in range(8):
        part = query[:, h * HD : (h + 1) * HD].astype(jnp.float32).T.astype(jnp.bfloat16)
        queries[h // 2, :, (h % 2) * 128 : (h % 2 + 1) * 128] = part
    top[...] = jnp.full_like(top, -1e30)
    acc[...] = jnp.zeros_like(acc)
    factor = 1.4426950408889634 / HD**0.5

    def attend(blocks):
        for b in range(4):
            digits = kv[blocks[b], 768:784].astype(jnp.float32)
            place_of = digits[0:1] * 64.0 + digits[1:2]
            column = jnp.broadcast_to(place_of, (128, 128)).T
            seen = column <= own_pos.astype(jnp.float32)
            bias[b] = jnp.where(seen, 0.0, -1e30)

        @pl.loop(0, 4, unroll=4)
        def _(t):
            part = queries[t]
            pieces = []
            for b in range(4):
                scores = jnp.dot(kv[blocks[b], 0:384], part, preferred_element_type=jnp.float32)
                wide = jnp.concatenate([bias[b], bias[b]], 1)
                pieces += [scores[:256], scores[256:] + wide]
            old_top = top[t, 0:1]
            new_top = old_top
            for piece in pieces:
                new_top = jnp.maximum(new_top, jnp.max(piece, 0, keepdims=True))
            probs = jnp.concatenate(
                [jnp.exp2((piece - new_top) * factor).astype(jnp.bfloat16) for piece in pieces], 0
            )
            values = jnp.concatenate(
                [
                    kv[blocks[b], 384 + 128 * i : 512 + 128 * i]
                    for b in range(4)
                    for i in range(3)
                ],
                1,
            )
            ones = jnp.ones((16, values.shape[1]), jnp.bfloat16)
            added = jnp.dot(
                jnp.concatenate([values, ones], 0), probs, preferred_element_type=jnp.float32
            )
            acc[t] = acc[t] * jnp.exp2((old_top - new_top) * factor) + added
            top[t] = jnp.broadcast_to(new_top, (8, 256))

    def attend_near(d):
        kc[0, d].wait_recv()
        attend([d * 8 + b for b in (0, 4, 1, 3)])

    def attend_far(d):
        for dy in (1, 3, 2):
            kc[dy, d].wait_recv()
        attend([d * 8 + b for b in (5, 7, 2, 6)])

    kz[1].wait_recv()
    kz[2].start()
    begin_y(1)
    pass_on(0)
    attend_near(0)
    kz[2].wait_recv()
    kz[3].start()
    begin_y(2)
    for d in (1, 3):
        wz[d].start()
    last(0)
    pass_on(1)
    attend_far(0)
    kz[3].wait_recv()
    begin_y(3)
    wz[2].start()
    attend_near(1)
    last(1)
    pass_on(2)
    attend_far(1)
    attend_near(2)
    last(2)
    pass_on(3)
    attend_far(2)
    attend_near(3)
    last(3)
    attend_far(3)

    for h in range(8):
        part = slice((h % 2) * 128, (h % 2 + 1) * 128)
        scaled = acc[h // 2, 0:128, part] / acc[h // 2, 128:129, part]
        attended[0, :, h * HD : (h + 1) * HD] = scaled.T.astype(jnp.bfloat16)

    def half_of(slot, k):
        return attended.at[slot, pl.ds(k * 64, 64)]

    ay = {
        1: remote(attended.at[0], attended.at[1], ay_send.at[0], ay_recv.at[0], up),
        3: remote(attended.at[0], attended.at[3], ay_send.at[1], ay_recv.at[1], down),
        "up": remote(half_of(1, 0), half_of(2, 0), ay_send.at[2], ay_recv.at[2], up),
        "down": remote(half_of(3, 1), half_of(2, 1), ay_send.at[3], ay_recv.at[3], down),
    }
    ac = [
        remote(attended.at[s], attended.at[4 + s], ac_send.at[s], ac_recv.at[s], sibling)
        for s in range(4)
    ]
    ay[1].start()
    ay[3].start()
    ac[0].start()
    for d in range(1, 4):
        wz[d].wait_recv()

    def project(s):
        for pair in range(2):
            both = jnp.concatenate([weight[2 * pair], weight[2 * pair + 1]], 1)
            result = jnp.dot(attended[s], both, preferred_element_type=jnp.float32)
            projected[:, ORDER.index(s), :, pair * 256 : (pair + 1) * 256] = result.astype(
                jnp.bfloat16
            ).reshape(8, 16, 256)

    x_copy = [
        None
        if d == 0
        else remote(
            projected.at[other(d), pl.ds(half * 4, 4)],
            from_exp.at[d, pl.ds(half * 4, 4)],
            x_send.at[half * 8 + d],
            x_recv.at[half * 8 + d],
            (ctx, other(d)),
        )
        for half in range(2)
        for d in range(8)
    ]
    p_copy = [None] + [
        remote(summed.at[s], pieces.at[s], p_send.at[s], p_recv.at[s], behind(s))
        for s in range(1, 8)
    ]

    project(0)
    ac[0].wait_recv()
    project(4)
    ay[1].wait_recv()
    ay["up"].start()
    ac[1].start()
    ay[3].wait_recv()
    ay["down"].start()
    ac[3].start()
    project(1)
    project(3)
    for d in range(1, 8):
        x_copy[d].start()
    ac[1].wait_recv()
    project(5)
    ac[3].wait_recv()
    project(7)
    ay["up"].wait_recv()
    ay["down"].wait_recv()
    ac[2].start()
    project(2)
    ac[2].wait_recv()
    project(6)
    for d in range(1, 8):
        x_copy[8 + d].start()

    for half in range(2):
        for d in range(1, 8):
            x_copy[half * 8 + d].wait_recv()
        for k in range(half * 4, half * 4 + 4):
            s = ORDER[k]
            total = projected[e, k].astype(jnp.float32)
            for d in range(1, 8):
                total += from_exp[d, k].astype(jnp.float32)
            if s == 0:
                pieces[0] = total
            else:
                summed[s] = total
                p_copy[s].start()
    for s in ORDER:
        if s > 0:
            p_copy[s].wait_recv()
        sender = lax.rem(y + s % 4, 4) * 2 + (core if s < 4 else 1 - core)
        for d in range(4):
            owner = lax.rem(hi + 4 - d, 4) * 8 + sender
            gathered[:, pl.ds(pl.multiple_of(owner * 128, 128), 128)] = pieces[
                s, :, d * 128 : (d + 1) * 128
            ]

    def rows_of(index):
        return pl.ds(pl.multiple_of(index * 16, 16), 16)

    residual = hidden[...].astype(jnp.float32) + gathered[...]
    residual_own[...] = residual
    mean = jnp.sum(residual * residual, 1, keepdims=True) * (1.0 / model)
    own = (residual * lax.rsqrt(mean + 1e-06) * norm_gain[...]).astype(jnp.bfloat16)
    own_normed[...] = own
    n_copy = [None] + [
        remote(own_normed, normed.at[rows_of(e)], n_send.at[d], n_recv.at[d], (ctx, other(d)))
        for d in range(1, 8)
    ]
    for d in range(1, 8):
        n_copy[d].start()
    normed[rows_of(e), :] = own
    for d in range(1, 8):
        n_copy[d].wait_recv()

    for d in range(1, 4):
        kz[d].wait_send()
        wz[d].wait_send()
    for d in range(4):
        for dy in range(4):
            kc[dy, d].wait_send()
        for step in (1, 3, "up", "down"):
            ky[step, d].wait_send()
        ac[d].wait_send()
    for copy in ay.values():
        copy.wait_send()
    for d in range(1, 8):
        x_copy[d].wait_send()
        x_copy[8 + d].wait_send()
        p_copy[d].wait_send()
        n_copy[d].wait_send()


def tables(ids, gates, pick, pick_rest, mix_hi, mix_lo):
    hi, y, core, e = place()
    chosen = ids[...]
    weights = gates[...]
    members, factors = [], []
    for i in range(8):
        expert = e * 8 + lax.rem(hi + i // 2, 4) * 2 + lax.rem(y // 2 + i, 2)
        hit = chosen == expert
        members.append(jnp.max(jnp.where(hit, 1.0, 0.0), 0, keepdims=True))
        factors.append(jnp.sum(jnp.where(hit, weights, 0.0), 0, keepdims=True))
    member = jnp.concatenate(members, 0)
    row = lax.broadcasted_iota(jnp.int32, (128, 128), 0)
    column = lax.broadcasted_iota(jnp.int32, (128, 128), 1)
    before = jnp.where(row < column, 1.0, 0.0).astype(jnp.bfloat16)
    rank = jnp.dot(member.astype(jnp.bfloat16), before, preferred_element_type=jnp.float32)
    slot = jnp.where(member > 0.5, rank, -1.0)
    slots = jnp.concatenate([jnp.broadcast_to(slot[i : i + 1], (16, 128)) for i in range(8)], 0)
    factor = jnp.concatenate([jnp.broadcast_to(f, (16, 128)) for f in factors], 0)
    r = row & 15
    for m in range(5):
        if m < 4:
            wanted = jnp.where(r >> 2 == m, 16 + (r & 3), -2)
        else:
            wanted = r
        found = slots == wanted.astype(jnp.float32)
        ones = jnp.where(found, 1.0, 0.0).astype(jnp.bfloat16)
        mix = jnp.where(found, factor, 0.0).T
        high = mix.astype(jnp.bfloat16)
        low = (mix - high.astype(jnp.float32)).astype(jnp.bfloat16)
        if m < 4:
            pick_rest[:, m * 128 : (m + 1) * 128] = ones
            mix_hi[m, :, 128:256] = high
            mix_lo[m, :, 128:256] = low
        else:
            pick[...] = ones
            for q in range(4):
                mix_hi[q, :, 0:128] = high
                mix_lo[q, :, 0:128] = low


def moe(
    normed,
    residual_own,
    out_ref,
    loads,
    w_in,
    w_out,
    pick,
    pick_rest,
    mix_hi,
    mix_lo,
    sent,
    got,
    both,
    rest_in,
    act,
    rest_out,
    part,
    from_core,
    to_pair,
    from_pair,
    to_home,
    home,
    mixed,
    from_exp,
    d_send,
    d_recv,
    f_send,
    f_recv,
    c_send,
    c_recv,
    rc_send,
    rc_recv,
    rf_send,
    rf_recv,
    rd_send,
    rd_recv,
    x_send,
    x_recv,
):
    hi, y, core, e = place()
    width = sent.shape[-1]
    sibling = (ctx_of(hi, y, 1 - core), e)
    pair = (ctx_of(hi, y + 1 - 2 * lax.rem(y, 2), core), e)

    def slot(i, group):
        chunk = [i in blocks for blocks in CHUNKS].index(True)
        blocks = CHUNKS[chunk]
        return 4 * sum(map(len, CHUNKS[:chunk])) + group * len(blocks) + blocks.index(i)

    def back(i):
        return (ctx_of(hi + 4 - i // 2, y if i % 2 == 0 else 3 - y, core), e)

    def other(d):
        return lax.rem(e + d, 8)

    for m in range(4):
        rows = jnp.dot(
            pick[...], normed[:, m * width : (m + 1) * width], preferred_element_type=jnp.float32
        )
        sent[:, m] = rows.astype(jnp.bfloat16).reshape(8, 16, width)
    rest = jnp.zeros((128, width), jnp.float32)
    for m in range(4):
        rest += jnp.dot(
            pick_rest[:, m * 128 : (m + 1) * 128],
            normed[:, m * width : (m + 1) * width],
            preferred_element_type=jnp.float32,
        )
    sent[:, 4] = rest.astype(jnp.bfloat16).reshape(8, 16, width)
    got[slot(0, 0)] = sent[0]

    d_copy = [
        None if i == 0 else remote(
            sent.at[i], got.at[slot(i, 0)], d_send.at[i], d_recv.at[i], across(i)
        )
        for i in range(8)
    ]
    f_copy = [
        remote(got.at[slot(i, 0)], got.at[slot(i, 2)], f_send.at[i], f_recv.at[i], pair)
        for i in range(8)
    ]
    c_copy = [
        remote(got.at[slot(i, g)], got.at[slot(i, g + 1)], c_send.at[k], c_recv.at[k], sibling)
        for k, (g, i) in enumerate((g, i) for g in (0, 2) for i in range(8))
    ]
    rc_copy = [
        remote(part.at[slot(i, g)], from_core.at[k], rc_send.at[k], rc_recv.at[k], sibling)
        for k, (g, i) in enumerate((g, i) for g in (1, 3) for i in range(8))
    ]
    rf_copy = [
        remote(to_pair.at[i], from_pair.at[i], rf_send.at[i], rf_recv.at[i], pair)
        for i in range(8)
    ]
    rd_copy = [
        None if i == 0 else remote(to_home.at[i], home.at[i], rd_send.at[i], rd_recv.at[i], back(i))
        for i in range(8)
    ]
    def regroup(m, rows, columns):
        row = lax.broadcasted_iota(jnp.int32, (rows, columns), 0)
        column = lax.broadcasted_iota(jnp.int32, (rows, columns), 1)
        small, large = (row, column) if rows < columns else (column, row)
        return (large == (small // 4) * 16 + m * 4 + small % 4).astype(jnp.bfloat16)

    def experts(base, count):
        tall, low = count * 16, count * 4
        rest_rows = got[base : base + count, 4].reshape(tall, width)
        for m in range(4):
            rest_in[:low, m * width : (m + 1) * width] = jnp.dot(
                regroup(m, low, tall), rest_rows, preferred_element_type=jnp.float32
            ).astype(jnp.bfloat16)

        @pl.loop(0, 3)
        def _(n):
            columns = pl.ds(pl.multiple_of(n * 256, 256), 256)
            total = jnp.zeros((tall + low, 256), jnp.float32)
            for m in range(4):
                rows = jnp.concatenate(
                    [
                        got[base : base + count, m].reshape(tall, width),
                        rest_in[:low, m * width : (m + 1) * width],
                    ],
                    0,
                )
                total += jnp.dot(
                    rows,
                    w_in[m * width : (m + 1) * width, columns],
                    preferred_element_type=jnp.float32,
                )
            both[: tall + low, columns] = total

        gate = both[: tall + low, :FFQ]
        act[: tall + low] = (gate / (1.0 + jnp.exp(-gate)) * both[: tall + low, FFQ:]).astype(
            jnp.bfloat16
        )
        steps = width // 256

        @pl.loop(0, 4 * steps)
        def _(n):
            columns = pl.ds(pl.multiple_of(n * 256, 256), 256)
            inner = pl.ds(pl.multiple_of((n % steps) * 256, 256), 256)
            result = jnp.dot(
                act[: tall + low], w_out[:, columns], preferred_element_type=jnp.float32
            ).astype(jnp.bfloat16)
            part[base : base + count, n // steps, :, inner] = result[:tall].reshape(count, 16, 256)
            rest_out[:low, columns] = result[tall:]

        rest_part = jnp.zeros((tall, width), jnp.float32)
        for m in range(4):
            rest_part += jnp.dot(
                regroup(m, tall, low),
                rest_out[:low, m * width : (m + 1) * width],
                preferred_element_type=jnp.float32,
            )
        part[base : base + count, 4] = rest_part.astype(jnp.bfloat16).reshape(count, 16, width)

    loaded = False
    for step, i in ((step, i) for step, *blocks in SCHEDULE for i in blocks):
        if step == "send":
            d_copy[i].start()
        elif step == "sent":
            d_copy[i].wait_send()
        elif step == "pass":
            if i > 0:
                d_copy[i].wait_recv()
            f_copy[i].start()
            c_copy[i].start()
        elif step == "core":
            f_copy[i].wait_recv()
            c_copy[8 + i].start()
        elif step == "work":
            if not loaded:
                for load in loads:
                    load.wait()
                loaded = True
            for block in CHUNKS[i]:
                c_copy[block].wait_recv()
                c_copy[8 + block].wait_recv()
            experts(slot(CHUNKS[i][0], 0), 4 * len(CHUNKS[i]))
            for block in CHUNKS[i]:
                rc_copy[8 + block].start()
            for block in CHUNKS[i]:
                rc_copy[block].start()
        elif step == "back":
            rc_copy[8 + i].wait_recv()
            to_pair[i] = (
                part[slot(i, 2)].astype(jnp.float32) + from_core[8 + i].astype(jnp.float32)
            ).astype(jnp.bfloat16)
            rf_copy[i].start()
        elif step == "home":
            rc_copy[i].wait_recv()
            rf_copy[i].wait_recv()
            total = (
                part[slot(i, 0)].astype(jnp.float32)
                + from_core[i].astype(jnp.float32)
                + from_pair[i].astype(jnp.float32)
            ).astype(jnp.bfloat16)
            if i == 0:
                home[0] = total
            else:
                to_home[i] = total
                rd_copy[i].start()
    for i in ARRIVE:
        rd_copy[i].wait_recv()

    own = pl.ds(pl.multiple_of(e * 16, 16), 16)
    x_copy = []
    for m in range(4):
        rows = jnp.concatenate(
            [home[:, m].reshape(128, width), home[:, 4].reshape(128, width)], 0
        )
        mixed[m] = (
            jnp.dot(mix_hi[m], rows, preferred_element_type=jnp.float32)
            + jnp.dot(mix_lo[m], rows, preferred_element_type=jnp.float32)
        ).astype(jnp.bfloat16)
        for d in range(1, 8):
            theirs = pl.ds(pl.multiple_of(other(d) * 16, 16), 16)
            copy = remote(
                mixed.at[m, theirs],
                from_exp.at[d, m],
                x_send.at[m * 8 + d],
                x_recv.at[m * 8 + d],
                (lax.axis_index("ctx"), other(d)),
            )
            copy.start()
            x_copy.append(copy)
    for m in range(4):
        columns = slice(m * width, (m + 1) * width)
        total = residual_own[:, columns] + mixed[m, own, :].astype(jnp.float32)
        for d in range(1, 8):
            x_copy[m * 7 + d - 1].wait_recv()
            total += from_exp[d, m].astype(jnp.float32)
        out_ref[:, columns] = total.astype(jnp.bfloat16)

    for copy in x_copy:
        copy.wait_send()
    for i in range(8):
        if i > 0:
            rd_copy[i].wait_send()
            if not any(step == "sent" and i in blocks for step, *blocks in SCHEDULE):
                d_copy[i].wait_send()
        rf_copy[i].wait_send()
        f_copy[i].wait_send()
    for i in range(16):
        c_copy[i].wait_send()
        rc_copy[i].wait_send()


def kernel(*refs):
    inputs, (ids, gates, w_in_hbm, w_out_hbm, out_ref), rest = refs[:7], refs[7:12], refs[12:]
    first, (w_in, w_out, w_sem), second = rest[:ATTENTION], rest[ATTENTION:][:3], rest[ATTENTION:][3:]
    loads = [
        pltpu.make_async_copy(w_in_hbm, w_in, w_sem.at[0]),
        pltpu.make_async_copy(w_out_hbm, w_out, w_sem.at[1]),
    ]

    def meanwhile():
        for load in loads:
            load.start()
        tables(ids, gates, *second[:4])

    attention(*inputs, meanwhile, *first)
    moe(first[NORMED], first[NORMED + 1], out_ref, loads, w_in, w_out, *second)


def layer(
    query,
    new_kv,
    old_kv,
    new_pos,
    o_weight,
    hidden,
    norm_gain,
    expert_ids,
    gate_weights,
    w_in,
    w_out,
):
    rows = query.shape[0]
    model = hidden.shape[1]
    width = model // 4
    block = (5, 16, width)
    half = jnp.bfloat16
    vmem = pl.BlockSpec(memory_space=pltpu.VMEM)

    def dma(*counts):
        return [pltpu.SemaphoreType.DMA((count,)) for count in counts for _ in range(2)]

    first = [
        pltpu.VMEM((32, 784, HD), half),
        pltpu.VMEM((4,) + o_weight.shape, half),
        pltpu.VMEM((4, HD, 256), half),
        pltpu.VMEM((4, 128, 128), jnp.float32),
        pltpu.VMEM((4, 8, 256), jnp.float32),
        pltpu.VMEM((4, 144, 256), jnp.float32),
        pltpu.VMEM((8,) + query.shape, half),
        pltpu.VMEM((8, 8, 16, 512), half),
        pltpu.VMEM((8, 8, 16, 512), half),
        pltpu.VMEM((8, 16, 512), jnp.float32),
        pltpu.VMEM((8, 16, 512), jnp.float32),
        pltpu.VMEM(hidden.shape, jnp.float32),
        pltpu.VMEM(hidden.shape, half),
        pltpu.VMEM((rows, model), half),
        pltpu.VMEM(hidden.shape, jnp.float32),
    ] + dma(4, 16, 16, 4, 4, 4, 16, 8, 8)
    assert len(first) == ATTENTION
    loaded = [
        pltpu.VMEM(w_in.shape, half),
        pltpu.VMEM(w_out.shape, half),
        pltpu.SemaphoreType.DMA((2,)),
    ]
    second = [
        pltpu.VMEM((128, 128), half),
        pltpu.VMEM((128, 512), half),
        pltpu.VMEM((4, 128, 256), half),
        pltpu.VMEM((4, 128, 256), half),
        pltpu.VMEM((8,) + block, half),
        pltpu.VMEM((32,) + block, half),
        pltpu.VMEM((160, 2 * FFQ), jnp.float32),
        pltpu.VMEM((32, model), half),
        pltpu.VMEM((160, FFQ), half),
        pltpu.VMEM((32, model), half),
        pltpu.VMEM((32,) + block, half),
        pltpu.VMEM((16,) + block, half),
        pltpu.VMEM((8,) + block, half),
        pltpu.VMEM((8,) + block, half),
        pltpu.VMEM((8,) + block, half),
        pltpu.VMEM((8,) + block, half),
        pltpu.VMEM((4, 128, width), half),
        pltpu.VMEM((8, 4, 16, width), half),
    ] + dma(8, 8, 16, 16, 8, 8, 32)
    return pl.pallas_call(
        kernel,
        out_shape=jax.ShapeDtypeStruct(hidden.shape, half),
        in_specs=[vmem] * 9 + [pl.BlockSpec(memory_space=pl.ANY)] * 2,
        out_specs=vmem,
        scratch_shapes=first + loaded + second,
        compiler_params=pltpu.CompilerParams(
            collective_id=1, has_side_effects=True, vmem_limit_bytes=58 * 2**20
        ),
        name="layer",
    )(
        query,
        new_kv,
        old_kv,
        new_pos.reshape(1, rows),
        o_weight,
        hidden,
        norm_gain.reshape(1, model),
        expert_ids.T,
        gate_weights.T,
        w_in,
        w_out,
    )


def per_device(
    query,
    new_kv,
    old_kv,
    new_pos,
    o_weight,
    hidden,
    norm_gain,
    expert_ids,
    gate_weights,
    w_in,
    w_out,
):
    return layer(
        query,
        new_kv,
        old_kv,
        new_pos,
        o_weight,
        hidden,
        norm_gain,
        expert_ids,
        gate_weights,
        w_in[0, 0],
        w_out[0, 0],
    )


def solution(mesh):
    return jax.shard_map(
        per_device,
        mesh=mesh,
        in_specs=(
            P("ctx", "exp"),
            P(None, "ctx", None),
            P(None, "ctx", None),
            P("ctx"),
            P("exp", "ctx"),
            P(("ctx", "exp"), None),
            P(),
            P("ctx", None),
            P("ctx", None),
            P("ctx", "exp", None, None),
            P("ctx", "exp", None, None),
        ),
        out_specs=P(("ctx", "exp"), None),
        check_vma=False,
    )
```

```python
import jax
import jax.numpy as jnp
from jax import lax
from jax.experimental import pallas as pl
from jax.experimental.pallas import tpu as pltpu
from jax.sharding import PartitionSpec as P

HD = 128
FFQ = 384
MESH = pl.DeviceIdType.MESH
ARRIVE = (1, 2, 6, 3, 7, 4, 5)
ATTENTION = 33
NORMED = 13
ORDER = (0, 4, 1, 3, 5, 7, 2, 6)


CHUNKS = ((0, 1), (2, 6), (3, 7), (4,), (5,))
SCHEDULE = (
    ("send", 2, 6, 1),
    ("pass", 0, 1),
    ("sent", 2),
    ("send", 3),
    ("sent", 6),
    ("send", 7),
    ("pass", 2, 6),
    ("core", 0, 1),
    ("work", 0),
    ("sent", 3, 7),
    ("send", 4),
    ("pass", 3, 7),
    ("core", 2, 6),
    ("work", 1),
    ("sent", 4),
    ("send", 5),
    ("pass", 4),
    ("back", 2, 6),
    ("core", 3, 7),
    ("work", 2),
    ("core", 4),
    ("back", 3, 7),
    ("work", 3),
    ("pass", 5),
    ("home", 2, 6),
    ("back", 4),
    ("core", 5),
    ("home", 3, 7),
    ("work", 4),
    ("home", 4),
    ("back", 5, 1, 0),
    ("home", 5, 1, 0),
)


def place():
    ctx = lax.axis_index("ctx")
    return ctx // 8, (ctx // 2) % 4, ctx % 2, lax.axis_index("exp")


def ctx_of(hi, y, core):
    return lax.rem(hi, 4) * 8 + y * 2 + core


def across(i):
    hi, y, core, e = place()
    return (ctx_of(hi + i // 2, y if i % 2 == 0 else 3 - y, core), e)


def remote(src, dst, send, recv, device):
    return pltpu.make_async_remote_copy(
        src_ref=src, dst_ref=dst, send_sem=send, recv_sem=recv, device_id=device, device_id_type=MESH
    )


def attention(
    query,
    new_kv,
    old_kv,
    new_pos,
    o_weight,
    hidden,
    norm_gain,
    meanwhile,
    kv,
    weight,
    queries,
    bias,
    top,
    acc,
    attended,
    projected,
    from_exp,
    summed,
    pieces,
    gathered,
    own_normed,
    normed,
    residual_own,
    kz_send,
    kz_recv,
    ky_send,
    ky_recv,
    kc_send,
    kc_recv,
    wz_send,
    wz_recv,
    ay_send,
    ay_recv,
    ac_send,
    ac_recv,
    x_send,
    x_recv,
    p_send,
    p_recv,
    n_send,
    n_recv,
):
    hi, y, core, e = place()
    ctx = lax.axis_index("ctx")
    model = hidden.shape[1]
    sibling = (ctx_of(hi, y, 1 - core), e)
    up = (ctx_of(hi, lax.rem(y + 1, 4), core), e)
    down = (ctx_of(hi, lax.rem(y + 3, 4), core), e)

    def along(d):
        return (ctx_of(hi + d, y, core), e)

    parity = lax.rem(e, 2)
    outer = (ctx_of(hi + 3 + 2 * parity, y, core), e + 1 - 2 * parity)
    inner = (ctx, e + 1 - 2 * parity)

    def behind(s):
        return (ctx_of(hi, lax.rem(y + 4 - s % 4, 4), core if s < 4 else 1 - core), e)

    def other(d):
        return lax.rem(e + d, 8)

    barrier = pltpu.get_barrier_semaphore()
    for d in range(1, 4):
        pl.semaphore_signal(barrier, inc=1, device_id=along(d), device_id_type=MESH)
        pl.semaphore_signal(
            barrier, inc=1, device_id=across(2 * d + 1), device_id_type=MESH
        )
    pl.semaphore_signal(barrier, inc=1, device_id=outer, device_id_type=MESH)
    for s in range(1, 8):
        pl.semaphore_signal(barrier, inc=1, device_id=behind(s), device_id_type=MESH)
    for d in range(1, 8):
        pl.semaphore_signal(barrier, inc=1, device_id=(ctx, other(d)), device_id_type=MESH)

    lanes = pl.ds(pl.multiple_of((e // 2) * HD, HD), HD)
    kv[0, 0:256] = old_kv[0, :, lanes]
    kv[0, 256:384] = new_kv[0, :, lanes]
    for b in range(3):
        values = new_kv[1, :, lanes] if b == 2 else old_kv[1, b * 128 : (b + 1) * 128, lanes]
        kv[0, 384 + b * 128 : 512 + b * 128] = values.astype(jnp.float32).T.astype(jnp.bfloat16)
    own_pos = new_pos[...]
    row = lax.broadcasted_iota(jnp.int32, (16, 128), 0)
    kv[0, 768:784] = (
        jnp.where(row == 0, own_pos >> 6, jnp.where(row == 1, own_pos & 63, 0))
        .astype(jnp.float32)
        .astype(jnp.bfloat16)
    )
    weight[0] = o_weight[...]

    pl.semaphore_wait(barrier, 21)

    kz = [None] + [
        remote(kv.at[d * 8 - 8], kv.at[d * 8], kz_send.at[d], kz_recv.at[d], device)
        for d, device in ((1, outer), (2, inner), (3, outer))
    ]
    wz = [None] + [
        remote(weight.at[0], weight.at[d], wz_send.at[d], wz_recv.at[d], along(d))
        for d in range(1, 4)
    ]
    ky = {}
    for d in range(4):
        for dy, device in ((1, up), (3, down)):
            ky[dy, d] = remote(
                kv.at[d * 8],
                kv.at[d * 8 + dy],
                ky_send.at[d * 4 + dy],
                ky_recv.at[d * 4 + dy],
                device,
            )
        for part, dy, device in ((0, 1, up), (1, 3, down)):
            some = pl.ds(400 * part, 400 - 16 * part)
            ky["up" if part == 0 else "down", d] = remote(
                kv.at[d * 8 + dy, some],
                kv.at[d * 8 + 2, some],
                ky_send.at[d * 4 + 2 * part],
                ky_recv.at[d * 4 + 2 * part],
                device,
            )
    kc = {
        (dy, d): remote(
            kv.at[d * 8 + dy],
            kv.at[d * 8 + 4 + dy],
            kc_send.at[d * 4 + dy],
            kc_recv.at[d * 4 + dy],
            sibling,
        )
        for d in range(4)
        for dy in range(4)
    }

    def begin_y(d):
        ky[1, d].start()
        ky[3, d].start()
        kc[0, d].start()

    def pass_on(d):
        ky[1, d].wait_recv()
        ky["up", d].start()
        kc[1, d].start()
        ky[3, d].wait_recv()
        ky["down", d].start()
        kc[3, d].start()

    def last(d):
        ky["up", d].wait_recv()
        ky["down", d].wait_recv()
        kc[2, d].start()

    kz[1].start()
    begin_y(0)
    meanwhile()

    for h in range(8):
        part = query[:, h * HD : (h + 1) * HD].astype(jnp.float32).T.astype(jnp.bfloat16)
        queries[h // 2, :, (h % 2) * 128 : (h % 2 + 1) * 128] = part
    top[...] = jnp.full_like(top, -1e30)
    acc[...] = jnp.zeros_like(acc)
    factor = 1.4426950408889634 / HD**0.5

    def attend(blocks):
        for b in range(len(blocks)):
            digits = kv[blocks[b], 768:784].astype(jnp.float32)
            place_of = digits[0:1] * 64.0 + digits[1:2]
            column = jnp.broadcast_to(place_of, (128, 128)).T
            seen = column <= own_pos.astype(jnp.float32)
            bias[b] = jnp.where(seen, 0.0, -1e30)

        @pl.loop(0, 4, unroll=4)
        def _(t):
            part = queries[t]
            pieces = []
            for b in range(len(blocks)):
                scores = jnp.dot(kv[blocks[b], 0:384], part, preferred_element_type=jnp.float32)
                wide = jnp.concatenate([bias[b], bias[b]], 1)
                pieces += [scores[:256], scores[256:] + wide]
            old_top = top[t, 0:1]
            new_top = old_top
            for piece in pieces:
                new_top = jnp.maximum(new_top, jnp.max(piece, 0, keepdims=True))
            probs = jnp.concatenate(
                [jnp.exp2((piece - new_top) * factor).astype(jnp.bfloat16) for piece in pieces], 0
            )
            values = jnp.concatenate(
                [
                    kv[blocks[b], 384 + 128 * i : 512 + 128 * i]
                    for b in range(len(blocks))
                    for i in range(3)
                ],
                1,
            )
            ones = jnp.ones((16, values.shape[1]), jnp.bfloat16)
            added = jnp.dot(
                jnp.concatenate([values, ones], 0), probs, preferred_element_type=jnp.float32
            )
            acc[t] = acc[t] * jnp.exp2((old_top - new_top) * factor) + added
            top[t] = jnp.broadcast_to(new_top, (8, 256))

    def attend_near(d):
        kc[0, d].wait_recv()
        attend([d * 8 + b for b in (0, 4, 1, 3)])

    def attend_far(d):
        for dy in (1, 3, 2):
            kc[dy, d].wait_recv()
        attend([d * 8 + b for b in (5, 7, 2, 6)])

    kz[1].wait_recv()
    kz[2].start()
    begin_y(1)
    pass_on(0)
    attend_near(0)
    kz[2].wait_recv()
    kz[3].start()
    begin_y(2)
    for d in (1, 3):
        wz[d].start()
    last(0)
    pass_on(1)
    attend_far(0)
    kz[3].wait_recv()
    begin_y(3)
    wz[2].start()
    attend_near(1)
    last(1)
    pass_on(2)
    attend_far(1)
    attend_near(2)
    last(2)
    pass_on(3)
    attend_far(2)
    attend_near(3)
    last(3)
    kc[1, 3].wait_recv()
    kc[3, 3].wait_recv()
    attend([29, 31])
    kc[2, 3].wait_recv()
    attend([26, 30])

    for h in range(8):
        part = slice((h % 2) * 128, (h % 2 + 1) * 128)
        scaled = acc[h // 2, 0:128, part] / acc[h // 2, 128:129, part]
        attended[0, :, h * HD : (h + 1) * HD] = scaled.T.astype(jnp.bfloat16)

    def half_of(slot, k):
        return attended.at[slot, pl.ds(k * 64, 64)]

    ay = {
        1: remote(attended.at[0], attended.at[1], ay_send.at[0], ay_recv.at[0], up),
        3: remote(attended.at[0], attended.at[3], ay_send.at[1], ay_recv.at[1], down),
        "up": remote(half_of(1, 0), half_of(2, 0), ay_send.at[2], ay_recv.at[2], up),
        "down": remote(half_of(3, 1), half_of(2, 1), ay_send.at[3], ay_recv.at[3], down),
    }
    ac = [
        remote(attended.at[s], attended.at[4 + s], ac_send.at[s], ac_recv.at[s], sibling)
        for s in range(4)
    ]
    ay[1].start()
    ay[3].start()
    ac[0].start()
    for d in range(1, 4):
        wz[d].wait_recv()

    def project(s):
        for pair in range(2):
            both = jnp.concatenate([weight[2 * pair], weight[2 * pair + 1]], 1)
            result = jnp.dot(attended[s], both, preferred_element_type=jnp.float32)
            projected[:, ORDER.index(s), :, pair * 256 : (pair + 1) * 256] = result.astype(
                jnp.bfloat16
            ).reshape(8, 16, 256)

    x_copy = [
        None
        if d == 0
        else remote(
            projected.at[other(d), pl.ds(pair * 2, 2)],
            from_exp.at[d, pl.ds(pair * 2, 2)],
            x_send.at[pair * 8 + d],
            x_recv.at[pair * 8 + d],
            (ctx, other(d)),
        )
        for pair in range(4)
        for d in range(8)
    ]

    def begin_x(pair):
        for d in range(1, 8):
            x_copy[pair * 8 + d].start()

    p_copy = [None] + [
        remote(summed.at[s], pieces.at[s], p_send.at[s], p_recv.at[s], behind(s))
        for s in range(1, 8)
    ]

    project(0)
    ac[0].wait_recv()
    project(4)
    begin_x(0)
    ay[1].wait_recv()
    ay["up"].start()
    ac[1].start()
    ay[3].wait_recv()
    ay["down"].start()
    ac[3].start()
    project(1)
    project(3)
    begin_x(1)
    ac[1].wait_recv()
    project(5)
    ac[3].wait_recv()
    project(7)
    begin_x(2)
    ay["up"].wait_recv()
    ay["down"].wait_recv()
    ac[2].start()
    project(2)
    ac[2].wait_recv()
    project(6)
    begin_x(3)

    for pair in range(4):
        for d in range(1, 8):
            x_copy[pair * 8 + d].wait_recv()
        for k in range(pair * 2, pair * 2 + 2):
            s = ORDER[k]
            total = projected[e, k].astype(jnp.float32)
            for d in range(1, 8):
                total += from_exp[d, k].astype(jnp.float32)
            if s == 0:
                pieces[0] = total
            else:
                summed[s] = total
                p_copy[s].start()
    for s in ORDER:
        if s > 0:
            p_copy[s].wait_recv()
        sender = lax.rem(y + s % 4, 4) * 2 + (core if s < 4 else 1 - core)
        for d in range(4):
            owner = lax.rem(hi + 4 - d, 4) * 8 + sender
            gathered[:, pl.ds(pl.multiple_of(owner * 128, 128), 128)] = pieces[
                s, :, d * 128 : (d + 1) * 128
            ]

    def rows_of(index):
        return pl.ds(pl.multiple_of(index * 16, 16), 16)

    residual = hidden[...].astype(jnp.float32) + gathered[...]
    residual_own[...] = residual
    mean = jnp.sum(residual * residual, 1, keepdims=True) * (1.0 / model)
    own = (residual * lax.rsqrt(mean + 1e-06) * norm_gain[...]).astype(jnp.bfloat16)
    own_normed[...] = own
    n_copy = [None] + [
        remote(own_normed, normed.at[rows_of(e)], n_send.at[d], n_recv.at[d], (ctx, other(d)))
        for d in range(1, 8)
    ]
    for d in range(1, 8):
        n_copy[d].start()
    normed[rows_of(e), :] = own
    for d in range(1, 8):
        n_copy[d].wait_recv()

    for d in range(1, 4):
        kz[d].wait_send()
        wz[d].wait_send()
    for d in range(4):
        for dy in range(4):
            kc[dy, d].wait_send()
        for step in (1, 3, "up", "down"):
            ky[step, d].wait_send()
        ac[d].wait_send()
    for copy in ay.values():
        copy.wait_send()
    for d in range(1, 8):
        for pair in range(4):
            x_copy[pair * 8 + d].wait_send()
        p_copy[d].wait_send()
        n_copy[d].wait_send()


def tables(ids, gates, pick, pick_rest, mix_hi, mix_lo):
    hi, y, core, e = place()
    chosen = ids[...]
    weights = gates[...]
    members, factors = [], []
    for i in range(8):
        expert = e * 8 + lax.rem(hi + i // 2, 4) * 2 + lax.rem(y // 2 + i, 2)
        hit = chosen == expert
        members.append(jnp.max(jnp.where(hit, 1.0, 0.0), 0, keepdims=True))
        factors.append(jnp.sum(jnp.where(hit, weights, 0.0), 0, keepdims=True))
    member = jnp.concatenate(members, 0)
    row = lax.broadcasted_iota(jnp.int32, (128, 128), 0)
    column = lax.broadcasted_iota(jnp.int32, (128, 128), 1)
    before = jnp.where(row < column, 1.0, 0.0).astype(jnp.bfloat16)
    rank = jnp.dot(member.astype(jnp.bfloat16), before, preferred_element_type=jnp.float32)
    slot = jnp.where(member > 0.5, rank, -1.0)
    slots = jnp.concatenate([jnp.broadcast_to(slot[i : i + 1], (16, 128)) for i in range(8)], 0)
    factor = jnp.concatenate([jnp.broadcast_to(f, (16, 128)) for f in factors], 0)
    r = row & 15
    for m in range(5):
        if m < 4:
            wanted = jnp.where(r >> 2 == m, 16 + (r & 3), -2)
        else:
            wanted = r
        found = slots == wanted.astype(jnp.float32)
        ones = jnp.where(found, 1.0, 0.0).astype(jnp.bfloat16)
        mix = jnp.where(found, factor, 0.0).T
        high = mix.astype(jnp.bfloat16)
        low = (mix - high.astype(jnp.float32)).astype(jnp.bfloat16)
        if m < 4:
            pick_rest[:, m * 128 : (m + 1) * 128] = ones
            mix_hi[m, :, 128:256] = high
            mix_lo[m, :, 128:256] = low
        else:
            pick[...] = ones
            for q in range(4):
                mix_hi[q, :, 0:128] = high
                mix_lo[q, :, 0:128] = low


def moe(
    normed,
    residual_own,
    out_ref,
    loads,
    w_in,
    w_out,
    pick,
    pick_rest,
    mix_hi,
    mix_lo,
    sent,
    got,
    both,
    rest_in,
    act,
    rest_out,
    part,
    from_core,
    to_pair,
    from_pair,
    to_home,
    home,
    mixed,
    from_exp,
    d_send,
    d_recv,
    f_send,
    f_recv,
    c_send,
    c_recv,
    rc_send,
    rc_recv,
    rf_send,
    rf_recv,
    rd_send,
    rd_recv,
    x_send,
    x_recv,
):
    hi, y, core, e = place()
    width = sent.shape[-1]
    sibling = (ctx_of(hi, y, 1 - core), e)
    pair = (ctx_of(hi, y + 1 - 2 * lax.rem(y, 2), core), e)

    def slot(i, group):
        chunk = [i in blocks for blocks in CHUNKS].index(True)
        blocks = CHUNKS[chunk]
        return 4 * sum(map(len, CHUNKS[:chunk])) + group * len(blocks) + blocks.index(i)

    def back(i):
        return (ctx_of(hi + 4 - i // 2, y if i % 2 == 0 else 3 - y, core), e)

    def other(d):
        return lax.rem(e + d, 8)

    for m in range(4):
        rows = jnp.dot(
            pick[...], normed[:, m * width : (m + 1) * width], preferred_element_type=jnp.float32
        )
        sent[:, m] = rows.astype(jnp.bfloat16).reshape(8, 16, width)
    rest = jnp.zeros((128, width), jnp.float32)
    for m in range(4):
        rest += jnp.dot(
            pick_rest[:, m * 128 : (m + 1) * 128],
            normed[:, m * width : (m + 1) * width],
            preferred_element_type=jnp.float32,
        )
    sent[:, 4] = rest.astype(jnp.bfloat16).reshape(8, 16, width)
    got[slot(0, 0)] = sent[0]

    d_copy = [
        None if i == 0 else remote(
            sent.at[i], got.at[slot(i, 0)], d_send.at[i], d_recv.at[i], across(i)
        )
        for i in range(8)
    ]
    f_copy = [
        remote(got.at[slot(i, 0)], got.at[slot(i, 2)], f_send.at[i], f_recv.at[i], pair)
        for i in range(8)
    ]
    c_copy = [
        remote(got.at[slot(i, g)], got.at[slot(i, g + 1)], c_send.at[k], c_recv.at[k], sibling)
        for k, (g, i) in enumerate((g, i) for g in (0, 2) for i in range(8))
    ]
    rc_copy = [
        remote(part.at[slot(i, g)], from_core.at[k], rc_send.at[k], rc_recv.at[k], sibling)
        for k, (g, i) in enumerate((g, i) for g in (1, 3) for i in range(8))
    ]
    rf_copy = [
        remote(to_pair.at[i], from_pair.at[i], rf_send.at[i], rf_recv.at[i], pair)
        for i in range(8)
    ]
    rd_copy = [
        None if i == 0 else remote(to_home.at[i], home.at[i], rd_send.at[i], rd_recv.at[i], back(i))
        for i in range(8)
    ]
    def regroup(m, rows, columns):
        row = lax.broadcasted_iota(jnp.int32, (rows, columns), 0)
        column = lax.broadcasted_iota(jnp.int32, (rows, columns), 1)
        small, large = (row, column) if rows < columns else (column, row)
        return (large == (small // 4) * 16 + m * 4 + small % 4).astype(jnp.bfloat16)

    def experts(base, count):
        tall, low = count * 16, count * 4
        rest_rows = got[base : base + count, 4].reshape(tall, width)
        for m in range(4):
            rest_in[:low, m * width : (m + 1) * width] = jnp.dot(
                regroup(m, low, tall), rest_rows, preferred_element_type=jnp.float32
            ).astype(jnp.bfloat16)

        @pl.loop(0, 3)
        def _(n):
            columns = pl.ds(pl.multiple_of(n * 256, 256), 256)
            total = jnp.zeros((tall + low, 256), jnp.float32)
            for m in range(4):
                rows = jnp.concatenate(
                    [
                        got[base : base + count, m].reshape(tall, width),
                        rest_in[:low, m * width : (m + 1) * width],
                    ],
                    0,
                )
                total += jnp.dot(
                    rows,
                    w_in[m * width : (m + 1) * width, columns],
                    preferred_element_type=jnp.float32,
                )
            both[: tall + low, columns] = total

        gate = both[: tall + low, :FFQ]
        act[: tall + low] = (gate / (1.0 + jnp.exp(-gate)) * both[: tall + low, FFQ:]).astype(
            jnp.bfloat16
        )
        steps = width // 256

        @pl.loop(0, 4 * steps)
        def _(n):
            columns = pl.ds(pl.multiple_of(n * 256, 256), 256)
            inner = pl.ds(pl.multiple_of((n % steps) * 256, 256), 256)
            result = jnp.dot(
                act[: tall + low], w_out[:, columns], preferred_element_type=jnp.float32
            ).astype(jnp.bfloat16)
            part[base : base + count, n // steps, :, inner] = result[:tall].reshape(count, 16, 256)
            rest_out[:low, columns] = result[tall:]

        rest_part = jnp.zeros((tall, width), jnp.float32)
        for m in range(4):
            rest_part += jnp.dot(
                regroup(m, tall, low),
                rest_out[:low, m * width : (m + 1) * width],
                preferred_element_type=jnp.float32,
            )
        part[base : base + count, 4] = rest_part.astype(jnp.bfloat16).reshape(count, 16, width)

    loaded = False
    for step, i in ((step, i) for step, *blocks in SCHEDULE for i in blocks):
        if step == "send":
            d_copy[i].start()
        elif step == "sent":
            d_copy[i].wait_send()
        elif step == "pass":
            if i > 0:
                d_copy[i].wait_recv()
            f_copy[i].start()
            c_copy[i].start()
        elif step == "core":
            f_copy[i].wait_recv()
            c_copy[8 + i].start()
        elif step == "work":
            if not loaded:
                for load in loads:
                    load.wait()
                loaded = True
            for block in CHUNKS[i]:
                c_copy[block].wait_recv()
                c_copy[8 + block].wait_recv()
            experts(slot(CHUNKS[i][0], 0), 4 * len(CHUNKS[i]))
            for block in CHUNKS[i]:
                rc_copy[8 + block].start()
            for block in CHUNKS[i]:
                rc_copy[block].start()
        elif step == "back":
            rc_copy[8 + i].wait_recv()
            to_pair[i] = (
                part[slot(i, 2)].astype(jnp.float32) + from_core[8 + i].astype(jnp.float32)
            ).astype(jnp.bfloat16)
            rf_copy[i].start()
        elif step == "home":
            rc_copy[i].wait_recv()
            rf_copy[i].wait_recv()
            total = (
                part[slot(i, 0)].astype(jnp.float32)
                + from_core[i].astype(jnp.float32)
                + from_pair[i].astype(jnp.float32)
            ).astype(jnp.bfloat16)
            if i == 0:
                home[0] = total
            else:
                to_home[i] = total
                rd_copy[i].start()
    for i in ARRIVE:
        rd_copy[i].wait_recv()

    own = pl.ds(pl.multiple_of(e * 16, 16), 16)
    x_copy = []
    for m in range(4):
        rows = jnp.concatenate(
            [home[:, m].reshape(128, width), home[:, 4].reshape(128, width)], 0
        )
        mixed[m] = (
            jnp.dot(mix_hi[m], rows, preferred_element_type=jnp.float32)
            + jnp.dot(mix_lo[m], rows, preferred_element_type=jnp.float32)
        ).astype(jnp.bfloat16)
        for d in range(1, 8):
            theirs = pl.ds(pl.multiple_of(other(d) * 16, 16), 16)
            copy = remote(
                mixed.at[m, theirs],
                from_exp.at[d, m],
                x_send.at[m * 8 + d],
                x_recv.at[m * 8 + d],
                (lax.axis_index("ctx"), other(d)),
            )
            copy.start()
            x_copy.append(copy)
    for m in range(4):
        columns = slice(m * width, (m + 1) * width)
        total = residual_own[:, columns] + mixed[m, own, :].astype(jnp.float32)
        for d in range(1, 8):
            x_copy[m * 7 + d - 1].wait_recv()
            total += from_exp[d, m].astype(jnp.float32)
        out_ref[:, columns] = total.astype(jnp.bfloat16)

    for copy in x_copy:
        copy.wait_send()
    for i in range(8):
        if i > 0:
            rd_copy[i].wait_send()
            if not any(step == "sent" and i in blocks for step, *blocks in SCHEDULE):
                d_copy[i].wait_send()
        rf_copy[i].wait_send()
        f_copy[i].wait_send()
    for i in range(16):
        c_copy[i].wait_send()
        rc_copy[i].wait_send()


def kernel(*refs):
    inputs, (ids, gates, w_in_hbm, w_out_hbm, out_ref), rest = refs[:7], refs[7:12], refs[12:]
    first, (w_in, w_out, w_sem), second = rest[:ATTENTION], rest[ATTENTION:][:3], rest[ATTENTION:][3:]
    loads = [
        pltpu.make_async_copy(w_in_hbm, w_in, w_sem.at[0]),
        pltpu.make_async_copy(w_out_hbm, w_out, w_sem.at[1]),
    ]

    def meanwhile():
        for load in loads:
            load.start()
        tables(ids, gates, *second[:4])

    attention(*inputs, meanwhile, *first)
    moe(first[NORMED], first[NORMED + 1], out_ref, loads, w_in, w_out, *second)


def layer(
    query,
    new_kv,
    old_kv,
    new_pos,
    o_weight,
    hidden,
    norm_gain,
    expert_ids,
    gate_weights,
    w_in,
    w_out,
):
    rows = query.shape[0]
    model = hidden.shape[1]
    width = model // 4
    block = (5, 16, width)
    half = jnp.bfloat16
    vmem = pl.BlockSpec(memory_space=pltpu.VMEM)

    def dma(*counts):
        return [pltpu.SemaphoreType.DMA((count,)) for count in counts for _ in range(2)]

    first = [
        pltpu.VMEM((32, 784, HD), half),
        pltpu.VMEM((4,) + o_weight.shape, half),
        pltpu.VMEM((4, HD, 256), half),
        pltpu.VMEM((4, 128, 128), jnp.float32),
        pltpu.VMEM((4, 8, 256), jnp.float32),
        pltpu.VMEM((4, 144, 256), jnp.float32),
        pltpu.VMEM((8,) + query.shape, half),
        pltpu.VMEM((8, 8, 16, 512), half),
        pltpu.VMEM((8, 8, 16, 512), half),
        pltpu.VMEM((8, 16, 512), jnp.float32),
        pltpu.VMEM((8, 16, 512), jnp.float32),
        pltpu.VMEM(hidden.shape, jnp.float32),
        pltpu.VMEM(hidden.shape, half),
        pltpu.VMEM((rows, model), half),
        pltpu.VMEM(hidden.shape, jnp.float32),
    ] + dma(4, 16, 16, 4, 4, 4, 32, 8, 8)
    assert len(first) == ATTENTION
    loaded = [
        pltpu.VMEM(w_in.shape, half),
        pltpu.VMEM(w_out.shape, half),
        pltpu.SemaphoreType.DMA((2,)),
    ]
    second = [
        pltpu.VMEM((128, 128), half),
        pltpu.VMEM((128, 512), half),
        pltpu.VMEM((4, 128, 256), half),
        pltpu.VMEM((4, 128, 256), half),
        pltpu.VMEM((8,) + block, half),
        pltpu.VMEM((32,) + block, half),
        pltpu.VMEM((160, 2 * FFQ), jnp.float32),
        pltpu.VMEM((32, model), half),
        pltpu.VMEM((160, FFQ), half),
        pltpu.VMEM((32, model), half),
        pltpu.VMEM((32,) + block, half),
        pltpu.VMEM((16,) + block, half),
        pltpu.VMEM((8,) + block, half),
        pltpu.VMEM((8,) + block, half),
        pltpu.VMEM((8,) + block, half),
        pltpu.VMEM((8,) + block, half),
        pltpu.VMEM((4, 128, width), half),
        pltpu.VMEM((8, 4, 16, width), half),
    ] + dma(8, 8, 16, 16, 8, 8, 32)
    return pl.pallas_call(
        kernel,
        out_shape=jax.ShapeDtypeStruct(hidden.shape, half),
        in_specs=[vmem] * 9 + [pl.BlockSpec(memory_space=pl.ANY)] * 2,
        out_specs=vmem,
        scratch_shapes=first + loaded + second,
        compiler_params=pltpu.CompilerParams(
            collective_id=1, has_side_effects=True, vmem_limit_bytes=58 * 2**20
        ),
        name="layer",
    )(
        query,
        new_kv,
        old_kv,
        new_pos.reshape(1, rows),
        o_weight,
        hidden,
        norm_gain.reshape(1, model),
        expert_ids.T,
        gate_weights.T,
        w_in,
        w_out,
    )


def per_device(
    query,
    new_kv,
    old_kv,
    new_pos,
    o_weight,
    hidden,
    norm_gain,
    expert_ids,
    gate_weights,
    w_in,
    w_out,
):
    return layer(
        query,
        new_kv,
        old_kv,
        new_pos,
        o_weight,
        hidden,
        norm_gain,
        expert_ids,
        gate_weights,
        w_in[0, 0],
        w_out[0, 0],
    )


def solution(mesh):
    return jax.shard_map(
        per_device,
        mesh=mesh,
        in_specs=(
            P("ctx", "exp"),
            P(None, "ctx", None),
            P(None, "ctx", None),
            P("ctx"),
            P("exp", "ctx"),
            P(("ctx", "exp"), None),
            P(),
            P("ctx", None),
            P("ctx", None),
            P("ctx", "exp", None, None),
            P("ctx", "exp", None, None),
        ),
        out_specs=P(("ctx", "exp"), None),
        check_vma=False,
    )
```

```python
import jax
import jax.numpy as jnp
from jax import lax
from jax.experimental import pallas as pl
from jax.experimental.pallas import tpu as pltpu
from jax.sharding import PartitionSpec as P

HD = 128
FFQ = 384
MESH = pl.DeviceIdType.MESH
ARRIVE = (1, 2, 6, 3, 7, 4, 5)
ATTENTION = 33
NORMED = 13
ORDER = (0, 4, 1, 3, 5, 7, 2, 6)


CHUNKS = ((0, 1), (2, 6), (3, 7), (4,), (5,))
SCHEDULE = (
    ("send", 2, 6, 1),
    ("pass", 0, 1),
    ("sent", 2),
    ("send", 3),
    ("sent", 6),
    ("send", 7),
    ("pass", 2, 6),
    ("core", 0, 1),
    ("work", 0),
    ("sent", 3, 7),
    ("send", 4),
    ("pass", 3, 7),
    ("core", 2, 6),
    ("work", 1),
    ("sent", 4),
    ("send", 5),
    ("pass", 4),
    ("back", 2, 6),
    ("core", 3, 7),
    ("work", 2),
    ("core", 4),
    ("back", 3, 7),
    ("work", 3),
    ("pass", 5),
    ("home", 2, 6),
    ("back", 4),
    ("core", 5),
    ("home", 3, 7),
    ("work", 4),
    ("home", 4),
    ("back", 5, 1, 0),
    ("home", 5, 1, 0),
)


def place():
    ctx = lax.axis_index("ctx")
    return ctx // 8, (ctx // 2) % 4, ctx % 2, lax.axis_index("exp")


def ctx_of(hi, y, core):
    return lax.rem(hi, 4) * 8 + y * 2 + core


def across(i):
    hi, y, core, e = place()
    return (ctx_of(hi + i // 2, y if i % 2 == 0 else 3 - y, core), e)


def remote(src, dst, send, recv, device):
    return pltpu.make_async_remote_copy(
        src_ref=src, dst_ref=dst, send_sem=send, recv_sem=recv, device_id=device, device_id_type=MESH
    )


def attention(
    query,
    new_kv,
    old_kv,
    new_pos,
    o_weight,
    hidden,
    norm_gain,
    meanwhile,
    kv,
    weight,
    queries,
    bias,
    top,
    acc,
    attended,
    projected,
    from_exp,
    summed,
    pieces,
    gathered,
    own_normed,
    normed,
    residual_own,
    kz_send,
    kz_recv,
    ky_send,
    ky_recv,
    kc_send,
    kc_recv,
    wz_send,
    wz_recv,
    ay_send,
    ay_recv,
    ac_send,
    ac_recv,
    x_send,
    x_recv,
    p_send,
    p_recv,
    n_send,
    n_recv,
):
    hi, y, core, e = place()
    ctx = lax.axis_index("ctx")
    model = hidden.shape[1]
    sibling = (ctx_of(hi, y, 1 - core), e)
    up = (ctx_of(hi, lax.rem(y + 1, 4), core), e)
    down = (ctx_of(hi, lax.rem(y + 3, 4), core), e)

    def along(d):
        return (ctx_of(hi + d, y, core), e)

    parity = lax.rem(e, 2)
    outer = (ctx_of(hi + 3 + 2 * parity, y, core), e + 1 - 2 * parity)
    inner = (ctx, e + 1 - 2 * parity)

    def behind(s):
        return (ctx_of(hi, lax.rem(y + 4 - s % 4, 4), core if s < 4 else 1 - core), e)

    def other(d):
        return lax.rem(e + d, 8)

    barrier = pltpu.get_barrier_semaphore()
    for d in range(1, 4):
        pl.semaphore_signal(barrier, inc=1, device_id=along(d), device_id_type=MESH)
        pl.semaphore_signal(
            barrier, inc=1, device_id=across(2 * d + 1), device_id_type=MESH
        )
    pl.semaphore_signal(barrier, inc=1, device_id=outer, device_id_type=MESH)
    for s in range(1, 8):
        pl.semaphore_signal(barrier, inc=1, device_id=behind(s), device_id_type=MESH)
    for d in range(1, 8):
        pl.semaphore_signal(barrier, inc=1, device_id=(ctx, other(d)), device_id_type=MESH)

    lanes = pl.ds(pl.multiple_of((e // 2) * HD, HD), HD)
    kv[0, 0:256] = old_kv[0, :, lanes]
    kv[0, 256:384] = new_kv[0, :, lanes]
    for b in range(3):
        values = new_kv[1, :, lanes] if b == 2 else old_kv[1, b * 128 : (b + 1) * 128, lanes]
        kv[0, 384 + b * 128 : 512 + b * 128] = values.astype(jnp.float32).T.astype(jnp.bfloat16)
    own_pos = new_pos[...]
    row = lax.broadcasted_iota(jnp.int32, (16, 128), 0)
    kv[0, 768:784] = (
        jnp.where(row == 0, own_pos >> 6, jnp.where(row == 1, own_pos & 63, 0))
        .astype(jnp.float32)
        .astype(jnp.bfloat16)
    )

    pl.semaphore_wait(barrier, 21)

    kz = [None] + [
        remote(kv.at[d * 8 - 8], kv.at[d * 8], kz_send.at[d], kz_recv.at[d], device)
        for d, device in ((1, outer), (2, inner), (3, outer))
    ]
    wz = [None] + [
        remote(weight.at[0], weight.at[d], wz_send.at[d], wz_recv.at[d], along(d))
        for d in range(1, 4)
    ]
    ky = {}
    for d in range(4):
        for dy, device in ((1, up), (3, down)):
            ky[dy, d] = remote(
                kv.at[d * 8],
                kv.at[d * 8 + dy],
                ky_send.at[d * 4 + dy],
                ky_recv.at[d * 4 + dy],
                device,
            )
        for part, dy, device in ((0, 1, up), (1, 3, down)):
            some = pl.ds(400 * part, 400 - 16 * part)
            ky["up" if part == 0 else "down", d] = remote(
                kv.at[d * 8 + dy, some],
                kv.at[d * 8 + 2, some],
                ky_send.at[d * 4 + 2 * part],
                ky_recv.at[d * 4 + 2 * part],
                device,
            )
    kc = {
        (dy, d): remote(
            kv.at[d * 8 + dy],
            kv.at[d * 8 + 4 + dy],
            kc_send.at[d * 4 + dy],
            kc_recv.at[d * 4 + dy],
            sibling,
        )
        for d in range(4)
        for dy in range(4)
    }

    def begin_y(d):
        ky[1, d].start()
        ky[3, d].start()
        kc[0, d].start()

    def pass_on(d):
        ky[1, d].wait_recv()
        ky["up", d].start()
        kc[1, d].start()
        ky[3, d].wait_recv()
        ky["down", d].start()
        kc[3, d].start()

    def last(d):
        ky["up", d].wait_recv()
        ky["down", d].wait_recv()
        kc[2, d].start()

    kz[1].start()
    begin_y(0)
    weight[0] = o_weight[...]
    meanwhile()

    for h in range(8):
        part = query[:, h * HD : (h + 1) * HD].astype(jnp.float32).T.astype(jnp.bfloat16)
        queries[h // 2, :, (h % 2) * 128 : (h % 2 + 1) * 128] = part
    top[...] = jnp.full_like(top, -1e30)
    acc[...] = jnp.zeros_like(acc)
    factor = 1.4426950408889634 / HD**0.5

    def attend(blocks):
        for b in range(len(blocks)):
            digits = kv[blocks[b], 768:784].astype(jnp.float32)
            place_of = digits[0:1] * 64.0 + digits[1:2]
            column = jnp.broadcast_to(place_of, (128, 128)).T
            seen = column <= own_pos.astype(jnp.float32)
            bias[b] = jnp.where(seen, 0.0, -1e30)

        @pl.loop(0, 4, unroll=4)
        def _(t):
            part = queries[t]
            pieces = []
            for b in range(len(blocks)):
                scores = jnp.dot(kv[blocks[b], 0:384], part, preferred_element_type=jnp.float32)
                wide = jnp.concatenate([bias[b], bias[b]], 1)
                pieces += [scores[:256], scores[256:] + wide]
            old_top = top[t, 0:1]
            new_top = old_top
            for piece in pieces:
                new_top = jnp.maximum(new_top, jnp.max(piece, 0, keepdims=True))
            probs = jnp.concatenate(
                [jnp.exp2((piece - new_top) * factor).astype(jnp.bfloat16) for piece in pieces], 0
            )
            values = jnp.concatenate(
                [
                    kv[blocks[b], 384 + 128 * i : 512 + 128 * i]
                    for b in range(len(blocks))
                    for i in range(3)
                ],
                1,
            )
            ones = jnp.ones((16, values.shape[1]), jnp.bfloat16)
            added = jnp.dot(
                jnp.concatenate([values, ones], 0), probs, preferred_element_type=jnp.float32
            )
            acc[t] = acc[t] * jnp.exp2((old_top - new_top) * factor) + added
            top[t] = jnp.broadcast_to(new_top, (8, 256))

    def attend_from(blocks, *handed):
        for dy, d in handed:
            kc[dy, d].wait_recv()
        attend(blocks)

    attend_from([0, 4], (0, 0))
    kz[1].wait_recv()
    kz[2].start()
    begin_y(1)
    pass_on(0)
    attend_from([1, 3, 5, 7], (1, 0), (3, 0))
    kz[2].wait_recv()
    kz[3].start()
    begin_y(2)
    for d in (1, 3):
        wz[d].start()
    last(0)
    attend_from([8, 12], (0, 1))
    pass_on(1)
    attend_from([2, 6, 9, 11], (2, 0))
    kz[3].wait_recv()
    begin_y(3)
    wz[2].start()
    attend_from([13, 15, 16, 20], (1, 1), (3, 1), (0, 2))
    last(1)
    pass_on(2)
    attend_from([10, 14, 17, 19], (2, 1))
    attend_from([21, 23, 24, 28], (1, 2), (3, 2), (0, 3))
    last(2)
    pass_on(3)
    attend_from([18, 22, 25, 27], (2, 2))
    last(3)
    attend_from([29, 31], (1, 3), (3, 3))
    attend_from([26, 30], (2, 3))

    for h in range(8):
        part = slice((h % 2) * 128, (h % 2 + 1) * 128)
        scaled = acc[h // 2, 0:128, part] / acc[h // 2, 128:129, part]
        attended[0, :, h * HD : (h + 1) * HD] = scaled.T.astype(jnp.bfloat16)

    def half_of(slot, k):
        return attended.at[slot, pl.ds(k * 64, 64)]

    ay = {
        1: remote(attended.at[0], attended.at[1], ay_send.at[0], ay_recv.at[0], up),
        3: remote(attended.at[0], attended.at[3], ay_send.at[1], ay_recv.at[1], down),
        "up": remote(half_of(1, 0), half_of(2, 0), ay_send.at[2], ay_recv.at[2], up),
        "down": remote(half_of(3, 1), half_of(2, 1), ay_send.at[3], ay_recv.at[3], down),
    }
    ac = [
        remote(attended.at[s], attended.at[4 + s], ac_send.at[s], ac_recv.at[s], sibling)
        for s in range(4)
    ]
    ay[1].start()
    ay[3].start()
    ac[0].start()
    for d in range(1, 4):
        wz[d].wait_recv()

    def project(s):
        for pair in range(2):
            both = jnp.concatenate([weight[2 * pair], weight[2 * pair + 1]], 1)
            result = jnp.dot(attended[s], both, preferred_element_type=jnp.float32)
            projected[:, ORDER.index(s), :, pair * 256 : (pair + 1) * 256] = result.astype(
                jnp.bfloat16
            ).reshape(8, 16, 256)

    x_copy = [
        None
        if d == 0
        else remote(
            projected.at[other(d), pl.ds(pair * 2, 2)],
            from_exp.at[d, pl.ds(pair * 2, 2)],
            x_send.at[pair * 8 + d],
            x_recv.at[pair * 8 + d],
            (ctx, other(d)),
        )
        for pair in range(4)
        for d in range(8)
    ]

    def begin_x(pair):
        for d in range(1, 8):
            x_copy[pair * 8 + d].start()

    p_copy = [None] + [
        remote(summed.at[s], pieces.at[s], p_send.at[s], p_recv.at[s], behind(s))
        for s in range(1, 8)
    ]

    project(0)
    ac[0].wait_recv()
    project(4)
    begin_x(0)
    ay[1].wait_recv()
    ay["up"].start()
    ac[1].start()
    ay[3].wait_recv()
    ay["down"].start()
    ac[3].start()
    project(1)
    project(3)
    begin_x(1)
    ac[1].wait_recv()
    project(5)
    ac[3].wait_recv()
    project(7)
    begin_x(2)
    ay["up"].wait_recv()
    ay["down"].wait_recv()
    ac[2].start()
    project(2)
    ac[2].wait_recv()
    project(6)
    begin_x(3)

    for pair in range(4):
        for d in range(1, 8):
            x_copy[pair * 8 + d].wait_recv()
        for k in range(pair * 2, pair * 2 + 2):
            s = ORDER[k]
            total = projected[e, k].astype(jnp.float32)
            for d in range(1, 8):
                total += from_exp[d, k].astype(jnp.float32)
            if s == 0:
                pieces[0] = total
            else:
                summed[s] = total
                p_copy[s].start()
    for s in ORDER:
        if s > 0:
            p_copy[s].wait_recv()
        sender = lax.rem(y + s % 4, 4) * 2 + (core if s < 4 else 1 - core)
        for d in range(4):
            owner = lax.rem(hi + 4 - d, 4) * 8 + sender
            gathered[:, pl.ds(pl.multiple_of(owner * 128, 128), 128)] = pieces[
                s, :, d * 128 : (d + 1) * 128
            ]

    def rows_of(index):
        return pl.ds(pl.multiple_of(index * 16, 16), 16)

    residual = hidden[...].astype(jnp.float32) + gathered[...]
    residual_own[...] = residual
    mean = jnp.sum(residual * residual, 1, keepdims=True) * (1.0 / model)
    own = (residual * lax.rsqrt(mean + 1e-06) * norm_gain[...]).astype(jnp.bfloat16)
    own_normed[...] = own
    n_copy = [None] + [
        remote(own_normed, normed.at[rows_of(e)], n_send.at[d], n_recv.at[d], (ctx, other(d)))
        for d in range(1, 8)
    ]
    for d in range(1, 8):
        n_copy[d].start()
    normed[rows_of(e), :] = own
    for d in range(1, 8):
        n_copy[d].wait_recv()

    for d in range(1, 4):
        kz[d].wait_send()
        wz[d].wait_send()
    for d in range(4):
        for dy in range(4):
            kc[dy, d].wait_send()
        for step in (1, 3, "up", "down"):
            ky[step, d].wait_send()
        ac[d].wait_send()
    for copy in ay.values():
        copy.wait_send()
    for d in range(1, 8):
        for pair in range(4):
            x_copy[pair * 8 + d].wait_send()
        p_copy[d].wait_send()
        n_copy[d].wait_send()


def tables(ids, gates, pick, pick_rest, mix_hi, mix_lo):
    hi, y, core, e = place()
    chosen = ids[...]
    weights = gates[...]
    members, factors = [], []
    for i in range(8):
        expert = e * 8 + lax.rem(hi + i // 2, 4) * 2 + lax.rem(y // 2 + i, 2)
        hit = chosen == expert
        members.append(jnp.max(jnp.where(hit, 1.0, 0.0), 0, keepdims=True))
        factors.append(jnp.sum(jnp.where(hit, weights, 0.0), 0, keepdims=True))
    member = jnp.concatenate(members, 0)
    row = lax.broadcasted_iota(jnp.int32, (128, 128), 0)
    column = lax.broadcasted_iota(jnp.int32, (128, 128), 1)
    before = jnp.where(row < column, 1.0, 0.0).astype(jnp.bfloat16)
    rank = jnp.dot(member.astype(jnp.bfloat16), before, preferred_element_type=jnp.float32)
    slot = jnp.where(member > 0.5, rank, -1.0)
    slots = jnp.concatenate([jnp.broadcast_to(slot[i : i + 1], (16, 128)) for i in range(8)], 0)
    factor = jnp.concatenate([jnp.broadcast_to(f, (16, 128)) for f in factors], 0)
    r = row & 15
    for m in range(5):
        if m < 4:
            wanted = jnp.where(r >> 2 == m, 16 + (r & 3), -2)
        else:
            wanted = r
        found = slots == wanted.astype(jnp.float32)
        ones = jnp.where(found, 1.0, 0.0).astype(jnp.bfloat16)
        mix = jnp.where(found, factor, 0.0).T
        high = mix.astype(jnp.bfloat16)
        low = (mix - high.astype(jnp.float32)).astype(jnp.bfloat16)
        if m < 4:
            pick_rest[:, m * 128 : (m + 1) * 128] = ones
            mix_hi[m, :, 128:256] = high
            mix_lo[m, :, 128:256] = low
        else:
            pick[...] = ones
            for q in range(4):
                mix_hi[q, :, 0:128] = high
                mix_lo[q, :, 0:128] = low


def moe(
    normed,
    residual_own,
    out_ref,
    loads,
    w_in,
    w_out,
    pick,
    pick_rest,
    mix_hi,
    mix_lo,
    sent,
    got,
    both,
    rest_in,
    act,
    rest_out,
    part,
    from_core,
    to_pair,
    from_pair,
    to_home,
    home,
    mixed,
    from_exp,
    d_send,
    d_recv,
    f_send,
    f_recv,
    c_send,
    c_recv,
    rc_send,
    rc_recv,
    rf_send,
    rf_recv,
    rd_send,
    rd_recv,
    x_send,
    x_recv,
):
    hi, y, core, e = place()
    width = sent.shape[-1]
    sibling = (ctx_of(hi, y, 1 - core), e)
    pair = (ctx_of(hi, y + 1 - 2 * lax.rem(y, 2), core), e)

    def slot(i, group):
        chunk = [i in blocks for blocks in CHUNKS].index(True)
        blocks = CHUNKS[chunk]
        return 4 * sum(map(len, CHUNKS[:chunk])) + group * len(blocks) + blocks.index(i)

    def back(i):
        return (ctx_of(hi + 4 - i // 2, y if i % 2 == 0 else 3 - y, core), e)

    def other(d):
        return lax.rem(e + d, 8)

    for m in range(4):
        rows = jnp.dot(
            pick[...], normed[:, m * width : (m + 1) * width], preferred_element_type=jnp.float32
        )
        sent[:, m] = rows.astype(jnp.bfloat16).reshape(8, 16, width)
    rest = jnp.zeros((128, width), jnp.float32)
    for m in range(4):
        rest += jnp.dot(
            pick_rest[:, m * 128 : (m + 1) * 128],
            normed[:, m * width : (m + 1) * width],
            preferred_element_type=jnp.float32,
        )
    sent[:, 4] = rest.astype(jnp.bfloat16).reshape(8, 16, width)
    got[slot(0, 0)] = sent[0]

    d_copy = [
        None if i == 0 else remote(
            sent.at[i], got.at[slot(i, 0)], d_send.at[i], d_recv.at[i], across(i)
        )
        for i in range(8)
    ]
    f_copy = [
        remote(got.at[slot(i, 0)], got.at[slot(i, 2)], f_send.at[i], f_recv.at[i], pair)
        for i in range(8)
    ]
    c_copy = [
        remote(got.at[slot(i, g)], got.at[slot(i, g + 1)], c_send.at[k], c_recv.at[k], sibling)
        for k, (g, i) in enumerate((g, i) for g in (0, 2) for i in range(8))
    ]
    rc_copy = [
        remote(part.at[slot(i, g)], from_core.at[k], rc_send.at[k], rc_recv.at[k], sibling)
        for k, (g, i) in enumerate((g, i) for g in (1, 3) for i in range(8))
    ]
    rf_copy = [
        remote(to_pair.at[i], from_pair.at[i], rf_send.at[i], rf_recv.at[i], pair)
        for i in range(8)
    ]
    rd_copy = [
        None if i == 0 else remote(to_home.at[i], home.at[i], rd_send.at[i], rd_recv.at[i], back(i))
        for i in range(8)
    ]
    def regroup(m, rows, columns):
        row = lax.broadcasted_iota(jnp.int32, (rows, columns), 0)
        column = lax.broadcasted_iota(jnp.int32, (rows, columns), 1)
        small, large = (row, column) if rows < columns else (column, row)
        return (large == (small // 4) * 16 + m * 4 + small % 4).astype(jnp.bfloat16)

    def experts(base, count):
        tall, low = count * 16, count * 4
        rest_rows = got[base : base + count, 4].reshape(tall, width)
        for m in range(4):
            rest_in[:low, m * width : (m + 1) * width] = jnp.dot(
                regroup(m, low, tall), rest_rows, preferred_element_type=jnp.float32
            ).astype(jnp.bfloat16)

        @pl.loop(0, 3)
        def _(n):
            columns = pl.ds(pl.multiple_of(n * 256, 256), 256)
            total = jnp.zeros((tall + low, 256), jnp.float32)
            for m in range(4):
                rows = jnp.concatenate(
                    [
                        got[base : base + count, m].reshape(tall, width),
                        rest_in[:low, m * width : (m + 1) * width],
                    ],
                    0,
                )
                total += jnp.dot(
                    rows,
                    w_in[m * width : (m + 1) * width, columns],
                    preferred_element_type=jnp.float32,
                )
            both[: tall + low, columns] = total

        gate = both[: tall + low, :FFQ]
        act[: tall + low] = (gate / (1.0 + jnp.exp(-gate)) * both[: tall + low, FFQ:]).astype(
            jnp.bfloat16
        )
        steps = width // 256

        @pl.loop(0, 4 * steps)
        def _(n):
            columns = pl.ds(pl.multiple_of(n * 256, 256), 256)
            inner = pl.ds(pl.multiple_of((n % steps) * 256, 256), 256)
            result = jnp.dot(
                act[: tall + low], w_out[:, columns], preferred_element_type=jnp.float32
            ).astype(jnp.bfloat16)
            part[base : base + count, n // steps, :, inner] = result[:tall].reshape(count, 16, 256)
            rest_out[:low, columns] = result[tall:]

        rest_part = jnp.zeros((tall, width), jnp.float32)
        for m in range(4):
            rest_part += jnp.dot(
                regroup(m, tall, low),
                rest_out[:low, m * width : (m + 1) * width],
                preferred_element_type=jnp.float32,
            )
        part[base : base + count, 4] = rest_part.astype(jnp.bfloat16).reshape(count, 16, width)

    loaded = False
    for step, i in ((step, i) for step, *blocks in SCHEDULE for i in blocks):
        if step == "send":
            d_copy[i].start()
        elif step == "sent":
            d_copy[i].wait_send()
        elif step == "pass":
            if i > 0:
                d_copy[i].wait_recv()
            f_copy[i].start()
            c_copy[i].start()
        elif step == "core":
            f_copy[i].wait_recv()
            c_copy[8 + i].start()
        elif step == "work":
            if not loaded:
                for load in loads:
                    load.wait()
                loaded = True
            for block in CHUNKS[i]:
                c_copy[block].wait_recv()
                c_copy[8 + block].wait_recv()
            experts(slot(CHUNKS[i][0], 0), 4 * len(CHUNKS[i]))
            for block in CHUNKS[i]:
                rc_copy[8 + block].start()
            for block in CHUNKS[i]:
                rc_copy[block].start()
        elif step == "back":
            rc_copy[8 + i].wait_recv()
            to_pair[i] = (
                part[slot(i, 2)].astype(jnp.float32) + from_core[8 + i].astype(jnp.float32)
            ).astype(jnp.bfloat16)
            rf_copy[i].start()
        elif step == "home":
            rc_copy[i].wait_recv()
            rf_copy[i].wait_recv()
            total = (
                part[slot(i, 0)].astype(jnp.float32)
                + from_core[i].astype(jnp.float32)
                + from_pair[i].astype(jnp.float32)
            ).astype(jnp.bfloat16)
            if i == 0:
                home[0] = total
            else:
                to_home[i] = total
                rd_copy[i].start()
    for i in ARRIVE:
        rd_copy[i].wait_recv()

    own = pl.ds(pl.multiple_of(e * 16, 16), 16)
    x_copy = []
    for m in range(4):
        rows = jnp.concatenate(
            [home[:, m].reshape(128, width), home[:, 4].reshape(128, width)], 0
        )
        mixed[m] = (
            jnp.dot(mix_hi[m], rows, preferred_element_type=jnp.float32)
            + jnp.dot(mix_lo[m], rows, preferred_element_type=jnp.float32)
        ).astype(jnp.bfloat16)
        for d in range(1, 8):
            theirs = pl.ds(pl.multiple_of(other(d) * 16, 16), 16)
            copy = remote(
                mixed.at[m, theirs],
                from_exp.at[d, m],
                x_send.at[m * 8 + d],
                x_recv.at[m * 8 + d],
                (lax.axis_index("ctx"), other(d)),
            )
            copy.start()
            x_copy.append(copy)
    for m in range(4):
        columns = slice(m * width, (m + 1) * width)
        total = residual_own[:, columns] + mixed[m, own, :].astype(jnp.float32)
        for d in range(1, 8):
            x_copy[m * 7 + d - 1].wait_recv()
            total += from_exp[d, m].astype(jnp.float32)
        out_ref[:, columns] = total.astype(jnp.bfloat16)

    for copy in x_copy:
        copy.wait_send()
    for i in range(8):
        if i > 0:
            rd_copy[i].wait_send()
            if not any(step == "sent" and i in blocks for step, *blocks in SCHEDULE):
                d_copy[i].wait_send()
        rf_copy[i].wait_send()
        f_copy[i].wait_send()
    for i in range(16):
        c_copy[i].wait_send()
        rc_copy[i].wait_send()


def kernel(*refs):
    inputs, (ids, gates, w_in_hbm, w_out_hbm, out_ref), rest = refs[:7], refs[7:12], refs[12:]
    first, (w_in, w_out, w_sem), second = rest[:ATTENTION], rest[ATTENTION:][:3], rest[ATTENTION:][3:]
    loads = [
        pltpu.make_async_copy(w_in_hbm, w_in, w_sem.at[0]),
        pltpu.make_async_copy(w_out_hbm, w_out, w_sem.at[1]),
    ]

    def meanwhile():
        for load in loads:
            load.start()
        tables(ids, gates, *second[:4])

    attention(*inputs, meanwhile, *first)
    moe(first[NORMED], first[NORMED + 1], out_ref, loads, w_in, w_out, *second)


def layer(
    query,
    new_kv,
    old_kv,
    new_pos,
    o_weight,
    hidden,
    norm_gain,
    expert_ids,
    gate_weights,
    w_in,
    w_out,
):
    rows = query.shape[0]
    model = hidden.shape[1]
    width = model // 4
    block = (5, 16, width)
    half = jnp.bfloat16
    vmem = pl.BlockSpec(memory_space=pltpu.VMEM)

    def dma(*counts):
        return [pltpu.SemaphoreType.DMA((count,)) for count in counts for _ in range(2)]

    first = [
        pltpu.VMEM((32, 784, HD), half),
        pltpu.VMEM((4,) + o_weight.shape, half),
        pltpu.VMEM((4, HD, 256), half),
        pltpu.VMEM((4, 128, 128), jnp.float32),
        pltpu.VMEM((4, 8, 256), jnp.float32),
        pltpu.VMEM((4, 144, 256), jnp.float32),
        pltpu.VMEM((8,) + query.shape, half),
        pltpu.VMEM((8, 8, 16, 512), half),
        pltpu.VMEM((8, 8, 16, 512), half),
        pltpu.VMEM((8, 16, 512), jnp.float32),
        pltpu.VMEM((8, 16, 512), jnp.float32),
        pltpu.VMEM(hidden.shape, jnp.float32),
        pltpu.VMEM(hidden.shape, half),
        pltpu.VMEM((rows, model), half),
        pltpu.VMEM(hidden.shape, jnp.float32),
    ] + dma(4, 16, 16, 4, 4, 4, 32, 8, 8)
    assert len(first) == ATTENTION
    loaded = [
        pltpu.VMEM(w_in.shape, half),
        pltpu.VMEM(w_out.shape, half),
        pltpu.SemaphoreType.DMA((2,)),
    ]
    second = [
        pltpu.VMEM((128, 128), half),
        pltpu.VMEM((128, 512), half),
        pltpu.VMEM((4, 128, 256), half),
        pltpu.VMEM((4, 128, 256), half),
        pltpu.VMEM((8,) + block, half),
        pltpu.VMEM((32,) + block, half),
        pltpu.VMEM((160, 2 * FFQ), jnp.float32),
        pltpu.VMEM((32, model), half),
        pltpu.VMEM((160, FFQ), half),
        pltpu.VMEM((32, model), half),
        pltpu.VMEM((32,) + block, half),
        pltpu.VMEM((16,) + block, half),
        pltpu.VMEM((8,) + block, half),
        pltpu.VMEM((8,) + block, half),
        pltpu.VMEM((8,) + block, half),
        pltpu.VMEM((8,) + block, half),
        pltpu.VMEM((4, 128, width), half),
        pltpu.VMEM((8, 4, 16, width), half),
    ] + dma(8, 8, 16, 16, 8, 8, 32)
    return pl.pallas_call(
        kernel,
        out_shape=jax.ShapeDtypeStruct(hidden.shape, half),
        in_specs=[vmem] * 9 + [pl.BlockSpec(memory_space=pl.ANY)] * 2,
        out_specs=vmem,
        scratch_shapes=first + loaded + second,
        compiler_params=pltpu.CompilerParams(
            collective_id=1, has_side_effects=True, vmem_limit_bytes=58 * 2**20
        ),
        name="layer",
    )(
        query,
        new_kv,
        old_kv,
        new_pos.reshape(1, rows),
        o_weight,
        hidden,
        norm_gain.reshape(1, model),
        expert_ids.T,
        gate_weights.T,
        w_in,
        w_out,
    )


def per_device(
    query,
    new_kv,
    old_kv,
    new_pos,
    o_weight,
    hidden,
    norm_gain,
    expert_ids,
    gate_weights,
    w_in,
    w_out,
):
    return layer(
        query,
        new_kv,
        old_kv,
        new_pos,
        o_weight,
        hidden,
        norm_gain,
        expert_ids,
        gate_weights,
        w_in[0, 0],
        w_out[0, 0],
    )


def solution(mesh):
    return jax.shard_map(
        per_device,
        mesh=mesh,
        in_specs=(
            P("ctx", "exp"),
            P(None, "ctx", None),
            P(None, "ctx", None),
            P("ctx"),
            P("exp", "ctx"),
            P(("ctx", "exp"), None),
            P(),
            P("ctx", None),
            P("ctx", None),
            P("ctx", "exp", None, None),
            P("ctx", "exp", None, None),
        ),
        out_specs=P(("ctx", "exp"), None),
        check_vma=False,
    )
```

```python
import jax
import jax.numpy as jnp
from jax import lax
from jax.experimental import pallas as pl
from jax.experimental.pallas import tpu as pltpu
from jax.sharding import PartitionSpec as P

HD = 128
FFQ = 384
MESH = pl.DeviceIdType.MESH
ARRIVE = (1, 2, 6, 3, 7, 4, 5)
ATTENTION = 33
NORMED = 13
ORDER = (0, 4, 1, 3, 5, 7, 2, 6)


CHUNKS = ((0, 1), (2, 6), (3, 7), (4,), (5,))
SCHEDULE = (
    ("send", 2, 6, 1),
    ("pass", 0, 1),
    ("sent", 2),
    ("send", 3),
    ("sent", 6),
    ("send", 7),
    ("pass", 2, 6),
    ("core", 0, 1),
    ("work", 0),
    ("sent", 3, 7),
    ("send", 4),
    ("pass", 3, 7),
    ("core", 2, 6),
    ("work", 1),
    ("sent", 4),
    ("send", 5),
    ("pass", 4),
    ("back", 2, 6),
    ("core", 3, 7),
    ("work", 2),
    ("core", 4),
    ("back", 3, 7),
    ("work", 3),
    ("pass", 5),
    ("home", 2, 6),
    ("back", 4),
    ("core", 5),
    ("home", 3, 7),
    ("work", 4),
    ("home", 4),
    ("back", 5, 1, 0),
    ("home", 5, 1, 0),
)


def place():
    ctx = lax.axis_index("ctx")
    return ctx // 8, (ctx // 2) % 4, ctx % 2, lax.axis_index("exp")


def ctx_of(hi, y, core):
    return lax.rem(hi, 4) * 8 + y * 2 + core


def across(i):
    hi, y, core, e = place()
    return (ctx_of(hi + i // 2, y if i % 2 == 0 else 3 - y, core), e)


def remote(src, dst, send, recv, device):
    return pltpu.make_async_remote_copy(
        src_ref=src, dst_ref=dst, send_sem=send, recv_sem=recv, device_id=device, device_id_type=MESH
    )


def attention(
    query,
    new_kv,
    old_kv,
    new_pos,
    o_weight,
    hidden,
    norm_gain,
    meanwhile,
    kv,
    weight,
    queries,
    bias,
    top,
    acc,
    attended,
    projected,
    from_exp,
    summed,
    pieces,
    gathered,
    own_normed,
    normed,
    residual_own,
    kz_send,
    kz_recv,
    ky_send,
    ky_recv,
    kc_send,
    kc_recv,
    wz_send,
    wz_recv,
    ay_send,
    ay_recv,
    ac_send,
    ac_recv,
    x_send,
    x_recv,
    p_send,
    p_recv,
    n_send,
    n_recv,
):
    hi, y, core, e = place()
    ctx = lax.axis_index("ctx")
    model = hidden.shape[1]
    sibling = (ctx_of(hi, y, 1 - core), e)
    up = (ctx_of(hi, lax.rem(y + 1, 4), core), e)
    down = (ctx_of(hi, lax.rem(y + 3, 4), core), e)

    def along(d):
        return (ctx_of(hi + d, y, core), e)

    parity = lax.rem(e, 2)
    outer = (ctx_of(hi + 3 + 2 * parity, y, core), e + 1 - 2 * parity)
    inner = (ctx, e + 1 - 2 * parity)

    def behind(s):
        return (ctx_of(hi, lax.rem(y + 4 - s % 4, 4), core if s < 4 else 1 - core), e)

    def other(d):
        return lax.rem(e + d, 8)

    barrier = pltpu.get_barrier_semaphore()
    for d in range(1, 4):
        pl.semaphore_signal(barrier, inc=1, device_id=along(d), device_id_type=MESH)
        pl.semaphore_signal(
            barrier, inc=1, device_id=across(2 * d + 1), device_id_type=MESH
        )
    pl.semaphore_signal(barrier, inc=1, device_id=outer, device_id_type=MESH)
    for s in range(1, 8):
        pl.semaphore_signal(barrier, inc=1, device_id=behind(s), device_id_type=MESH)
    for d in range(1, 8):
        pl.semaphore_signal(barrier, inc=1, device_id=(ctx, other(d)), device_id_type=MESH)

    lanes = pl.ds(pl.multiple_of((e // 2) * HD, HD), HD)
    kv[0, 0:256] = old_kv[0, :, lanes]
    kv[0, 256:384] = new_kv[0, :, lanes]
    for b in range(3):
        values = new_kv[1, :, lanes] if b == 2 else old_kv[1, b * 128 : (b + 1) * 128, lanes]
        kv[0, 384 + b * 128 : 512 + b * 128] = values.astype(jnp.float32).T.astype(jnp.bfloat16)
    own_pos = new_pos[...]
    row = lax.broadcasted_iota(jnp.int32, (16, 128), 0)
    kv[0, 768:784] = (
        jnp.where(row == 0, own_pos >> 6, jnp.where(row == 1, own_pos & 63, 0))
        .astype(jnp.float32)
        .astype(jnp.bfloat16)
    )

    pl.semaphore_wait(barrier, 21)

    kz = [None] + [
        remote(kv.at[d * 8 - 8], kv.at[d * 8], kz_send.at[d], kz_recv.at[d], device)
        for d, device in ((1, outer), (2, inner), (3, outer))
    ]
    wz = [None] + [
        remote(weight.at[0], weight.at[d], wz_send.at[d], wz_recv.at[d], along(d))
        for d in range(1, 4)
    ]
    ky = {}
    for d in range(4):
        for dy, device in ((1, up), (3, down)):
            ky[dy, d] = remote(
                kv.at[d * 8],
                kv.at[d * 8 + dy],
                ky_send.at[d * 4 + dy],
                ky_recv.at[d * 4 + dy],
                device,
            )
        for part, dy, device in ((0, 1, up), (1, 3, down)):
            some = pl.ds(400 * part, 400 - 16 * part)
            ky["up" if part == 0 else "down", d] = remote(
                kv.at[d * 8 + dy, some],
                kv.at[d * 8 + 2, some],
                ky_send.at[d * 4 + 2 * part],
                ky_recv.at[d * 4 + 2 * part],
                device,
            )
    kc = {
        (dy, d): remote(
            kv.at[d * 8 + dy],
            kv.at[d * 8 + 4 + dy],
            kc_send.at[d * 4 + dy],
            kc_recv.at[d * 4 + dy],
            sibling,
        )
        for d in range(4)
        for dy in range(4)
    }

    def begin_y(d):
        ky[1, d].start()
        ky[3, d].start()
        kc[0, d].start()

    def pass_on(d):
        ky[1, d].wait_recv()
        ky["up", d].start()
        kc[1, d].start()
        ky[3, d].wait_recv()
        ky["down", d].start()
        kc[3, d].start()

    def last(d):
        ky["up", d].wait_recv()
        ky["down", d].wait_recv()
        kc[2, d].start()

    kz[1].start()
    begin_y(0)
    weight[0] = o_weight[...]
    meanwhile()

    for h in range(8):
        part = query[:, h * HD : (h + 1) * HD].astype(jnp.float32).T.astype(jnp.bfloat16)
        queries[h // 2, :, (h % 2) * 128 : (h % 2 + 1) * 128] = part
    top[...] = jnp.full_like(top, -1e30)
    acc[...] = jnp.zeros_like(acc)
    factor = 1.4426950408889634 / HD**0.5

    def attend(blocks):
        for b in range(len(blocks)):
            digits = kv[blocks[b], 768:784].astype(jnp.float32)
            place_of = digits[0:1] * 64.0 + digits[1:2]
            column = jnp.broadcast_to(place_of, (128, 128)).T
            seen = column <= own_pos.astype(jnp.float32)
            bias[b] = jnp.where(seen, 0.0, -1e30)

        @pl.loop(0, 4, unroll=4)
        def _(t):
            part = queries[t]
            pieces = []
            for b in range(len(blocks)):
                scores = jnp.dot(kv[blocks[b], 0:384], part, preferred_element_type=jnp.float32)
                wide = jnp.concatenate([bias[b], bias[b]], 1)
                pieces += [scores[:256], scores[256:] + wide]
            old_top = top[t, 0:1]
            new_top = old_top
            for piece in pieces:
                new_top = jnp.maximum(new_top, jnp.max(piece, 0, keepdims=True))
            probs = jnp.concatenate(
                [jnp.exp2((piece - new_top) * factor).astype(jnp.bfloat16) for piece in pieces], 0
            )
            values = jnp.concatenate(
                [
                    kv[blocks[b], 384 + 128 * i : 512 + 128 * i]
                    for b in range(len(blocks))
                    for i in range(3)
                ],
                1,
            )
            ones = jnp.ones((16, values.shape[1]), jnp.bfloat16)
            added = jnp.dot(
                jnp.concatenate([values, ones], 0), probs, preferred_element_type=jnp.float32
            )
            acc[t] = acc[t] * jnp.exp2((old_top - new_top) * factor) + added
            top[t] = jnp.broadcast_to(new_top, (8, 256))

    def attend_from(blocks, *handed):
        for dy, d in handed:
            kc[dy, d].wait_recv()
        attend(blocks)

    attend_from([0, 4], (0, 0))
    kz[1].wait_recv()
    kz[2].start()
    begin_y(1)
    pass_on(0)
    attend_from([1, 3, 5, 7], (1, 0), (3, 0))
    kz[2].wait_recv()
    kz[3].start()
    begin_y(2)
    last(0)
    attend_from([8, 12], (0, 1))
    pass_on(1)
    attend_from([2, 6, 9, 11], (2, 0))
    kz[3].wait_recv()
    begin_y(3)
    for d in (1, 3, 2):
        wz[d].start()
    attend_from([13, 15, 16, 20], (1, 1), (3, 1), (0, 2))
    last(1)
    pass_on(2)
    attend_from([10, 14, 17, 19], (2, 1))
    attend_from([21, 23, 24, 28], (1, 2), (3, 2), (0, 3))
    last(2)
    pass_on(3)
    attend_from([18, 22, 25, 27], (2, 2))
    last(3)
    attend_from([29, 31], (1, 3), (3, 3))
    attend_from([26, 30], (2, 3))

    for h in range(8):
        part = slice((h % 2) * 128, (h % 2 + 1) * 128)
        scaled = acc[h // 2, 0:128, part] / acc[h // 2, 128:129, part]
        attended[0, :, h * HD : (h + 1) * HD] = scaled.T.astype(jnp.bfloat16)

    def half_of(slot, k):
        return attended.at[slot, pl.ds(k * 64, 64)]

    ay = {
        1: remote(attended.at[0], attended.at[1], ay_send.at[0], ay_recv.at[0], up),
        3: remote(attended.at[0], attended.at[3], ay_send.at[1], ay_recv.at[1], down),
        "up": remote(half_of(1, 0), half_of(2, 0), ay_send.at[2], ay_recv.at[2], up),
        "down": remote(half_of(3, 1), half_of(2, 1), ay_send.at[3], ay_recv.at[3], down),
    }
    ac = [
        remote(attended.at[s], attended.at[4 + s], ac_send.at[s], ac_recv.at[s], sibling)
        for s in range(4)
    ]
    ay[1].start()
    ay[3].start()
    ac[0].start()
    for d in range(1, 4):
        wz[d].wait_recv()

    def project(s):
        for pair in range(2):
            both = jnp.concatenate([weight[2 * pair], weight[2 * pair + 1]], 1)
            result = jnp.dot(attended[s], both, preferred_element_type=jnp.float32)
            projected[:, ORDER.index(s), :, pair * 256 : (pair + 1) * 256] = result.astype(
                jnp.bfloat16
            ).reshape(8, 16, 256)

    x_copy = [
        None
        if d == 0
        else remote(
            projected.at[other(d), pl.ds(pair * 2, 2)],
            from_exp.at[d, pl.ds(pair * 2, 2)],
            x_send.at[pair * 8 + d],
            x_recv.at[pair * 8 + d],
            (ctx, other(d)),
        )
        for pair in range(4)
        for d in range(8)
    ]

    def begin_x(pair):
        for d in range(1, 8):
            x_copy[pair * 8 + d].start()

    p_copy = [None] + [
        remote(summed.at[s], pieces.at[s], p_send.at[s], p_recv.at[s], behind(s))
        for s in range(1, 8)
    ]

    project(0)
    ac[0].wait_recv()
    project(4)
    begin_x(0)
    ay[1].wait_recv()
    ay["up"].start()
    ac[1].start()
    ay[3].wait_recv()
    ay["down"].start()
    ac[3].start()
    project(1)
    project(3)
    begin_x(1)
    ac[1].wait_recv()
    project(5)
    ac[3].wait_recv()
    project(7)
    begin_x(2)
    ay["up"].wait_recv()
    ay["down"].wait_recv()
    ac[2].start()
    project(2)
    ac[2].wait_recv()
    project(6)
    begin_x(3)

    for pair in range(4):
        for d in range(1, 8):
            x_copy[pair * 8 + d].wait_recv()
        for k in range(pair * 2, pair * 2 + 2):
            s = ORDER[k]
            total = projected[e, k].astype(jnp.float32)
            for d in range(1, 8):
                total += from_exp[d, k].astype(jnp.float32)
            if s == 0:
                pieces[0] = total
            else:
                summed[s] = total
                p_copy[s].start()
    for s in ORDER:
        if s > 0:
            p_copy[s].wait_recv()
        sender = lax.rem(y + s % 4, 4) * 2 + (core if s < 4 else 1 - core)
        for d in range(4):
            owner = lax.rem(hi + 4 - d, 4) * 8 + sender
            gathered[:, pl.ds(pl.multiple_of(owner * 128, 128), 128)] = pieces[
                s, :, d * 128 : (d + 1) * 128
            ]

    def rows_of(index):
        return pl.ds(pl.multiple_of(index * 16, 16), 16)

    residual = hidden[...].astype(jnp.float32) + gathered[...]
    residual_own[...] = residual
    mean = jnp.sum(residual * residual, 1, keepdims=True) * (1.0 / model)
    own = (residual * lax.rsqrt(mean + 1e-06) * norm_gain[...]).astype(jnp.bfloat16)
    own_normed[...] = own
    n_copy = [None] + [
        remote(own_normed, normed.at[rows_of(e)], n_send.at[d], n_recv.at[d], (ctx, other(d)))
        for d in range(1, 8)
    ]
    for d in range(1, 8):
        n_copy[d].start()
    normed[rows_of(e), :] = own
    for d in range(1, 8):
        n_copy[d].wait_recv()

    for d in range(1, 4):
        kz[d].wait_send()
        wz[d].wait_send()
    for d in range(4):
        for dy in range(4):
            kc[dy, d].wait_send()
        for step in (1, 3, "up", "down"):
            ky[step, d].wait_send()
        ac[d].wait_send()
    for copy in ay.values():
        copy.wait_send()
    for d in range(1, 8):
        for pair in range(4):
            x_copy[pair * 8 + d].wait_send()
        p_copy[d].wait_send()
        n_copy[d].wait_send()


def tables(ids, gates, pick, pick_rest, mix_hi, mix_lo):
    hi, y, core, e = place()
    chosen = ids[...]
    weights = gates[...]
    members, factors = [], []
    for i in range(8):
        expert = e * 8 + lax.rem(hi + i // 2, 4) * 2 + lax.rem(y // 2 + i, 2)
        hit = chosen == expert
        members.append(jnp.max(jnp.where(hit, 1.0, 0.0), 0, keepdims=True))
        factors.append(jnp.sum(jnp.where(hit, weights, 0.0), 0, keepdims=True))
    member = jnp.concatenate(members, 0)
    row = lax.broadcasted_iota(jnp.int32, (128, 128), 0)
    column = lax.broadcasted_iota(jnp.int32, (128, 128), 1)
    before = jnp.where(row < column, 1.0, 0.0).astype(jnp.bfloat16)
    rank = jnp.dot(member.astype(jnp.bfloat16), before, preferred_element_type=jnp.float32)
    slot = jnp.where(member > 0.5, rank, -1.0)
    slots = jnp.concatenate([jnp.broadcast_to(slot[i : i + 1], (16, 128)) for i in range(8)], 0)
    factor = jnp.concatenate([jnp.broadcast_to(f, (16, 128)) for f in factors], 0)
    r = row & 15
    for m in range(5):
        if m < 4:
            wanted = jnp.where(r >> 2 == m, 16 + (r & 3), -2)
        else:
            wanted = r
        found = slots == wanted.astype(jnp.float32)
        ones = jnp.where(found, 1.0, 0.0).astype(jnp.bfloat16)
        mix = jnp.where(found, factor, 0.0).T
        high = mix.astype(jnp.bfloat16)
        low = (mix - high.astype(jnp.float32)).astype(jnp.bfloat16)
        if m < 4:
            pick_rest[:, m * 128 : (m + 1) * 128] = ones
            mix_hi[m, :, 128:256] = high
            mix_lo[m, :, 128:256] = low
        else:
            pick[...] = ones
            for q in range(4):
                mix_hi[q, :, 0:128] = high
                mix_lo[q, :, 0:128] = low


def moe(
    normed,
    residual_own,
    out_ref,
    loads,
    w_in,
    w_out,
    pick,
    pick_rest,
    mix_hi,
    mix_lo,
    sent,
    got,
    both,
    rest_in,
    act,
    rest_out,
    part,
    from_core,
    to_pair,
    from_pair,
    to_home,
    home,
    mixed,
    from_exp,
    d_send,
    d_recv,
    f_send,
    f_recv,
    c_send,
    c_recv,
    rc_send,
    rc_recv,
    rf_send,
    rf_recv,
    rd_send,
    rd_recv,
    x_send,
    x_recv,
):
    hi, y, core, e = place()
    width = sent.shape[-1]
    sibling = (ctx_of(hi, y, 1 - core), e)
    pair = (ctx_of(hi, y + 1 - 2 * lax.rem(y, 2), core), e)

    def slot(i, group):
        chunk = [i in blocks for blocks in CHUNKS].index(True)
        blocks = CHUNKS[chunk]
        return 4 * sum(map(len, CHUNKS[:chunk])) + group * len(blocks) + blocks.index(i)

    def back(i):
        return (ctx_of(hi + 4 - i // 2, y if i % 2 == 0 else 3 - y, core), e)

    def other(d):
        return lax.rem(e + d, 8)

    for m in range(4):
        rows = jnp.dot(
            pick[...], normed[:, m * width : (m + 1) * width], preferred_element_type=jnp.float32
        )
        sent[:, m] = rows.astype(jnp.bfloat16).reshape(8, 16, width)
    rest = jnp.zeros((128, width), jnp.float32)
    for m in range(4):
        rest += jnp.dot(
            pick_rest[:, m * 128 : (m + 1) * 128],
            normed[:, m * width : (m + 1) * width],
            preferred_element_type=jnp.float32,
        )
    sent[:, 4] = rest.astype(jnp.bfloat16).reshape(8, 16, width)
    got[slot(0, 0)] = sent[0]

    d_copy = [
        None if i == 0 else remote(
            sent.at[i], got.at[slot(i, 0)], d_send.at[i], d_recv.at[i], across(i)
        )
        for i in range(8)
    ]
    f_copy = [
        remote(got.at[slot(i, 0)], got.at[slot(i, 2)], f_send.at[i], f_recv.at[i], pair)
        for i in range(8)
    ]
    c_copy = [
        remote(got.at[slot(i, g)], got.at[slot(i, g + 1)], c_send.at[k], c_recv.at[k], sibling)
        for k, (g, i) in enumerate((g, i) for g in (0, 2) for i in range(8))
    ]
    rc_copy = [
        remote(part.at[slot(i, g)], from_core.at[k], rc_send.at[k], rc_recv.at[k], sibling)
        for k, (g, i) in enumerate((g, i) for g in (1, 3) for i in range(8))
    ]
    rf_copy = [
        remote(to_pair.at[i], from_pair.at[i], rf_send.at[i], rf_recv.at[i], pair)
        for i in range(8)
    ]
    rd_copy = [
        None if i == 0 else remote(to_home.at[i], home.at[i], rd_send.at[i], rd_recv.at[i], back(i))
        for i in range(8)
    ]
    def regroup(m, rows, columns):
        row = lax.broadcasted_iota(jnp.int32, (rows, columns), 0)
        column = lax.broadcasted_iota(jnp.int32, (rows, columns), 1)
        small, large = (row, column) if rows < columns else (column, row)
        return (large == (small // 4) * 16 + m * 4 + small % 4).astype(jnp.bfloat16)

    def experts(base, count):
        tall, low = count * 16, count * 4
        rest_rows = got[base : base + count, 4].reshape(tall, width)
        for m in range(4):
            rest_in[:low, m * width : (m + 1) * width] = jnp.dot(
                regroup(m, low, tall), rest_rows, preferred_element_type=jnp.float32
            ).astype(jnp.bfloat16)

        @pl.loop(0, 3)
        def _(n):
            columns = pl.ds(pl.multiple_of(n * 256, 256), 256)
            total = jnp.zeros((tall + low, 256), jnp.float32)
            for m in range(4):
                rows = jnp.concatenate(
                    [
                        got[base : base + count, m].reshape(tall, width),
                        rest_in[:low, m * width : (m + 1) * width],
                    ],
                    0,
                )
                total += jnp.dot(
                    rows,
                    w_in[m * width : (m + 1) * width, columns],
                    preferred_element_type=jnp.float32,
                )
            both[: tall + low, columns] = total

        gate = both[: tall + low, :FFQ]
        act[: tall + low] = (gate / (1.0 + jnp.exp(-gate)) * both[: tall + low, FFQ:]).astype(
            jnp.bfloat16
        )
        steps = width // 256

        @pl.loop(0, 4 * steps)
        def _(n):
            columns = pl.ds(pl.multiple_of(n * 256, 256), 256)
            inner = pl.ds(pl.multiple_of((n % steps) * 256, 256), 256)
            result = jnp.dot(
                act[: tall + low], w_out[:, columns], preferred_element_type=jnp.float32
            ).astype(jnp.bfloat16)
            part[base : base + count, n // steps, :, inner] = result[:tall].reshape(count, 16, 256)
            rest_out[:low, columns] = result[tall:]

        rest_part = jnp.zeros((tall, width), jnp.float32)
        for m in range(4):
            rest_part += jnp.dot(
                regroup(m, tall, low),
                rest_out[:low, m * width : (m + 1) * width],
                preferred_element_type=jnp.float32,
            )
        part[base : base + count, 4] = rest_part.astype(jnp.bfloat16).reshape(count, 16, width)

    loaded = False
    for step, i in ((step, i) for step, *blocks in SCHEDULE for i in blocks):
        if step == "send":
            d_copy[i].start()
        elif step == "sent":
            d_copy[i].wait_send()
        elif step == "pass":
            if i > 0:
                d_copy[i].wait_recv()
            f_copy[i].start()
            c_copy[i].start()
        elif step == "core":
            f_copy[i].wait_recv()
            c_copy[8 + i].start()
        elif step == "work":
            if not loaded:
                for load in loads:
                    load.wait()
                loaded = True
            for block in CHUNKS[i]:
                c_copy[block].wait_recv()
                c_copy[8 + block].wait_recv()
            experts(slot(CHUNKS[i][0], 0), 4 * len(CHUNKS[i]))
            for block in CHUNKS[i]:
                rc_copy[8 + block].start()
            for block in CHUNKS[i]:
                rc_copy[block].start()
        elif step == "back":
            rc_copy[8 + i].wait_recv()
            to_pair[i] = (
                part[slot(i, 2)].astype(jnp.float32) + from_core[8 + i].astype(jnp.float32)
            ).astype(jnp.bfloat16)
            rf_copy[i].start()
        elif step == "home":
            rc_copy[i].wait_recv()
            rf_copy[i].wait_recv()
            total = (
                part[slot(i, 0)].astype(jnp.float32)
                + from_core[i].astype(jnp.float32)
                + from_pair[i].astype(jnp.float32)
            ).astype(jnp.bfloat16)
            if i == 0:
                home[0] = total
            else:
                to_home[i] = total
                rd_copy[i].start()
    for i in ARRIVE:
        rd_copy[i].wait_recv()

    own = pl.ds(pl.multiple_of(e * 16, 16), 16)
    x_copy = []
    for m in range(4):
        rows = jnp.concatenate(
            [home[:, m].reshape(128, width), home[:, 4].reshape(128, width)], 0
        )
        mixed[m] = (
            jnp.dot(mix_hi[m], rows, preferred_element_type=jnp.float32)
            + jnp.dot(mix_lo[m], rows, preferred_element_type=jnp.float32)
        ).astype(jnp.bfloat16)
        for d in range(1, 8):
            theirs = pl.ds(pl.multiple_of(other(d) * 16, 16), 16)
            copy = remote(
                mixed.at[m, theirs],
                from_exp.at[d, m],
                x_send.at[m * 8 + d],
                x_recv.at[m * 8 + d],
                (lax.axis_index("ctx"), other(d)),
            )
            copy.start()
            x_copy.append(copy)
    for m in range(4):
        columns = slice(m * width, (m + 1) * width)
        total = residual_own[:, columns] + mixed[m, own, :].astype(jnp.float32)
        for d in range(1, 8):
            x_copy[m * 7 + d - 1].wait_recv()
            total += from_exp[d, m].astype(jnp.float32)
        out_ref[:, columns] = total.astype(jnp.bfloat16)

    for copy in x_copy:
        copy.wait_send()
    for i in range(8):
        if i > 0:
            rd_copy[i].wait_send()
            if not any(step == "sent" and i in blocks for step, *blocks in SCHEDULE):
                d_copy[i].wait_send()
        rf_copy[i].wait_send()
        f_copy[i].wait_send()
    for i in range(16):
        c_copy[i].wait_send()
        rc_copy[i].wait_send()


def kernel(*refs):
    inputs, (ids, gates, w_in_hbm, w_out_hbm, out_ref), rest = refs[:7], refs[7:12], refs[12:]
    first, (w_in, w_out, w_sem), second = rest[:ATTENTION], rest[ATTENTION:][:3], rest[ATTENTION:][3:]
    loads = [
        pltpu.make_async_copy(w_in_hbm, w_in, w_sem.at[0]),
        pltpu.make_async_copy(w_out_hbm, w_out, w_sem.at[1]),
    ]

    def meanwhile():
        for load in loads:
            load.start()
        tables(ids, gates, *second[:4])

    attention(*inputs, meanwhile, *first)
    moe(first[NORMED], first[NORMED + 1], out_ref, loads, w_in, w_out, *second)


def layer(
    query,
    new_kv,
    old_kv,
    new_pos,
    o_weight,
    hidden,
    norm_gain,
    expert_ids,
    gate_weights,
    w_in,
    w_out,
):
    rows = query.shape[0]
    model = hidden.shape[1]
    width = model // 4
    block = (5, 16, width)
    half = jnp.bfloat16
    vmem = pl.BlockSpec(memory_space=pltpu.VMEM)

    def dma(*counts):
        return [pltpu.SemaphoreType.DMA((count,)) for count in counts for _ in range(2)]

    first = [
        pltpu.VMEM((32, 784, HD), half),
        pltpu.VMEM((4,) + o_weight.shape, half),
        pltpu.VMEM((4, HD, 256), half),
        pltpu.VMEM((4, 128, 128), jnp.float32),
        pltpu.VMEM((4, 8, 256), jnp.float32),
        pltpu.VMEM((4, 144, 256), jnp.float32),
        pltpu.VMEM((8,) + query.shape, half),
        pltpu.VMEM((8, 8, 16, 512), half),
        pltpu.VMEM((8, 8, 16, 512), half),
        pltpu.VMEM((8, 16, 512), jnp.float32),
        pltpu.VMEM((8, 16, 512), jnp.float32),
        pltpu.VMEM(hidden.shape, jnp.float32),
        pltpu.VMEM(hidden.shape, half),
        pltpu.VMEM((rows, model), half),
        pltpu.VMEM(hidden.shape, jnp.float32),
    ] + dma(4, 16, 16, 4, 4, 4, 32, 8, 8)
    assert len(first) == ATTENTION
    loaded = [
        pltpu.VMEM(w_in.shape, half),
        pltpu.VMEM(w_out.shape, half),
        pltpu.SemaphoreType.DMA((2,)),
    ]
    second = [
        pltpu.VMEM((128, 128), half),
        pltpu.VMEM((128, 512), half),
        pltpu.VMEM((4, 128, 256), half),
        pltpu.VMEM((4, 128, 256), half),
        pltpu.VMEM((8,) + block, half),
        pltpu.VMEM((32,) + block, half),
        pltpu.VMEM((160, 2 * FFQ), jnp.float32),
        pltpu.VMEM((32, model), half),
        pltpu.VMEM((160, FFQ), half),
        pltpu.VMEM((32, model), half),
        pltpu.VMEM((32,) + block, half),
        pltpu.VMEM((16,) + block, half),
        pltpu.VMEM((8,) + block, half),
        pltpu.VMEM((8,) + block, half),
        pltpu.VMEM((8,) + block, half),
        pltpu.VMEM((8,) + block, half),
        pltpu.VMEM((4, 128, width), half),
        pltpu.VMEM((8, 4, 16, width), half),
    ] + dma(8, 8, 16, 16, 8, 8, 32)
    return pl.pallas_call(
        kernel,
        out_shape=jax.ShapeDtypeStruct(hidden.shape, half),
        in_specs=[vmem] * 9 + [pl.BlockSpec(memory_space=pl.ANY)] * 2,
        out_specs=vmem,
        scratch_shapes=first + loaded + second,
        compiler_params=pltpu.CompilerParams(
            collective_id=1, has_side_effects=True, vmem_limit_bytes=58 * 2**20
        ),
        name="layer",
    )(
        query,
        new_kv,
        old_kv,
        new_pos.reshape(1, rows),
        o_weight,
        hidden,
        norm_gain.reshape(1, model),
        expert_ids.T,
        gate_weights.T,
        w_in,
        w_out,
    )


def per_device(
    query,
    new_kv,
    old_kv,
    new_pos,
    o_weight,
    hidden,
    norm_gain,
    expert_ids,
    gate_weights,
    w_in,
    w_out,
):
    return layer(
        query,
        new_kv,
        old_kv,
        new_pos,
        o_weight,
        hidden,
        norm_gain,
        expert_ids,
        gate_weights,
        w_in[0, 0],
        w_out[0, 0],
    )


def solution(mesh):
    return jax.shard_map(
        per_device,
        mesh=mesh,
        in_specs=(
            P("ctx", "exp"),
            P(None, "ctx", None),
            P(None, "ctx", None),
            P("ctx"),
            P("exp", "ctx"),
            P(("ctx", "exp"), None),
            P(),
            P("ctx", None),
            P("ctx", None),
            P("ctx", "exp", None, None),
            P("ctx", "exp", None, None),
        ),
        out_specs=P(("ctx", "exp"), None),
        check_vma=False,
    )
```
